32 devices in a mesh: dp: 4 (over y, x), ctx: 8 (over z, core).
Axes of the slice: x: 2, y: 2, z: 4, core: 2. Of those that a mesh axis runs over, the one named last changes fastest.
Arguments:
- hidden_in: float32 [4, 1024, 640], P('dp', 'ctx'), may hold values from -6 to 6
- positions: int32 [4, 1024], P('dp', 'ctx'), may hold values from 0 to 511, as said below
- w_query: bfloat16 [1024, 640], P(('dp', 'ctx')), may hold values from -0.25 to 0.25
- w_key: bfloat16 [256, 640], P(('dp', 'ctx')), may hold values from -0.25 to 0.25
- w_value: bfloat16 [256, 640], P(('dp', 'ctx')), may hold values from -0.25 to 0.25
- w_output: bfloat16 [1024, 640], P(('dp', 'ctx')), may hold values from -0.1875 to 0.1875
- w_gate: bfloat16 [2048, 640], P(('dp', 'ctx')), may hold values from -0.25 to 0.25
- w_up: bfloat16 [2048, 640], P(('dp', 'ctx')), may hold values from -0.25 to 0.25
- w_down: bfloat16 [2048, 640], P(('dp', 'ctx')), may hold values from -0.125 to 0.125
- norm_scales: bfloat16 [3072], P(('dp', 'ctx')), may hold values from -0.5 to 0.5
- grad_out: float32 [4, 1024, 640], P('dp', 'ctx'), may hold values from -6 to 6
Outputs:
- block_out: float32 [4, 1024, 640], P('dp', 'ctx')
- grad_in: float32 [4, 1024, 640], P('dp', 'ctx')
- grad_w_query: float32 [1024, 640], P(('dp', 'ctx'))
- grad_w_key: float32 [256, 640], P(('dp', 'ctx'))
- grad_w_value: float32 [256, 640], P(('dp', 'ctx'))
- grad_w_output: float32 [1024, 640], P(('dp', 'ctx'))
- grad_w_gate: float32 [2048, 640], P(('dp', 'ctx'))
- grad_w_up: float32 [2048, 640], P(('dp', 'ctx'))
- grad_w_down: float32 [2048, 640], P(('dp', 'ctx'))
- grad_scales: float32 [3072], P(('dp', 'ctx'))
The draws below stay inside these ranges and needn't reach their ends.
Inputs may be any that keep to these rules, and one draw needn't show every extreme that they name: `positions`: each sequence is a pack of documents in natural order; the first document is the first half of the sequence (512 tokens), the rest are shorter; a token's entry is its distance from the first token of its document, rising by one from token to token within a document, listed in stored order.
All inputs are finite; a program needn't handle non-finite values.
Results may differ from the reference program's by a relative error of at most 0.015.
Values may be sent and summed in bfloat16 or wider, within the bound.
No kernel may reach another device: no remote copies, remote signals or barrier semaphores. Data moves between devices by JAX's collectives and lax.ppermute only.
A program may use at most 192 MiB of HBM per device.

```python
import math
from functools import partial
import jax
import jax.numpy as jnp
from jax import lax

D = 640
HEADS = 4
HEAD_DIM = 256
FF = 2048
BLK = 64
SEQ = 1024
SEQS = 4
SCALES = 3072
N_CTX = 8


def natural_of_stored(length, block):
    groups = length // (2 * block)
    device = jnp.arange(groups, dtype=jnp.int32)[:, None]
    within = jnp.arange(block, dtype=jnp.int32)[None, :]
    early = device * block + within
    late = (2 * groups - 1 - device) * block + within
    return jnp.stack([early, late], axis=1).reshape(length)


def one_pack(seed_key):
    later_cuts = jax.random.randint(seed_key, (2,), SEQ // 2 + 1, SEQ, dtype=jnp.int32)
    cuts = jnp.concatenate([jnp.full((1,), SEQ // 2, jnp.int32), later_cuts])
    natural = natural_of_stored(SEQ, BLK)
    begins = jnp.max(jnp.where(cuts[None, :] <= natural[:, None], cuts[None, :], 0), axis=1)
    return natural - begins


def draw_positions(key, part):
    seed_keys = jax.random.split(jax.random.fold_in(key, 11), SEQS)
    return jax.vmap(one_pack)(seed_keys).astype(jnp.int32)


def steps_of(key, shape, shards, least, high):
    loudness = 1.0
    for dim, shards_of in shards:
        draws = jax.random.uniform(jax.random.fold_in(jax.random.fold_in(key, 6), dim), (shards_of,), jnp.float32, least / len(shards), high / len(shards))
        loudness = loudness * jnp.repeat(jnp.exp(draws), shape[dim] // shards_of).reshape((-1,) + (1,) * (len(shape) - 1 - dim))
    return loudness


def bell_draw(own_key, shape, scale, limit, cuts=(), held_as=jnp.bfloat16):
    array = scale * jax.random.normal(own_key, shape, jnp.float32)
    if cuts:
        array = array * steps_of(own_key, shape, cuts, -0.22, 0.18)
    return jnp.clip(array, -limit, limit).astype(held_as)


def setup_inputs(seed: int = 0) -> dict:
    keys = jax.random.split(jax.random.key(seed), 12)
    hidden_in = bell_draw(keys[0], (SEQS, SEQ, D), 1.0, 6.0, ((0, 4), (1, 8)), jnp.float32)
    positions = draw_positions(jax.random.fold_in(keys[11], 71), 0)
    w_query = bell_draw(keys[2], (HEADS * HEAD_DIM, D), D ** -0.5, 0.25, ((0, 32),))
    w_key = bell_draw(keys[3], (HEAD_DIM, D), D ** -0.5, 0.25, ((0, 32),))
    w_value = bell_draw(keys[4], (HEAD_DIM, D), D ** -0.5, 0.25, ((0, 32),))
    w_output = bell_draw(keys[5], (HEADS * HEAD_DIM, D), (HEADS * HEAD_DIM) ** -0.5, 0.1875, ((0, 32),))
    w_gate = bell_draw(keys[6], (FF, D), D ** -0.5, 0.25, ((0, 32),))
    w_up = bell_draw(keys[7], (FF, D), D ** -0.5, 0.25, ((0, 32),))
    w_down = bell_draw(keys[8], (FF, D), FF ** -0.5, 0.125, ((0, 32),))
    norm_scales = jnp.clip(jax.random.uniform(keys[9], (SCALES,), jnp.float32, -0.5, 0.5) * steps_of(keys[9], (SCALES,), ((0, 32),), -0.4, 0.0), -0.5, 0.5).astype(jnp.bfloat16)
    grad_out = bell_draw(keys[10], (SEQS, SEQ, D), 1.0, 6.0, ((0, 4), (1, 8)), jnp.float32)
    return dict(hidden_in=hidden_in, positions=positions, w_query=w_query, w_key=w_key, w_value=w_value, w_output=w_output, w_gate=w_gate, w_up=w_up, w_down=w_down, norm_scales=norm_scales, grad_out=grad_out)


EPS = 1e-06

def rms_scale(vector, scale):
    return vector * lax.rsqrt(lax.optimization_barrier(jnp.mean(vector * vector, axis=-1, keepdims=True)) + EPS) * (1.0 + scale)

def rotate(vector, position):
    half = vector.shape[-1] // 2
    freq_table = 1000000.0 ** (-jnp.arange(half, dtype=jnp.float32) / half)
    angle = position.astype(jnp.float32)[:, None] * freq_table[None, :]
    cosine = jnp.cos(angle)[:, None, :]
    sine = jnp.sin(angle)[:, None, :]
    first = vector[..., :half]
    second = vector[..., half:]
    return jnp.concatenate([first * cosine - second * sine, second * cosine + first * sine], axis=-1)

def in_piece(resid, scale_in):
    return rms_scale(resid, scale_in)

def qk_piece(query_raw, key_raw, scale_query, scale_key, position):
    query_rot = rotate(rms_scale(query_raw, scale_query), position) * query_raw.shape[-1] ** (-0.5)
    key_rot = rotate(rms_scale(key_raw, scale_key)[:, None, :], position)[:, 0, :]
    return (query_rot, key_rot)

def mid_piece(resid, projected, scale_attn, scale_pre):
    middle = resid + rms_scale(projected, scale_attn)
    return (middle, rms_scale(middle, scale_pre))

def glu_piece(gate, upward):
    return jax.nn.gelu(gate, approximate=True) * upward

def out_piece(middle, ffn, scale_post):
    return middle + rms_scale(ffn, scale_post)

def times_wt(left, weight):
    return lax.dot_general(left, weight, (((1,), (1,)), ((), ())), preferred_element_type=jnp.float32)

def outer_sum(left, right):
    return lax.dot_general(left, right, (((0,), (0,)), ((), ())), preferred_element_type=jnp.float32)

def split_scales(norm_scales, width, head_width):
    scales = norm_scales.astype(jnp.float32)
    pieces = [scales[index * width:(index + 1) * width] for index in range(4)]
    offset = 4 * width
    return pieces + [scales[offset:offset + head_width], scales[offset + head_width:offset + 2 * head_width]]

def to_natural(stored, groups):
    block = stored.shape[0] // (2 * groups)
    trailing = stored.shape[1:]
    shaped = stored.reshape((groups, 2, block) + trailing)
    early = shaped[:, 0].reshape((groups * block,) + trailing)
    late = jnp.flip(shaped[:, 1], axis=0).reshape((groups * block,) + trailing)
    return jnp.concatenate([early, late], axis=0)

def to_stored(natural, groups):
    block = natural.shape[0] // (2 * groups)
    trailing = natural.shape[1:]
    early = natural[:groups * block].reshape((groups, 1, block) + trailing)
    late = jnp.flip(natural[groups * block:].reshape((groups, 1, block) + trailing), axis=0)
    return jnp.concatenate([early, late], axis=1).reshape(natural.shape)

def tile_count(first_row, count, key_tile):
    return (first_row + count + key_tile - 1) // key_tile

def tile_scores(q_rows, key_rows, row_index, tile_no, key_tile):
    first_key = tile_no * key_tile
    key_part = lax.dynamic_slice_in_dim(key_rows, first_key, key_tile, 0)
    scores = lax.dot_general(q_rows, key_part, (((1,), (1,)), ((), ())), preferred_element_type=jnp.float32)
    key_index = first_key + jnp.arange(key_tile, dtype=jnp.int32)
    return jnp.where(key_index[None, :] <= row_index[:, None], scores, -1e+30)

def attend_forward(q_rows, key_rows, values, row_index, tile_total, key_tile):
    row_count = q_rows.shape[0]

    def running(tile_no, state_in):
        row_top, row_sum = state_in
        scores = tile_scores(q_rows, key_rows, row_index, tile_no, key_tile)
        new_top = jnp.maximum(row_top, lax.optimization_barrier(jnp.max(scores, axis=1)))
        row_sum = row_sum * jnp.exp(row_top - new_top) + lax.optimization_barrier(jnp.sum(jnp.exp(scores - new_top[:, None]), axis=1))
        return (new_top, row_sum)
    start_state = (jnp.full((row_count,), -1e+30, jnp.float32), jnp.zeros((row_count,), jnp.float32))
    row_top, row_sum = lax.fori_loop(0, tile_total, running, start_state)
    lse = row_top + jnp.log(row_sum)

    def weigh(tile_no, summed):
        scores = tile_scores(q_rows, key_rows, row_index, tile_no, key_tile)
        weights = jnp.exp(scores - lse[:, None]).astype(jnp.bfloat16)
        value_part = lax.dynamic_slice_in_dim(values, tile_no * key_tile, key_tile, 0)
        return summed + jnp.dot(weights, value_part, preferred_element_type=jnp.float32)
    summed = lax.fori_loop(0, tile_total, weigh, jnp.zeros((row_count, values.shape[1]), jnp.float32))
    return (summed.astype(jnp.bfloat16), lse)

def attend_backward(q_rows, key_rows, values, row_index, tile_total, key_tile, lse, grad_rows, delta, grad_keys, grad_values):

    def step_back(tile_no, state_in):
        grad_q, grad_keys, grad_values = state_in
        first_key = tile_no * key_tile
        scores = tile_scores(q_rows, key_rows, row_index, tile_no, key_tile)
        weights = jnp.exp(scores - lse[:, None])
        key_part = lax.dynamic_slice_in_dim(key_rows, first_key, key_tile, 0)
        value_part = lax.dynamic_slice_in_dim(values, first_key, key_tile, 0)
        grad_weights = times_wt(grad_rows, value_part)
        grad_scores = (weights * (grad_weights - delta[:, None])).astype(jnp.bfloat16)
        grad_q = grad_q + jnp.dot(grad_scores, key_part, preferred_element_type=jnp.float32)
        key_term = outer_sum(grad_scores, q_rows)
        value_term = outer_sum(weights.astype(jnp.bfloat16), grad_rows)
        grad_keys = lax.dynamic_update_slice_in_dim(grad_keys, lax.dynamic_slice_in_dim(grad_keys, first_key, key_tile, 0) + key_term, first_key, 0)
        grad_values = lax.dynamic_update_slice_in_dim(grad_values, lax.dynamic_slice_in_dim(grad_values, first_key, key_tile, 0) + value_term, first_key, 0)
        return (grad_q, grad_keys, grad_values)
    start_state = (jnp.zeros(q_rows.shape, jnp.float32), grad_keys, grad_values)
    return lax.fori_loop(0, tile_total, step_back, start_state)

def reference(hidden_in, positions, w_query, w_key, w_value, w_output, w_gate, w_up, w_down, norm_scales, grad_out):
    scale_in, scale_attn, scale_pre, scale_post, scale_query, scale_key = split_scales(norm_scales, D, HEAD_DIM)
    key_tile = SEQ // 8
    query_len = math.gcd(SEQ, 128)
    block_starts = jnp.arange(SEQ // query_len, dtype=jnp.int32) * query_len

    def one_sequence(totals, inputs):
        rows_in, pos_in, grad_seq = inputs
        resid = to_natural(rows_in, N_CTX)
        posit = to_natural(pos_in, N_CTX)
        grad_nat = to_natural(grad_seq, N_CTX)
        normed = in_piece(resid, scale_in).astype(jnp.bfloat16)
        query_raw = times_wt(normed, w_query).reshape(SEQ, HEADS, HEAD_DIM)
        key_raw = times_wt(normed, w_key)
        value_bf = times_wt(normed, w_value).astype(jnp.bfloat16)
        query_rot, key_rot = qk_piece(query_raw, key_raw, scale_query, scale_key, posit)
        query_bf = query_rot.astype(jnp.bfloat16)
        key_bf = key_rot.astype(jnp.bfloat16)

        def forward_block(unused, first_row):
            q_rows = lax.dynamic_slice_in_dim(query_bf, first_row, query_len, 0).reshape(query_len * HEADS, HEAD_DIM)
            row_index = first_row + jnp.arange(query_len * HEADS, dtype=jnp.int32) // HEADS
            mixed, lse = attend_forward(q_rows, key_bf, value_bf, row_index, tile_count(first_row, query_len, key_tile), key_tile)
            return (unused, (mixed.reshape(query_len, HEADS * HEAD_DIM), lse))
        _, (attn_bf, lse_all) = lax.scan(forward_block, jnp.zeros((), jnp.int32), block_starts)
        attn_bf = attn_bf.reshape(SEQ, HEADS * HEAD_DIM)
        projected = jnp.dot(attn_bf, w_output, preferred_element_type=jnp.float32)
        (middle, pre_ffn), mid_back = jax.vjp(mid_piece, resid, projected, scale_attn, scale_pre)
        pre_bf = pre_ffn.astype(jnp.bfloat16)
        gate = times_wt(pre_bf, w_gate)
        upward = times_wt(pre_bf, w_up)
        inner, glu_back = jax.vjp(glu_piece, gate, upward)
        inner_bf = inner.astype(jnp.bfloat16)
        ffn = jnp.dot(inner_bf, w_down, preferred_element_type=jnp.float32)
        block_out, out_back = jax.vjp(out_piece, middle, ffn, scale_post)
        grad_mid, grad_ffn, grad_scale_post = out_back(grad_nat)
        grad_ffn_bf = grad_ffn.astype(jnp.bfloat16)
        grad_inner = times_wt(grad_ffn_bf, w_down)
        grad_w_down = outer_sum(inner_bf, grad_ffn_bf)
        grad_gate, grad_upward = glu_back(grad_inner)
        gate_bf = grad_gate.astype(jnp.bfloat16)
        upward_bf = grad_upward.astype(jnp.bfloat16)
        grad_pre = jnp.dot(gate_bf, w_gate, preferred_element_type=jnp.float32) + jnp.dot(upward_bf, w_up, preferred_element_type=jnp.float32)
        grad_w_gate = outer_sum(gate_bf, pre_bf)
        grad_w_up = outer_sum(upward_bf, pre_bf)
        grad_resid_a, grad_proj, grad_scale_attn, grad_scale_pre = mid_back((grad_mid, grad_pre))
        grad_proj_bf = grad_proj.astype(jnp.bfloat16)
        grad_attn_bf = times_wt(grad_proj_bf, w_output).astype(jnp.bfloat16)
        grad_w_output = outer_sum(attn_bf, grad_proj_bf)

        def backward_block(state_in, inputs):
            grad_keys, grad_values = state_in
            first_row, lse = inputs
            q_rows = lax.dynamic_slice_in_dim(query_bf, first_row, query_len, 0).reshape(query_len * HEADS, HEAD_DIM)
            grad_rows = lax.dynamic_slice_in_dim(grad_attn_bf, first_row, query_len, 0).reshape(query_len * HEADS, HEAD_DIM)
            out_rows = lax.dynamic_slice_in_dim(attn_bf, first_row, query_len, 0).reshape(query_len * HEADS, HEAD_DIM)
            delta = lax.optimization_barrier(jnp.sum(grad_rows.astype(jnp.float32) * out_rows.astype(jnp.float32), axis=1))
            row_index = first_row + jnp.arange(query_len * HEADS, dtype=jnp.int32) // HEADS
            grad_q, grad_keys, grad_values = attend_backward(q_rows, key_bf, value_bf, row_index, tile_count(first_row, query_len, key_tile), key_tile, lse, grad_rows, delta, grad_keys, grad_values)
            return ((grad_keys, grad_values), grad_q.reshape(query_len, HEADS, HEAD_DIM))
        zero_rows = jnp.zeros((SEQ, HEAD_DIM), jnp.float32)
        (grad_key_rot, grad_value), grad_query_rot = lax.scan(backward_block, (zero_rows, zero_rows), (block_starts, lse_all))
        grad_query_rot = grad_query_rot.reshape(SEQ, HEADS, HEAD_DIM)
        _, qk_back = jax.vjp(partial(qk_piece, position=posit), query_raw, key_raw, scale_query, scale_key)
        grad_qraw, grad_kraw, grad_scale_query, grad_scale_key = qk_back((grad_query_rot, grad_key_rot))
        grad_qraw_bf = grad_qraw.reshape(SEQ, HEADS * HEAD_DIM).astype(jnp.bfloat16)
        grad_kraw_bf = grad_kraw.astype(jnp.bfloat16)
        grad_value_bf = grad_value.astype(jnp.bfloat16)
        grad_normed = jnp.dot(grad_qraw_bf, w_query, preferred_element_type=jnp.float32) + jnp.dot(grad_kraw_bf, w_key, preferred_element_type=jnp.float32) + jnp.dot(grad_value_bf, w_value, preferred_element_type=jnp.float32)
        grad_w_query = outer_sum(grad_qraw_bf, normed)
        grad_w_key = outer_sum(grad_kraw_bf, normed)
        grad_w_value = outer_sum(grad_value_bf, normed)
        _, in_back = jax.vjp(in_piece, resid, scale_in)
        grad_resid_b, grad_scale_in = in_back(grad_normed)
        grad_scales = jnp.concatenate([grad_scale_in, grad_scale_attn, grad_scale_pre, grad_scale_post, grad_scale_query, grad_scale_key])
        terms = (grad_w_query, grad_w_key, grad_w_value, grad_w_output, grad_w_gate, grad_w_up, grad_w_down, grad_scales)
        totals = jax.tree.map(lambda total, term: total + term, totals, terms)
        return (totals, (to_stored(block_out, N_CTX), to_stored(grad_resid_a + grad_resid_b, N_CTX)))
    start_totals = (jnp.zeros((HEADS * HEAD_DIM, D), jnp.float32), jnp.zeros((HEAD_DIM, D), jnp.float32), jnp.zeros((HEAD_DIM, D), jnp.float32), jnp.zeros((HEADS * HEAD_DIM, D), jnp.float32), jnp.zeros((FF, D), jnp.float32), jnp.zeros((FF, D), jnp.float32), jnp.zeros((FF, D), jnp.float32), jnp.zeros((SCALES,), jnp.float32))
    totals, (block_out, grad_in) = lax.scan(one_sequence, start_totals, (hidden_in, positions, grad_out))
    return (block_out, grad_in, totals[0], totals[1], totals[2], totals[3], totals[4], totals[5], totals[6], totals[7])
```

```python
import jax
import jax.numpy as jnp
from jax import lax
from jax.sharding import PartitionSpec as P

EPS = 1e-06


def rms_scale(vector, scale):
    return (
        vector * lax.rsqrt(jnp.mean(vector * vector, axis=-1, keepdims=True) + EPS) * (1.0 + scale)
    )


def rotate(vector, position):
    half = vector.shape[-1] // 2
    freq_table = 1000000.0 ** (-jnp.arange(half, dtype=jnp.float32) / half)
    angle = position.astype(jnp.float32)[:, None] * freq_table[None, :]
    cosine = jnp.cos(angle)[:, None, :]
    sine = jnp.sin(angle)[:, None, :]
    first = vector[..., :half]
    second = vector[..., half:]
    return jnp.concatenate(
        [first * cosine - second * sine, second * cosine + first * sine], axis=-1
    )


def mid_piece(resid, projected, scale_attn, scale_pre):
    middle = resid + rms_scale(projected, scale_attn)
    return (middle, rms_scale(middle, scale_pre))


def glu_piece(gate, upward):
    return jax.nn.gelu(gate, approximate=True) * upward


def out_piece(middle, ffn, scale_post):
    return middle + rms_scale(ffn, scale_post)


def times_wt(left, weight):
    return lax.dot_general(
        left, weight, (((1,), (1,)), ((), ())), preferred_element_type=jnp.float32
    )


def outer_sum(left, right):
    return lax.dot_general(
        left, right, (((0,), (0,)), ((), ())), preferred_element_type=jnp.float32
    )


def split_scales(norm_scales, width, head_width):
    scales = norm_scales.astype(jnp.float32)
    pieces = [scales[index * width : (index + 1) * width] for index in range(4)]
    offset = 4 * width
    return pieces + [
        scales[offset : offset + head_width],
        scales[offset + head_width : offset + 2 * head_width],
    ]


BF = jnp.bfloat16


def swap_dp(block, bits):
    count = lax.axis_size("dp")
    return lax.ppermute(block, "dp", [(place, place ^ bits) for place in range(count)])


def swap_ctx(block, bits):
    count = lax.axis_size("ctx")
    return lax.ppermute(block, "ctx", [(place, place ^ bits) for place in range(count)])


def swap_z(block, bits):
    return swap_ctx(block, 2 * bits)


def gather_over(block, swap, count):
    if count <= 4:
        return jnp.concatenate([block] + [swap(block, bits) for bits in range(1, count)], axis=0)
    bits = 1
    while bits < count:
        block = jnp.concatenate([block, swap(block, bits)], axis=0)
        bits = 2 * bits
    return block


def add_bf16(first, *others):
    total = first.astype(jnp.float32)
    for other in others:
        total = total + other.astype(jnp.float32)
    return total


def scatter_over(blocks, swap, count):
    if count <= 4:
        return add_bf16(blocks[0], *[swap(blocks[bits], bits) for bits in range(1, count)])
    bits = count // 2
    while bits > 1:
        blocks = add_bf16(blocks[:bits], swap(blocks[bits:], bits)).astype(BF)
        bits = bits // 2
    return add_bf16(blocks[0], swap(blocks[1], 1))


def gather_chip(block):
    groups = lax.axis_size("ctx") // 2
    over_z = gather_over(block[None], swap_z, groups)
    over_dp = gather_over(over_z[None], swap_dp, lax.axis_size("dp"))
    return over_dp.reshape((-1,) + block.shape[1:])


def scatter_chip(blocks):
    groups = lax.axis_size("ctx") // 2
    count = lax.axis_size("dp")
    shaped = blocks.reshape((count, groups, -1) + blocks.shape[1:])
    mid = scatter_over(shaped, swap_dp, count).astype(BF)
    return scatter_over(mid, swap_z, groups)


def scatter_all(first, second):
    return scatter_chip(add_bf16(first, swap_ctx(second, 1)).astype(BF))


def natural_rows(places, block, groups):
    within = jnp.arange(2 * block, dtype=jnp.int32)[None, :]
    early = places[:, None] * block + within
    late = (2 * groups - 1 - places[:, None]) * block + within - block
    return jnp.where(within < block, early, late).reshape(-1)


def row_order(owner_of, rows):
    count = owner_of.shape[0] * rows
    held = (owner_of[:, None] * rows + jnp.arange(rows, dtype=jnp.int32)[None, :]).reshape(1, count)
    return (jnp.arange(count, dtype=jnp.int32)[:, None] == held).astype(BF)


def reorder(order, blocks):
    return jnp.dot(order, blocks, preferred_element_type=jnp.float32).astype(BF)


def reorder_back(order, blocks):
    return outer_sum(order, blocks.astype(BF)).astype(BF)


def rms_back(unit, inverse, grad_scaled):
    return inverse * (grad_scaled - unit * jnp.mean(grad_scaled * unit, axis=-1, keepdims=True))


def shards(
    hidden_in,
    positions,
    w_query,
    w_key,
    w_value,
    w_output,
    w_gate,
    w_up,
    w_down,
    norm_scales,
    grad_out,
):
    width = hidden_in.shape[2]
    groups = lax.axis_size("ctx")
    count_dp = lax.axis_size("dp")
    chips = groups // 2
    owners = count_dp * groups
    place = lax.axis_index("ctx")
    row = lax.axis_index("dp")
    resid = hidden_in[0]
    posit = positions[0]
    grad_nat = grad_out[0]
    tokens = resid.shape[0]
    block = tokens // 2
    head_width = w_key.shape[0] * owners
    heads = w_query.shape[0] * owners // head_width
    rows_q, rows_k = w_query.shape[0], w_key.shape[0]
    scale_part = norm_scales.shape[0]

    scale_rows = jnp.zeros((8, width), BF).at[0, :scale_part].set(norm_scales)
    first = gather_chip(jnp.concatenate([w_query, w_key, w_value, scale_rows], axis=0))
    inverse_in = lax.rsqrt(jnp.mean(resid * resid, axis=-1, keepdims=True) + EPS)
    unit_in = resid * inverse_in
    place_rows = jnp.zeros((8, width), BF)
    place_rows = place_rows.at[0, :tokens].set((posit // 64).astype(BF))
    place_rows = place_rows.at[1, :tokens].set((posit % 64).astype(BF))
    seq_part = jnp.concatenate([unit_in.astype(BF), place_rows], axis=0)
    seq_z = gather_over(seq_part[None], swap_z, chips)
    seq_all = jnp.concatenate([seq_z, swap_ctx(seq_z, 1)], axis=0)
    out_chip = gather_chip(w_output)
    gate_chip = gather_chip(w_gate)
    up_chip = gather_chip(w_up)
    down_chip = gather_chip(w_down)

    first = jnp.concatenate([first, swap_ctx(first, 1)], axis=0).reshape(owners, -1, width)
    far_core, far_dp, far_z = (
        jnp.arange(owners, dtype=jnp.int32) // (owners // 2),
        (jnp.arange(owners, dtype=jnp.int32) // chips) % count_dp,
        jnp.arange(owners, dtype=jnp.int32) % chips,
    )
    owner_of = (row ^ far_dp) * groups + (place ^ (2 * far_z + far_core))
    order_q = row_order(owner_of, rows_q)
    order_k = row_order(owner_of, rows_k)
    order_s = row_order(owner_of, 1)
    full_query = reorder(order_q, first[:, :rows_q].reshape(-1, width))
    full_key = reorder(order_k, first[:, rows_q : rows_q + rows_k].reshape(-1, width))
    full_value = reorder(order_k, first[:, rows_q + rows_k : rows_q + 2 * rows_k].reshape(-1, width))
    full_scales = reorder(order_s, first[:, rows_q + 2 * rows_k, :scale_part]).reshape(-1)
    scale_in, scale_attn, scale_pre, scale_post, scale_query, scale_key = split_scales(
        full_scales, width, head_width
    )

    seq_len = groups * tokens
    seq_core, seq_zed = (
        jnp.arange(groups, dtype=jnp.int32) // chips,
        jnp.arange(groups, dtype=jnp.int32) % chips,
    )
    key_index = natural_rows(place ^ (2 * seq_zed + seq_core), block, groups)
    row_index = natural_rows(place[None], block, groups)
    unit_all = seq_all[:, :tokens].reshape(seq_len, width).astype(jnp.float32)
    pos_all = (
        seq_all[:, tokens, :tokens].astype(jnp.int32) * 64
        + seq_all[:, tokens + 1, :tokens].astype(jnp.int32)
    ).reshape(seq_len)
    normed = (unit_in * (1.0 + scale_in)).astype(BF)
    normed_all = (unit_all * (1.0 + scale_in)).astype(BF)

    query_raw = times_wt(normed, full_query).reshape(tokens, heads, head_width)
    key_raw = times_wt(normed_all, full_key)
    value_bf = times_wt(normed_all, full_value).astype(BF)

    def query_piece(raw, scale):
        return rotate(rms_scale(raw, scale), posit) * head_width ** (-0.5)

    def key_piece(raw, scale):
        return rotate(rms_scale(raw, scale)[:, None, :], pos_all)[:, 0, :]

    query_rot, query_back = jax.vjp(query_piece, query_raw, scale_query)
    key_rot, key_back = jax.vjp(key_piece, key_raw, scale_key)
    query_bf = jnp.swapaxes(query_rot.astype(BF), 0, 1).reshape(heads * tokens, head_width)
    key_bf = key_rot.astype(BF)
    allowed = jnp.tile(key_index[None, :] <= row_index[:, None], (heads, 1))
    scores = jnp.where(allowed, times_wt(query_bf, key_bf), -1e30)
    top = jnp.max(scores, axis=1, keepdims=True)
    lse = top + jnp.log(jnp.sum(jnp.exp(scores - top), axis=1, keepdims=True))
    probs = jnp.exp(scores - lse)
    probs_bf = probs.astype(BF)
    mixed = jnp.dot(probs_bf, value_bf, preferred_element_type=jnp.float32).astype(BF)
    attn_bf = jnp.swapaxes(mixed.reshape(heads, tokens, head_width), 0, 1).reshape(tokens, -1)

    full_output = reorder(order_q, jnp.concatenate([out_chip, swap_ctx(out_chip, 1)], axis=0))
    projected = jnp.dot(attn_bf, full_output, preferred_element_type=jnp.float32)
    (middle, pre_ffn), mid_back = jax.vjp(mid_piece, resid, projected, scale_attn, scale_pre)
    pre_bf = pre_ffn.astype(BF)
    gates = (gate_chip, swap_ctx(gate_chip, 1))
    ups = (up_chip, swap_ctx(up_chip, 1))
    downs = (down_chip, swap_ctx(down_chip, 1))
    inners, glu_backs = [], []
    for half_no in range(2):
        inner, glu_back = jax.vjp(
            glu_piece, times_wt(pre_bf, gates[half_no]), times_wt(pre_bf, ups[half_no])
        )
        inners.append(inner.astype(BF))
        glu_backs.append(glu_back)
    ffn = sum(
        jnp.dot(inners[half_no], downs[half_no], preferred_element_type=jnp.float32)
        for half_no in range(2)
    )
    block_out, out_back = jax.vjp(out_piece, middle, ffn, scale_post)
    grad_mid, grad_ffn, grad_scale_post = out_back(grad_nat)
    grad_ffn_bf = grad_ffn.astype(BF)
    grad_pre = 0.0
    downs_grad, gates_grad, ups_grad = [], [], []
    for half_no in range(2):
        grad_gate, grad_upward = glu_backs[half_no](times_wt(grad_ffn_bf, downs[half_no]))
        gate_bf = grad_gate.astype(BF)
        upward_bf = grad_upward.astype(BF)
        grad_pre = grad_pre + (
            jnp.dot(gate_bf, gates[half_no], preferred_element_type=jnp.float32)
            + jnp.dot(upward_bf, ups[half_no], preferred_element_type=jnp.float32)
        )
        downs_grad.append(outer_sum(inners[half_no], grad_ffn_bf).astype(BF))
        gates_grad.append(outer_sum(gate_bf, pre_bf).astype(BF))
        ups_grad.append(outer_sum(upward_bf, pre_bf).astype(BF))
    own_down = scatter_all(*downs_grad)
    own_gate = scatter_all(*gates_grad)
    own_up = scatter_all(*ups_grad)
    grad_resid_a, grad_proj, grad_scale_attn, grad_scale_pre = mid_back((grad_mid, grad_pre))
    grad_proj_bf = grad_proj.astype(BF)
    grad_attn_bf = times_wt(grad_proj_bf, full_output).astype(BF)
    out_grad = reorder_back(order_q, outer_sum(attn_bf, grad_proj_bf))
    own_output = scatter_all(out_grad[: out_grad.shape[0] // 2], out_grad[out_grad.shape[0] // 2 :])

    grad_rows = jnp.swapaxes(grad_attn_bf.reshape(tokens, heads, head_width), 0, 1).reshape(
        heads * tokens, head_width
    )
    delta = jnp.sum(
        grad_rows.astype(jnp.float32) * mixed.astype(jnp.float32), axis=1, keepdims=True
    )
    grad_scores = (probs * (times_wt(grad_rows, value_bf) - delta)).astype(BF)
    grad_query = jnp.dot(grad_scores, key_bf, preferred_element_type=jnp.float32)
    grad_query = jnp.swapaxes(grad_query.reshape(heads, tokens, head_width), 0, 1)
    grad_key = outer_sum(grad_scores, query_bf)
    grad_value_bf = outer_sum(probs_bf, grad_rows).astype(BF)
    grad_qraw, grad_scale_query = query_back(grad_query)
    grad_kraw, grad_scale_key = key_back(grad_key)
    grad_qraw_bf = grad_qraw.reshape(tokens, heads * head_width).astype(BF)
    grad_kraw_bf = grad_kraw.astype(BF)

    grad_normed_q = jnp.dot(grad_qraw_bf, full_query, preferred_element_type=jnp.float32)
    grad_normed = jnp.dot(grad_kraw_bf, full_key, preferred_element_type=jnp.float32) + jnp.dot(
        grad_value_bf, full_value, preferred_element_type=jnp.float32
    )
    grad_scale_in = jnp.sum(grad_normed * unit_all, axis=0) + jnp.sum(
        grad_normed_q * unit_in, axis=0
    )
    far = grad_normed.astype(BF).reshape(2, chips, tokens, width)
    far_sum = add_bf16(far[0], swap_ctx(far[1], 1)).astype(BF)
    own_normed = scatter_over(far_sum, swap_z, chips) + grad_normed_q
    grad_w_query = reorder_back(order_q, outer_sum(grad_qraw_bf, normed))
    grad_w_key = reorder_back(order_k, outer_sum(grad_kraw_bf, normed_all))
    grad_w_value = reorder_back(order_k, outer_sum(grad_value_bf, normed_all))
    grad_scales = jnp.concatenate(
        [
            grad_scale_in,
            grad_scale_attn,
            grad_scale_pre,
            grad_scale_post,
            grad_scale_query,
            grad_scale_key,
        ]
    ).reshape(owners, scale_part)
    scales_back = reorder_back(order_s, grad_scales)
    packed = jnp.concatenate(
        [
            grad_w_query.reshape(owners, rows_q, width),
            grad_w_key.reshape(owners, rows_k, width),
            grad_w_value.reshape(owners, rows_k, width),
            jnp.zeros((owners, 8, width), BF).at[:, 0, :scale_part].set(scales_back),
        ],
        axis=1,
    ).reshape(2, -1, width)
    own_first = scatter_all(packed[0], packed[1])
    own_query = own_first[:rows_q]
    own_key = own_first[rows_q : rows_q + rows_k]
    own_value = own_first[rows_q + rows_k : rows_q + 2 * rows_k]
    own_scales = own_first[rows_q + 2 * rows_k, :scale_part]
    grad_resid = grad_resid_a + rms_back(unit_in, inverse_in, own_normed * (1.0 + scale_in))
    return (
        block_out[None],
        grad_resid[None],
        own_query,
        own_key,
        own_value,
        own_output,
        own_gate,
        own_up,
        own_down,
        own_scales,
    )


def solution(mesh):
    in_specs = (
        P("dp", "ctx", None),
        P("dp", "ctx"),
        P(("dp", "ctx"), None),
        P(("dp", "ctx"), None),
        P(("dp", "ctx"), None),
        P(("dp", "ctx"), None),
        P(("dp", "ctx"), None),
        P(("dp", "ctx"), None),
        P(("dp", "ctx"), None),
        P(("dp", "ctx")),
        P("dp", "ctx", None),
    )
    out_specs = (
        P("dp", "ctx", None),
        P("dp", "ctx", None),
        P(("dp", "ctx"), None),
        P(("dp", "ctx"), None),
        P(("dp", "ctx"), None),
        P(("dp", "ctx"), None),
        P(("dp", "ctx"), None),
        P(("dp", "ctx"), None),
        P(("dp", "ctx"), None),
        P(("dp", "ctx")),
    )
    return jax.shard_map(shards, mesh=mesh, in_specs=in_specs, out_specs=out_specs, check_vma=False)
```

```python
import jax
import jax.numpy as jnp
from jax import lax
from jax.experimental import pallas as pl
from jax.experimental.pallas import tpu as pltpu
from jax.sharding import PartitionSpec as P

EPS = 1e-06


def rms_scale(vector, scale):
    return (
        vector * lax.rsqrt(jnp.mean(vector * vector, axis=-1, keepdims=True) + EPS) * (1.0 + scale)
    )


def rotate(vector, position):
    half = vector.shape[-1] // 2
    freq_table = 1000000.0 ** (-jnp.arange(half, dtype=jnp.float32) / half)
    angle = position.astype(jnp.float32)[:, None] * freq_table[None, :]
    cosine = jnp.cos(angle)[:, None, :]
    sine = jnp.sin(angle)[:, None, :]
    first = vector[..., :half]
    second = vector[..., half:]
    return jnp.concatenate(
        [first * cosine - second * sine, second * cosine + first * sine], axis=-1
    )


def mid_piece(resid, projected, scale_attn, scale_pre):
    middle = resid + rms_scale(projected, scale_attn)
    return (middle, rms_scale(middle, scale_pre))


def glu_piece(gate, upward):
    return jax.nn.gelu(gate, approximate=True) * upward


def out_piece(middle, ffn, scale_post):
    return middle + rms_scale(ffn, scale_post)


def times_wt(left, weight):
    return lax.dot_general(
        left, weight, (((1,), (1,)), ((), ())), preferred_element_type=jnp.float32
    )


def outer_sum(left, right):
    return lax.dot_general(
        left, right, (((0,), (0,)), ((), ())), preferred_element_type=jnp.float32
    )


def split_scales(norm_scales, width, head_width):
    scales = norm_scales.astype(jnp.float32)
    pieces = [scales[index * width : (index + 1) * width] for index in range(4)]
    offset = 4 * width
    return pieces + [
        scales[offset : offset + head_width],
        scales[offset + head_width : offset + 2 * head_width],
    ]


BF = jnp.bfloat16


def swap_dp(block, bits):
    count = lax.axis_size("dp")
    return lax.ppermute(block, "dp", [(place, place ^ bits) for place in range(count)])


def swap_ctx(block, bits):
    count = lax.axis_size("ctx")
    return lax.ppermute(block, "ctx", [(place, place ^ bits) for place in range(count)])


def swap_z(block, bits):
    return swap_ctx(block, 2 * bits)


def gather_over(block, swap, count):
    if count <= 4:
        return jnp.concatenate([block] + [swap(block, bits) for bits in range(1, count)], axis=0)
    bits = 1
    while bits < count:
        block = jnp.concatenate([block, swap(block, bits)], axis=0)
        bits = 2 * bits
    return block


def add_bf16(first, *others):
    total = first.astype(jnp.float32)
    for other in others:
        total = total + other.astype(jnp.float32)
    return total


def scatter_over(blocks, swap, count):
    if count <= 4:
        return add_bf16(blocks[0], *[swap(blocks[bits], bits) for bits in range(1, count)])
    bits = count // 2
    while bits > 1:
        blocks = add_bf16(blocks[:bits], swap(blocks[bits:], bits)).astype(BF)
        bits = bits // 2
    return add_bf16(blocks[0], swap(blocks[1], 1))


def gather_chip(block):
    groups = lax.axis_size("ctx") // 2
    over_z = gather_over(block[None], swap_z, groups)
    over_dp = gather_over(over_z[None], swap_dp, lax.axis_size("dp"))
    return over_dp.reshape((-1,) + block.shape[1:])


def double(blocks, swap, bits):
    return jnp.concatenate([blocks, swap(blocks, bits)], axis=0)


def double_inner(blocks, swap, bits):
    pair = blocks.reshape((2, 1, -1) + blocks.shape[1:])
    return jnp.concatenate([pair, swap(pair, bits)], axis=1).reshape((-1,) + blocks.shape[1:])


def halve(blocks, swap, bits):
    half = blocks.shape[0] // 2
    return add_bf16(blocks[:half], swap(blocks[half:], bits)).astype(BF)


def halve_inner(blocks, swap, bits):
    quarters = blocks.reshape((2, 2, -1) + blocks.shape[1:])
    half = add_bf16(quarters[:, 0], swap(quarters[:, 1], bits)).astype(BF)
    return half.reshape((-1,) + blocks.shape[1:])


def scatter_chip(blocks):
    groups = lax.axis_size("ctx") // 2
    count = lax.axis_size("dp")
    shaped = blocks.reshape((count, groups, -1) + blocks.shape[1:])
    mid = scatter_over(shaped, swap_dp, count).astype(BF)
    return scatter_over(mid, swap_z, groups)


def scatter_all(first, second):
    return scatter_chip(add_bf16(first, swap_ctx(second, 1)).astype(BF))


def natural_rows(places, block, groups):
    within = jnp.arange(2 * block, dtype=jnp.int32)[None, :]
    early = places[:, None] * block + within
    late = (2 * groups - 1 - places[:, None]) * block + within - block
    return jnp.where(within < block, early, late).reshape(-1)


def row_order(owner_of, rows):
    count = owner_of.shape[0] * rows
    held = (owner_of[:, None] * rows + jnp.arange(rows, dtype=jnp.int32)[None, :]).reshape(1, count)
    return (jnp.arange(count, dtype=jnp.int32)[:, None] == held).astype(BF)


def reorder(order, blocks):
    return jnp.dot(order, blocks, preferred_element_type=jnp.float32).astype(BF)


def reorder_back(order, blocks):
    return outer_sum(order, blocks.astype(BF)).astype(BF)


def rms_back(unit, inverse, grad_scaled):
    return inverse * (grad_scaled - unit * jnp.mean(grad_scaled * unit, axis=-1, keepdims=True))


def dot_nt(left, right):
    return lax.dot_general(left, right, (((1,), (1,)), ((), ())), preferred_element_type=jnp.float32)


def dot_nn(left, right):
    return lax.dot_general(left, right, (((1,), (0,)), ((), ())), preferred_element_type=jnp.float32)


def dot_tn(left, right):
    return lax.dot_general(left, right, (((0,), (0,)), ((), ())), preferred_element_type=jnp.float32)


def unit_of(rows):
    inverse = lax.rsqrt(jnp.mean(rows * rows, axis=-1, keepdims=True) + EPS)
    return rows * inverse, inverse


def turn(rows, cosine, sine):
    half = rows.shape[1] // 2
    first, second = rows[:, :half], rows[:, half:]
    return jnp.concatenate([first * cosine - second * sine, second * cosine + first * sine], axis=1)


def turn_back(rows, cosine, sine):
    half = rows.shape[1] // 2
    first, second = rows[:, :half], rows[:, half:]
    return jnp.concatenate([first * cosine + second * sine, second * cosine - first * sine], axis=1)


def call_kernel(body, out_shapes, scratch, flops, inputs):
    whole = pl.BlockSpec(memory_space=pltpu.VMEM)
    return pl.pallas_call(
        body,
        out_shape=[jax.ShapeDtypeStruct(shape, dtype) for shape, dtype in out_shapes],
        in_specs=[whole] * len(inputs),
        out_specs=[whole] * len(out_shapes),
        scratch_shapes=[pltpu.VMEM(shape, dtype) for shape, dtype in scratch],
        compiler_params=pltpu.CompilerParams(vmem_limit_bytes=52 * 1024 * 1024),
        cost_estimate=pl.CostEstimate(flops=flops, bytes_accessed=20_000_000, transcendentals=0),
    )(*inputs)


def attend_kernel(
    unit_ref, near_ref, far_ref, wq_ref, wk_ref, wv_ref, sin_scale_ref, sq_ref, sk_ref,
    cos_ref, sine_ref, cos_all_ref, sine_all_ref, key_index_ref, row_index_ref,
    normed_ref, normed_all_ref, qraw_ref, kraw_ref, q_ref, k_ref, v_ref, attn_ref, lse_ref,
):
    scale_in = 1.0 + sin_scale_ref[...]
    normed_ref[...] = (unit_ref[...] * scale_in).astype(BF)
    half = near_ref.shape[0]
    normed_all_ref[:half] = (near_ref[...].astype(jnp.float32) * scale_in).astype(BF)
    normed_all_ref[half:] = (far_ref[...].astype(jnp.float32) * scale_in).astype(BF)
    head_width = wk_ref.shape[0]
    heads = wq_ref.shape[0] // head_width
    key_raw = dot_nt(normed_all_ref[...], wk_ref[...])
    kraw_ref[...] = key_raw
    v_ref[...] = dot_nt(normed_all_ref[...], wv_ref[...]).astype(BF)
    key_unit, _ = unit_of(key_raw)
    k_ref[...] = turn(key_unit * (1.0 + sk_ref[...]), cos_all_ref[...], sine_all_ref[...]).astype(BF)
    allowed = key_index_ref[...] <= row_index_ref[...]
    for head in range(heads):
        span = slice(head * head_width, (head + 1) * head_width)
        raw = dot_nt(normed_ref[...], wq_ref[span, :])
        qraw_ref[:, span] = raw
        unit, _ = unit_of(raw)
        turned = turn(unit * (1.0 + sq_ref[...]), cos_ref[...], sine_ref[...])
        query = (turned * head_width ** (-0.5)).astype(BF)
        q_ref[:, span] = query
        scores = jnp.where(allowed, dot_nt(query, k_ref[...]), -1e30)
        top = jnp.max(scores, axis=1, keepdims=True)
        lse = top + jnp.log(jnp.sum(jnp.exp(scores - top), axis=1, keepdims=True))
        lse_ref[:, head : head + 1] = lse
        probs = jnp.exp(scores - lse).astype(BF)
        attn_ref[:, span] = dot_nn(probs, v_ref[...]).astype(BF)


def attend_back_kernel(
    grad_attn_ref, attn_ref, q_ref, k_ref, v_ref, lse_ref, qraw_ref, kraw_ref, wq_ref, wk_ref, wv_ref,
    sq_ref, sk_ref, cos_ref, sine_ref, cos_all_ref, sine_all_ref, key_index_ref, row_index_ref,
    normed_ref, normed_all_ref, unit_ref, near_ref, far_ref,
    gwq_ref, gwk_ref, gwv_ref, gnear_ref, gfar_ref, gq_ref, gsin_ref, gsq_ref, gsk_ref,
    probs_scr, gscores_scr, grows_scr, qrows_scr, gqraw_scr,
):
    head_width = wk_ref.shape[0]
    heads = wq_ref.shape[0] // head_width
    tokens = q_ref.shape[0]
    allowed = key_index_ref[...] <= row_index_ref[...]
    grad_sq = jnp.zeros((1, head_width), jnp.float32)
    for head in range(heads):
        span = slice(head * head_width, (head + 1) * head_width)
        rows = slice(head * tokens, (head + 1) * tokens)
        query = q_ref[:, span]
        grad_rows = grad_attn_ref[:, span]
        delta = jnp.sum(
            grad_rows.astype(jnp.float32) * attn_ref[:, span].astype(jnp.float32),
            axis=1,
            keepdims=True,
        )
        scores = jnp.where(allowed, dot_nt(query, k_ref[...]), -1e30)
        probs = jnp.exp(scores - lse_ref[:, head : head + 1])
        grad_scores = (probs * (dot_nt(grad_rows, v_ref[...]) - delta)).astype(BF)
        probs_scr[rows, :] = probs.astype(BF)
        gscores_scr[rows, :] = grad_scores
        grows_scr[rows, :] = grad_rows
        qrows_scr[rows, :] = query
        grad_query = dot_nn(grad_scores, k_ref[...]) * head_width ** (-0.5)
        grad_query = turn_back(grad_query, cos_ref[...], sine_ref[...])
        unit, inverse = unit_of(qraw_ref[:, span])
        grad_sq = grad_sq + jnp.sum(grad_query * unit, axis=0, keepdims=True)
        grad_raw = rms_back(unit, inverse, grad_query * (1.0 + sq_ref[...]))
        gqraw_scr[:, span] = grad_raw.astype(BF)
    gsq_ref[...] = grad_sq
    grad_key = dot_tn(gscores_scr[...], qrows_scr[...])
    grad_value = dot_tn(probs_scr[...], grows_scr[...]).astype(BF)
    grad_key = turn_back(grad_key, cos_all_ref[...], sine_all_ref[...])
    unit, inverse = unit_of(kraw_ref[...])
    gsk_ref[...] = jnp.sum(grad_key * unit, axis=0, keepdims=True)
    grad_kraw = rms_back(unit, inverse, grad_key * (1.0 + sk_ref[...])).astype(BF)
    half = near_ref.shape[0]
    grad_normed = dot_nn(grad_kraw, wk_ref[...]) + dot_nn(grad_value, wv_ref[...])
    grad_q = dot_nn(gqraw_scr[...], wq_ref[...])
    gq_ref[...] = grad_q
    gsin_ref[...] = (
        jnp.sum(grad_normed[:half] * near_ref[...].astype(jnp.float32), axis=0, keepdims=True)
        + jnp.sum(grad_normed[half:] * far_ref[...].astype(jnp.float32), axis=0, keepdims=True)
        + jnp.sum(grad_q * unit_ref[...], axis=0, keepdims=True)
    )
    gnear_ref[...] = grad_normed[:half].astype(BF)
    gfar_ref[...] = grad_normed[half:].astype(BF)
    gwk_ref[...] = dot_tn(grad_kraw, normed_all_ref[...]).astype(BF)
    gwv_ref[...] = dot_tn(grad_value, normed_all_ref[...]).astype(BF)
    gwq_ref[...] = dot_tn(gqraw_scr[...], normed_ref[...]).astype(BF)


GELU_A = (2.0 / 3.141592653589793) ** 0.5


def mid_kernel(*refs):
    attn_ref, order_ref, resid_ref, gout_ref, sattn_ref, spre_ref, spost_ref = refs[:7]
    a_refs = (refs[7:9], refs[9:11])
    b_refs = (refs[11:13], refs[13:15])
    block_out_ref, gresid_ref, gattn_ref, gsattn_ref, gspre_ref, gspost_ref = refs[15:21]
    ga_refs = (refs[21:23], refs[23:25])
    gb_refs = (refs[25:27], refs[27:29])
    held_scr, ahead_scr, gate_scr, up_scr, inner_scr = refs[29:]
    chips = a_refs[0][0].shape[0] // 2
    width = resid_ref.shape[1]
    rows_f = b_refs[0][0].shape[1] // 2
    rows_o = a_refs[0][0].shape[1] - rows_f
    chunk = chips * rows_f

    def place_a(dp):
        return dp // 2, slice((dp % 2) * chips, (dp % 2 + 1) * chips)

    def place_b(dp):
        return dp % 2, slice((dp // 2) * chips, (dp // 2 + 1) * chips)

    def weights(core, dp):
        piece_a, at_a = place_a(dp)
        piece_b, at_b = place_b(dp)
        gate = a_refs[core][piece_a][at_a, :rows_f, :].reshape(chunk, width)
        up = b_refs[core][piece_b][at_b, :rows_f, :].reshape(chunk, width)
        down = b_refs[core][piece_b][at_b, rows_f:, :].reshape(chunk, width)
        return gate, up, down

    parts = [(core, dp) for core in range(2) for dp in range(4)]
    out_chunk = chips * rows_o
    for number, (core, dp) in enumerate(parts):
        piece, at = place_a(dp)
        held_scr[number * out_chunk : (number + 1) * out_chunk, :] = a_refs[core][piece][
            at, rows_f:, :
        ].reshape(out_chunk, width)
    ahead_scr[...] = dot_nn(attn_ref[...], order_ref[...]).astype(BF)
    projected = dot_nn(ahead_scr[...], held_scr[...])
    unit_a, inverse_a = unit_of(projected)
    middle = resid_ref[...] + unit_a * (1.0 + sattn_ref[...])
    unit_p, inverse_p = unit_of(middle)
    pre = (unit_p * (1.0 + spre_ref[...])).astype(BF)
    ffn = jnp.zeros(middle.shape, jnp.float32)
    for number, (core, dp) in enumerate(parts):
        span = slice(number * chunk, (number + 1) * chunk)
        w_gate, w_up, w_down = weights(core, dp)
        gate = dot_nt(pre, w_gate)
        up = dot_nt(pre, w_up)
        gate_scr[:, span] = gate
        up_scr[:, span] = up
        bent = jnp.tanh(GELU_A * (gate + 0.044715 * (gate * gate * gate)))
        inner = (0.5 * gate * (1.0 + bent) * up).astype(BF)
        inner_scr[:, span] = inner
        ffn = ffn + dot_nn(inner, w_down)
    unit_f, inverse_f = unit_of(ffn)
    block_out_ref[...] = middle + unit_f * (1.0 + spost_ref[...])
    grad_out = gout_ref[...]
    gspost_ref[...] = jnp.sum(grad_out * unit_f, axis=0, keepdims=True)
    grad_ffn = rms_back(unit_f, inverse_f, grad_out * (1.0 + spost_ref[...])).astype(BF)
    grad_pre = jnp.zeros(middle.shape, jnp.float32)
    for number, (core, dp) in enumerate(parts):
        span = slice(number * chunk, (number + 1) * chunk)
        w_gate, w_up, w_down = weights(core, dp)
        grad_inner = dot_nt(grad_ffn, w_down)
        gate = gate_scr[:, span]
        square = gate * gate
        bent = jnp.tanh(GELU_A * (gate + 0.044715 * (square * gate)))
        curve = 0.5 * gate * (1.0 + bent)
        slope = 0.5 * (1.0 + bent) + 0.5 * gate * (1.0 - bent * bent) * (
            GELU_A * (1.0 + 3.0 * 0.044715 * square)
        )
        grad_up = (grad_inner * curve).astype(BF)
        grad_gate = (grad_inner * up_scr[:, span] * slope).astype(BF)
        grad_pre = grad_pre + dot_nn(grad_gate, w_gate) + dot_nn(grad_up, w_up)
        piece_a, at_a = place_a(dp)
        piece_b, at_b = place_b(dp)
        shape = (chips, rows_f, width)
        ga_refs[core][piece_a][at_a, :rows_f, :] = dot_tn(grad_gate, pre).astype(BF).reshape(shape)
        gb_refs[core][piece_b][at_b, :rows_f, :] = dot_tn(grad_up, pre).astype(BF).reshape(shape)
        gb_refs[core][piece_b][at_b, rows_f:, :] = (
            dot_tn(inner_scr[:, span], grad_ffn).astype(BF).reshape(shape)
        )
    gspre_ref[...] = jnp.sum(grad_pre * unit_p, axis=0, keepdims=True)
    grad_middle = grad_out + rms_back(unit_p, inverse_p, grad_pre * (1.0 + spre_ref[...]))
    gresid_ref[...] = grad_middle
    gsattn_ref[...] = jnp.sum(grad_middle * unit_a, axis=0, keepdims=True)
    grad_proj = rms_back(unit_a, inverse_a, grad_middle * (1.0 + sattn_ref[...])).astype(BF)
    grad_held = dot_nt(grad_proj, held_scr[...]).astype(BF)
    gattn_ref[...] = dot_nt(grad_held, order_ref[...]).astype(BF)
    for number, (core, dp) in enumerate(parts):
        piece, at = place_a(dp)
        span = slice(number * out_chunk, (number + 1) * out_chunk)
        ga_refs[core][piece][at, rows_f:, :] = (
            dot_tn(ahead_scr[:, span], grad_proj).astype(BF).reshape(chips, rows_o, width)
        )


def shards_plain(
    hidden_in,
    positions,
    w_query,
    w_key,
    w_value,
    w_output,
    w_gate,
    w_up,
    w_down,
    norm_scales,
    grad_out,
):
    width = hidden_in.shape[2]
    groups = lax.axis_size("ctx")
    count_dp = lax.axis_size("dp")
    chips = groups // 2
    owners = count_dp * groups
    place = lax.axis_index("ctx")
    row = lax.axis_index("dp")
    resid = hidden_in[0]
    posit = positions[0]
    grad_nat = grad_out[0]
    tokens = resid.shape[0]
    block = tokens // 2
    head_width = w_key.shape[0] * owners
    heads = w_query.shape[0] * owners // head_width
    rows_q, rows_k = w_query.shape[0], w_key.shape[0]
    scale_part = norm_scales.shape[0]

    tie = lax.optimization_barrier
    scale_rows = jnp.zeros((8, width), BF).at[0, :scale_part].set(norm_scales)
    first = gather_over(
        jnp.concatenate([w_query, w_key, w_value, scale_rows], axis=0)[None], swap_z, chips
    )
    rows_f = w_gate.shape[0]
    group_a = jnp.concatenate([w_gate, w_output], axis=0)[None]
    group_b = jnp.concatenate([w_up, w_down], axis=0)[None]
    inverse_in = lax.rsqrt(jnp.mean(resid * resid, axis=-1, keepdims=True) + EPS)
    unit_in = resid * inverse_in
    place_rows = jnp.zeros((8, width), BF)
    place_rows = place_rows.at[0, :tokens].set((posit // 64).astype(BF))
    place_rows = place_rows.at[1, :tokens].set((posit % 64).astype(BF))
    seq_part = jnp.concatenate([unit_in.astype(BF), place_rows], axis=0)[None]
    first, group_a, group_b, seq_part = tie((first, group_a, group_b, seq_part))
    first = gather_over(first[None], swap_dp, count_dp)
    group_a = gather_over(group_a, swap_z, chips)
    group_b = gather_over(group_b, swap_z, chips)
    first, group_a, group_b, seq_part = tie((first, group_a, group_b, seq_part))
    first = first.reshape((owners // 2,) + first.shape[2:])
    group_a = double(group_a, swap_dp, 1)
    group_b = double(group_b, swap_dp, 2)
    seq_z = gather_over(seq_part, swap_z, chips)
    first = jnp.concatenate([first, swap_ctx(first, 1)], axis=0)
    first, group_a, group_b, seq_z = tie((first, group_a, group_b, seq_z))
    seq_all = jnp.concatenate([seq_z, swap_ctx(seq_z, 1)], axis=0)
    group_a = double(group_a, swap_dp, 2)
    group_b = double_inner(group_b, swap_dp, 1)
    far_core, far_dp, far_z = (
        jnp.arange(owners, dtype=jnp.int32) // (owners // 2),
        (jnp.arange(owners, dtype=jnp.int32) // chips) % count_dp,
        jnp.arange(owners, dtype=jnp.int32) % chips,
    )
    owner_of = (row ^ far_dp) * groups + (place ^ (2 * far_z + far_core))
    order_q = row_order(owner_of, rows_q)
    order_k = row_order(owner_of, rows_k)
    order_s = row_order(owner_of, 1)
    full_query = reorder(order_q, first[:, :rows_q].reshape(-1, width))
    full_key = reorder(order_k, first[:, rows_q : rows_q + rows_k].reshape(-1, width))
    full_value = reorder(order_k, first[:, rows_q + rows_k : rows_q + 2 * rows_k].reshape(-1, width))
    full_scales = reorder(order_s, first[:, rows_q + 2 * rows_k, :scale_part]).reshape(-1)
    scale_in, scale_attn, scale_pre, scale_post, scale_query, scale_key = split_scales(
        full_scales, width, head_width
    )

    seq_len = groups * tokens
    seq_core, seq_zed = (
        jnp.arange(groups, dtype=jnp.int32) // chips,
        jnp.arange(groups, dtype=jnp.int32) % chips,
    )
    key_index = natural_rows(place ^ (2 * seq_zed + seq_core), block, groups)
    row_index = natural_rows(place[None], block, groups)
    unit_all = seq_all[:, :tokens].reshape(seq_len, width).astype(jnp.float32)
    pos_all = (
        seq_all[:, tokens, :tokens].astype(jnp.int32) * 64
        + seq_all[:, tokens + 1, :tokens].astype(jnp.int32)
    ).reshape(seq_len)
    normed = (unit_in * (1.0 + scale_in)).astype(BF)
    normed_all = (unit_all * (1.0 + scale_in)).astype(BF)

    query_raw = times_wt(normed, full_query).reshape(tokens, heads, head_width)
    key_raw = times_wt(normed_all, full_key)
    value_bf = times_wt(normed_all, full_value).astype(BF)

    def query_piece(raw, scale):
        return rotate(rms_scale(raw, scale), posit) * head_width ** (-0.5)

    def key_piece(raw, scale):
        return rotate(rms_scale(raw, scale)[:, None, :], pos_all)[:, 0, :]

    query_rot, query_back = jax.vjp(query_piece, query_raw, scale_query)
    key_rot, key_back = jax.vjp(key_piece, key_raw, scale_key)
    query_bf = jnp.swapaxes(query_rot.astype(BF), 0, 1).reshape(heads * tokens, head_width)
    key_bf = key_rot.astype(BF)
    allowed = jnp.tile(key_index[None, :] <= row_index[:, None], (heads, 1))
    scores = jnp.where(allowed, times_wt(query_bf, key_bf), -1e30)
    top = jnp.max(scores, axis=1, keepdims=True)
    lse = top + jnp.log(jnp.sum(jnp.exp(scores - top), axis=1, keepdims=True))
    probs = jnp.exp(scores - lse)
    probs_bf = probs.astype(BF)
    mixed = jnp.dot(probs_bf, value_bf, preferred_element_type=jnp.float32).astype(BF)
    attn_bf = jnp.swapaxes(mixed.reshape(heads, tokens, head_width), 0, 1).reshape(tokens, -1)

    group_a, group_b, attn_bf, probs = lax.optimization_barrier((group_a, group_b, attn_bf, probs))
    halves_a = (group_a, swap_ctx(group_a, 1))
    halves_b = (group_b, swap_ctx(group_b, 1))
    gates = [half[:, :rows_f].reshape(-1, width) for half in halves_a]
    ups = [half[:, :rows_f].reshape(-1, width) for half in halves_b]
    downs = [half[:, rows_f:].reshape(-1, width) for half in halves_b]
    out_held = jnp.concatenate([half[:, rows_f:].reshape(-1, width) for half in halves_a], axis=0)
    full_output = reorder(order_q, out_held)
    projected = jnp.dot(attn_bf, full_output, preferred_element_type=jnp.float32)
    (middle, pre_ffn), mid_back = jax.vjp(mid_piece, resid, projected, scale_attn, scale_pre)
    pre_bf = pre_ffn.astype(BF)
    inners, glu_backs = [], []
    for half_no in range(2):
        inner, glu_back = jax.vjp(
            glu_piece, times_wt(pre_bf, gates[half_no]), times_wt(pre_bf, ups[half_no])
        )
        inners.append(inner.astype(BF))
        glu_backs.append(glu_back)
    ffn = sum(
        jnp.dot(inners[half_no], downs[half_no], preferred_element_type=jnp.float32)
        for half_no in range(2)
    )
    block_out, out_back = jax.vjp(out_piece, middle, ffn, scale_post)
    grad_mid, grad_ffn, grad_scale_post = out_back(grad_nat)
    grad_ffn_bf = grad_ffn.astype(BF)
    grad_pre = 0.0
    downs_grad, gates_grad, ups_grad = [], [], []
    for half_no in range(2):
        grad_gate, grad_upward = glu_backs[half_no](times_wt(grad_ffn_bf, downs[half_no]))
        gate_bf = grad_gate.astype(BF)
        upward_bf = grad_upward.astype(BF)
        grad_pre = grad_pre + (
            jnp.dot(gate_bf, gates[half_no], preferred_element_type=jnp.float32)
            + jnp.dot(upward_bf, ups[half_no], preferred_element_type=jnp.float32)
        )
        downs_grad.append(outer_sum(inners[half_no], grad_ffn_bf).astype(BF))
        gates_grad.append(outer_sum(gate_bf, pre_bf).astype(BF))
        ups_grad.append(outer_sum(upward_bf, pre_bf).astype(BF))
    grads_b = [
        jnp.concatenate(
            [
                ups_grad[half_no].reshape(-1, rows_f, width),
                downs_grad[half_no].reshape(-1, rows_f, width),
            ],
            axis=1,
        )
        for half_no in range(2)
    ]
    grads_b = add_bf16(grads_b[0], swap_ctx(grads_b[1], 1)).astype(BF)
    grad_resid_a, grad_proj, grad_scale_attn, grad_scale_pre = mid_back((grad_mid, grad_pre))
    grad_proj_bf = grad_proj.astype(BF)
    grad_attn_bf = times_wt(grad_proj_bf, full_output).astype(BF)
    out_grad = reorder_back(order_q, outer_sum(attn_bf, grad_proj_bf))
    out_grad = out_grad.reshape(2, -1, rows_q, width)
    grads_a = [
        jnp.concatenate([gates_grad[half_no].reshape(-1, rows_f, width), out_grad[half_no]], axis=1)
        for half_no in range(2)
    ]
    grads_a = add_bf16(grads_a[0], swap_ctx(grads_a[1], 1)).astype(BF)
    grads_a, grads_b, grad_attn_bf, pre_bf = lax.optimization_barrier(
        (grads_a, grads_b, grad_attn_bf, pre_bf)
    )
    grads_a = halve(grads_a, swap_dp, 2)
    grads_b = halve_inner(grads_b, swap_dp, 1)

    grad_rows = jnp.swapaxes(grad_attn_bf.reshape(tokens, heads, head_width), 0, 1).reshape(
        heads * tokens, head_width
    )
    delta = jnp.sum(
        grad_rows.astype(jnp.float32) * mixed.astype(jnp.float32), axis=1, keepdims=True
    )
    grad_scores = (probs * (times_wt(grad_rows, value_bf) - delta)).astype(BF)
    grad_query = jnp.dot(grad_scores, key_bf, preferred_element_type=jnp.float32)
    grad_query = jnp.swapaxes(grad_query.reshape(heads, tokens, head_width), 0, 1)
    grad_key = outer_sum(grad_scores, query_bf)
    grad_value_bf = outer_sum(probs_bf, grad_rows).astype(BF)
    grad_qraw, grad_scale_query = query_back(grad_query)
    grad_kraw, grad_scale_key = key_back(grad_key)
    grad_qraw_bf = grad_qraw.reshape(tokens, heads * head_width).astype(BF)
    grad_kraw_bf = grad_kraw.astype(BF)

    grad_normed_q = jnp.dot(grad_qraw_bf, full_query, preferred_element_type=jnp.float32)
    grad_normed = jnp.dot(grad_kraw_bf, full_key, preferred_element_type=jnp.float32) + jnp.dot(
        grad_value_bf, full_value, preferred_element_type=jnp.float32
    )
    grad_scale_in = jnp.sum(grad_normed * unit_all, axis=0) + jnp.sum(
        grad_normed_q * unit_in, axis=0
    )
    far = grad_normed.astype(BF).reshape(2, chips, tokens, width)
    grad_w_query = reorder_back(order_q, outer_sum(grad_qraw_bf, normed))
    grad_w_key = reorder_back(order_k, outer_sum(grad_kraw_bf, normed_all))
    grad_w_value = reorder_back(order_k, outer_sum(grad_value_bf, normed_all))
    grad_scales = jnp.concatenate(
        [
            grad_scale_in,
            grad_scale_attn,
            grad_scale_pre,
            grad_scale_post,
            grad_scale_query,
            grad_scale_key,
        ]
    ).reshape(owners, scale_part)
    scales_back = reorder_back(order_s, grad_scales)
    packed = jnp.concatenate(
        [
            grad_w_query.reshape(owners, rows_q, width),
            grad_w_key.reshape(owners, rows_k, width),
            grad_w_value.reshape(owners, rows_k, width),
            jnp.zeros((owners, 8, width), BF).at[:, 0, :scale_part].set(scales_back),
        ],
        axis=1,
    ).reshape(2, -1, width)
    far_sum = add_bf16(far[0], swap_ctx(far[1], 1)).astype(BF)
    grads_a, grads_b, packed, far_sum = tie((grads_a, grads_b, packed, far_sum))
    grads_a = halve(grads_a, swap_dp, 1)
    grads_b = halve(grads_b, swap_dp, 2)
    own_normed = scatter_over(far_sum, swap_z, chips) + grad_normed_q
    packed = add_bf16(packed[0], swap_ctx(packed[1], 1)).astype(BF)
    grads_a, grads_b, packed, own_normed = tie((grads_a, grads_b, packed, own_normed))
    own_first = scatter_chip(packed)
    sum_a = scatter_over(grads_a, swap_z, chips)
    sum_b = scatter_over(grads_b, swap_z, chips)
    own_gate, own_output = sum_a[:rows_f], sum_a[rows_f:]
    own_up, own_down = sum_b[:rows_f], sum_b[rows_f:]
    own_query = own_first[:rows_q]
    own_key = own_first[rows_q : rows_q + rows_k]
    own_value = own_first[rows_q + rows_k : rows_q + 2 * rows_k]
    own_scales = own_first[rows_q + 2 * rows_k, :scale_part]
    grad_resid = grad_resid_a + rms_back(unit_in, inverse_in, own_normed * (1.0 + scale_in))
    return (
        block_out[None],
        grad_resid[None],
        own_query,
        own_key,
        own_value,
        own_output,
        own_gate,
        own_up,
        own_down,
        own_scales,
    )


def shards(*args):
    hidden_in, w_query, w_gate = args[0], args[2], args[6]
    fits = hidden_in.shape[1] * lax.axis_size("ctx") <= 2048 and lax.axis_size("dp") == 4
    if fits and w_query.shape[0] % 16 == 0 and w_gate.shape[0] % 16 == 0:
        return shards_kernels(*args)
    return shards_plain(*args)


def shards_kernels(
    hidden_in,
    positions,
    w_query,
    w_key,
    w_value,
    w_output,
    w_gate,
    w_up,
    w_down,
    norm_scales,
    grad_out,
):
    width = hidden_in.shape[2]
    groups = lax.axis_size("ctx")
    count_dp = lax.axis_size("dp")
    chips = groups // 2
    owners = count_dp * groups
    place = lax.axis_index("ctx")
    row = lax.axis_index("dp")
    resid = hidden_in[0]
    posit = positions[0]
    tokens = resid.shape[0]
    block = tokens // 2
    seq_len = groups * tokens
    head_width = w_key.shape[0] * owners
    heads = w_query.shape[0] * owners // head_width
    rows_q, rows_k, rows_f = w_query.shape[0], w_key.shape[0], w_gate.shape[0]
    scale_part = norm_scales.shape[0]
    tie = lax.optimization_barrier

    far_core, far_dp, far_z = (
        jnp.arange(owners, dtype=jnp.int32) // (owners // 2),
        (jnp.arange(owners, dtype=jnp.int32) // chips) % count_dp,
        jnp.arange(owners, dtype=jnp.int32) % chips,
    )
    owner_of = (row ^ far_dp) * groups + (place ^ (2 * far_z + far_core))
    order_q = row_order(owner_of, rows_q)
    order_k = row_order(owner_of, rows_k)
    order_s = row_order(owner_of, 1)
    seq_core, seq_zed = (
        jnp.arange(groups, dtype=jnp.int32) // chips,
        jnp.arange(groups, dtype=jnp.int32) % chips,
    )
    key_index = natural_rows(place ^ (2 * seq_zed + seq_core), block, groups).reshape(1, seq_len)
    row_index = natural_rows(place[None], block, groups).reshape(tokens, 1)

    last_rows = jnp.zeros((8, width), BF).at[0, :scale_part].set(norm_scales)
    last_rows = last_rows.at[1, :tokens].set((posit // 64).astype(BF))
    last_rows = last_rows.at[2, :tokens].set((posit % 64).astype(BF))
    first = gather_over(
        jnp.concatenate([w_query, w_key, w_value, last_rows], axis=0)[None], swap_z, chips
    )
    group_a = jnp.concatenate([w_gate, w_output], axis=0)[None]
    group_b = jnp.concatenate([w_up, w_down], axis=0)[None]
    inverse_in = lax.rsqrt(jnp.mean(resid * resid, axis=-1, keepdims=True) + EPS)
    unit_in = resid * inverse_in
    first, group_a, group_b, unit_bf = tie((first, group_a, group_b, unit_in.astype(BF)[None]))
    first = gather_over(first[None], swap_dp, count_dp)
    group_a = gather_over(group_a, swap_z, chips)
    group_b = gather_over(group_b, swap_z, chips)
    first, group_a, group_b, unit_bf = tie((first, group_a, group_b, unit_bf))
    first = first.reshape((owners // 2,) + first.shape[2:])
    a_one = double(group_a, swap_dp, 1)
    b_one = double(group_b, swap_dp, 2)
    near = gather_over(unit_bf, swap_z, chips).reshape(chips * tokens, width)
    first = jnp.concatenate([first, swap_ctx(first, 1)], axis=0)
    full_query = reorder(order_q, first[:, :rows_q].reshape(-1, width))
    full_key = reorder(order_k, first[:, rows_q : rows_q + rows_k].reshape(-1, width))
    full_value = reorder(order_k, first[:, rows_q + rows_k : rows_q + 2 * rows_k].reshape(-1, width))
    last = rows_q + 2 * rows_k
    full_scales = reorder(order_s, first[:, last, :scale_part]).reshape(-1)
    same_seq = first.reshape((2, count_dp, chips) + first.shape[1:])[:, 0, :, last:, :tokens]
    pos_all = same_seq[:, :, 1].astype(jnp.float32) * 64.0 + same_seq[:, :, 2].astype(jnp.float32)
    half = head_width // 2
    freq_table = 1000000.0 ** (-jnp.arange(half, dtype=jnp.float32) / half)
    angle = pos_all.reshape(seq_len)[:, None] * freq_table[None, :]
    cos_all, sine_all = jnp.cos(angle), jnp.sin(angle)
    (a_one, b_one, near, full_query, full_key, full_value, full_scales, cos_all, sine_all) = tie(
        (a_one, b_one, near, full_query, full_key, full_value, full_scales, cos_all, sine_all)
    )
    far = swap_ctx(near, 1)
    a_two = swap_dp(a_one, 2)
    b_two = swap_dp(b_one, 1)
    a_one_far = swap_ctx(a_one, 1)
    b_one_far = swap_ctx(b_one, 1)
    scale_in, scale_attn, scale_pre, scale_post, scale_query, scale_key = [
        scale[None] for scale in split_scales(full_scales, width, head_width)
    ]
    cos_own, sine_own = cos_all[:tokens], sine_all[:tokens]
    f32 = jnp.float32
    normed, normed_all, query_raw, key_raw, query_bf, key_bf, value_bf, attn_bf, lse = call_kernel(
        attend_kernel,
        [
            ((tokens, width), BF),
            ((seq_len, width), BF),
            ((tokens, heads * head_width), f32),
            ((seq_len, head_width), f32),
            ((tokens, heads * head_width), BF),
            ((seq_len, head_width), BF),
            ((seq_len, head_width), BF),
            ((tokens, heads * head_width), BF),
            ((tokens, heads), f32),
        ],
        [],
        20_000_000_000,
        (
            unit_in, near, far, full_query, full_key, full_value, scale_in, scale_query, scale_key,
            cos_own, sine_own, cos_all, sine_all, key_index, row_index,
        ),
    )
    a_one_far, b_one_far, a_two, b_two, attn_bf = tie((a_one_far, b_one_far, a_two, b_two, attn_bf))
    a_two_far = swap_ctx(a_two, 1)
    b_two_far = swap_ctx(b_two, 1)

    pieces_a = (a_one, a_two, a_one_far, a_two_far)
    pieces_b = (b_one, b_two, b_one_far, b_two_far)
    held = owners * rows_q
    hidden = owners * rows_f
    outs = call_kernel(
        mid_kernel,
        [((tokens, width), f32), ((tokens, width), f32), ((tokens, heads * head_width), BF)]
        + [((1, width), f32)] * 3
        + [(piece.shape, BF) for piece in pieces_a + pieces_b],
        [
            ((held, width), BF),
            ((tokens, held), BF),
            ((tokens, hidden), f32),
            ((tokens, hidden), f32),
            ((tokens, hidden), BF),
        ],
        20_000_000_000,
        (attn_bf, order_q, resid, grad_out[0], scale_attn, scale_pre, scale_post)
        + pieces_a
        + pieces_b,
    )
    block_out, grad_resid_a, grad_attn_bf, grad_s_attn, grad_s_pre, grad_s_post = outs[:6]
    ga_one, ga_two, ga_one_far, ga_two_far, gb_one, gb_two, gb_one_far, gb_two_far = outs[6:]

    ga_two = add_bf16(ga_two, swap_ctx(ga_two_far, 1)).astype(BF)
    gb_two = add_bf16(gb_two, swap_ctx(gb_two_far, 1)).astype(BF)
    ga_two, gb_two, grad_attn_bf = tie((ga_two, gb_two, grad_attn_bf))
    ga_come = swap_dp(ga_two, 2)
    gb_come = swap_dp(gb_two, 1)
    ga_one = add_bf16(ga_one, swap_ctx(ga_one_far, 1))
    gb_one = add_bf16(gb_one, swap_ctx(gb_one_far, 1))

    (gwq, gwk, gwv, g_near, g_far, grad_normed_q, grad_s_in, grad_s_query, grad_s_key) = call_kernel(
        attend_back_kernel,
        [
            ((heads * head_width, width), BF),
            ((head_width, width), BF),
            ((head_width, width), BF),
            (near.shape, BF),
            (far.shape, BF),
            ((tokens, width), f32),
            ((1, width), f32),
            ((1, head_width), f32),
            ((1, head_width), f32),
        ],
        [
            ((heads * tokens, seq_len), BF),
            ((heads * tokens, seq_len), BF),
            ((heads * tokens, head_width), BF),
            ((heads * tokens, head_width), BF),
            ((tokens, heads * head_width), BF),
        ],
        20_000_000_000,
        (
            grad_attn_bf, attn_bf, query_bf, key_bf, value_bf, lse, query_raw, key_raw,
            full_query, full_key, full_value, scale_query, scale_key, cos_own, sine_own, cos_all,
            sine_all, key_index, row_index, normed, normed_all, unit_in, near, far,
        ),
    )
    far_sum = add_bf16(g_near, swap_ctx(g_far, 1)).astype(BF).reshape(chips, tokens, width)
    grad_scales = jnp.concatenate(
        [grad_s_in, grad_s_attn, grad_s_pre, grad_s_post, grad_s_query, grad_s_key], axis=1
    ).reshape(owners, scale_part)
    scales_back = reorder_back(order_s, grad_scales)
    packed = jnp.concatenate(
        [
            reorder_back(order_q, gwq).reshape(owners, rows_q, width),
            reorder_back(order_k, gwk).reshape(owners, rows_k, width),
            reorder_back(order_k, gwv).reshape(owners, rows_k, width),
            jnp.zeros((owners, 8, width), BF).at[:, 0, :scale_part].set(scales_back),
        ],
        axis=1,
    ).reshape(2, -1, width)
    packed = add_bf16(packed[0], swap_ctx(packed[1], 1)).astype(BF)
    grads_a = add_bf16(ga_one, ga_come).astype(BF)
    grads_b = add_bf16(gb_one, gb_come).astype(BF)
    grads_a, grads_b, packed, far_sum = tie((grads_a, grads_b, packed, far_sum))
    grads_a = halve(grads_a, swap_dp, 1)
    grads_b = halve(grads_b, swap_dp, 2)
    own_normed = scatter_over(far_sum, swap_z, chips) + grad_normed_q
    grads_a, grads_b, packed, own_normed = tie((grads_a, grads_b, packed, own_normed))
    own_first = scatter_chip(packed)
    sum_a = scatter_over(grads_a, swap_z, chips)
    sum_b = scatter_over(grads_b, swap_z, chips)
    grad_resid = grad_resid_a + rms_back(unit_in, inverse_in, own_normed * (1.0 + scale_in))
    return (
        block_out[None],
        grad_resid[None],
        own_first[:rows_q],
        own_first[rows_q : rows_q + rows_k],
        own_first[rows_q + rows_k : last],
        sum_a[rows_f:],
        sum_a[:rows_f],
        sum_b[:rows_f],
        sum_b[rows_f:],
        own_first[last, :scale_part],
    )


def solution(mesh):
    in_specs = (
        P("dp", "ctx", None),
        P("dp", "ctx"),
        P(("dp", "ctx"), None),
        P(("dp", "ctx"), None),
        P(("dp", "ctx"), None),
        P(("dp", "ctx"), None),
        P(("dp", "ctx"), None),
        P(("dp", "ctx"), None),
        P(("dp", "ctx"), None),
        P(("dp", "ctx")),
        P("dp", "ctx", None),
    )
    out_specs = (
        P("dp", "ctx", None),
        P("dp", "ctx", None),
        P(("dp", "ctx"), None),
        P(("dp", "ctx"), None),
        P(("dp", "ctx"), None),
        P(("dp", "ctx"), None),
        P(("dp", "ctx"), None),
        P(("dp", "ctx"), None),
        P(("dp", "ctx"), None),
        P(("dp", "ctx")),
    )
    return jax.shard_map(shards, mesh=mesh, in_specs=in_specs, out_specs=out_specs, check_vma=False)
```

```python
import jax
import jax.numpy as jnp
from jax import lax
from jax.experimental import pallas as pl
from jax.experimental.pallas import tpu as pltpu
from jax.sharding import PartitionSpec as P

EPS = 1e-06


def rms_scale(vector, scale):
    return (
        vector * lax.rsqrt(jnp.mean(vector * vector, axis=-1, keepdims=True) + EPS) * (1.0 + scale)
    )


def rotate(vector, position):
    half = vector.shape[-1] // 2
    freq_table = 1000000.0 ** (-jnp.arange(half, dtype=jnp.float32) / half)
    angle = position.astype(jnp.float32)[:, None] * freq_table[None, :]
    cosine = jnp.cos(angle)[:, None, :]
    sine = jnp.sin(angle)[:, None, :]
    first = vector[..., :half]
    second = vector[..., half:]
    return jnp.concatenate(
        [first * cosine - second * sine, second * cosine + first * sine], axis=-1
    )


def mid_piece(resid, projected, scale_attn, scale_pre):
    middle = resid + rms_scale(projected, scale_attn)
    return (middle, rms_scale(middle, scale_pre))


def glu_piece(gate, upward):
    return jax.nn.gelu(gate, approximate=True) * upward


def out_piece(middle, ffn, scale_post):
    return middle + rms_scale(ffn, scale_post)


def times_wt(left, weight):
    return lax.dot_general(
        left, weight, (((1,), (1,)), ((), ())), preferred_element_type=jnp.float32
    )


def outer_sum(left, right):
    return lax.dot_general(
        left, right, (((0,), (0,)), ((), ())), preferred_element_type=jnp.float32
    )


def split_scales(norm_scales, width, head_width):
    scales = norm_scales.astype(jnp.float32)
    pieces = [scales[index * width : (index + 1) * width] for index in range(4)]
    offset = 4 * width
    return pieces + [
        scales[offset : offset + head_width],
        scales[offset + head_width : offset + 2 * head_width],
    ]


BF = jnp.bfloat16


def swap_dp(block, bits):
    count = lax.axis_size("dp")
    return lax.ppermute(block, "dp", [(place, place ^ bits) for place in range(count)])


def swap_ctx(block, bits):
    count = lax.axis_size("ctx")
    return lax.ppermute(block, "ctx", [(place, place ^ bits) for place in range(count)])


def swap_z(block, bits):
    return swap_ctx(block, 2 * bits)


def gather_over(block, swap, count):
    if count <= 4:
        return jnp.concatenate([block] + [swap(block, bits) for bits in range(1, count)], axis=0)
    bits = 1
    while bits < count:
        block = jnp.concatenate([block, swap(block, bits)], axis=0)
        bits = 2 * bits
    return block


def add_bf16(first, *others):
    total = first.astype(jnp.float32)
    for other in others:
        total = total + other.astype(jnp.float32)
    return total


def scatter_over(blocks, swap, count):
    if count <= 4:
        return add_bf16(blocks[0], *[swap(blocks[bits], bits) for bits in range(1, count)])
    bits = count // 2
    while bits > 1:
        blocks = add_bf16(blocks[:bits], swap(blocks[bits:], bits)).astype(BF)
        bits = bits // 2
    return add_bf16(blocks[0], swap(blocks[1], 1))


def gather_chip(block):
    groups = lax.axis_size("ctx") // 2
    over_z = gather_over(block[None], swap_z, groups)
    over_dp = gather_over(over_z[None], swap_dp, lax.axis_size("dp"))
    return over_dp.reshape((-1,) + block.shape[1:])


def double(blocks, swap, bits):
    return jnp.concatenate([blocks, swap(blocks, bits)], axis=0)


def double_inner(blocks, swap, bits):
    pair = blocks.reshape((2, 1, -1) + blocks.shape[1:])
    return jnp.concatenate([pair, swap(pair, bits)], axis=1).reshape((-1,) + blocks.shape[1:])


def halve(blocks, swap, bits):
    half = blocks.shape[0] // 2
    return add_bf16(blocks[:half], swap(blocks[half:], bits)).astype(BF)


def halve_inner(blocks, swap, bits):
    quarters = blocks.reshape((2, 2, -1) + blocks.shape[1:])
    half = add_bf16(quarters[:, 0], swap(quarters[:, 1], bits)).astype(BF)
    return half.reshape((-1,) + blocks.shape[1:])


def scatter_chip(blocks):
    groups = lax.axis_size("ctx") // 2
    count = lax.axis_size("dp")
    shaped = blocks.reshape((count, groups, -1) + blocks.shape[1:])
    mid = scatter_over(shaped, swap_dp, count).astype(BF)
    return scatter_over(mid, swap_z, groups)


def scatter_all(first, second):
    return scatter_chip(add_bf16(first, swap_ctx(second, 1)).astype(BF))


def natural_rows(places, block, groups):
    within = jnp.arange(2 * block, dtype=jnp.int32)[None, :]
    early = places[:, None] * block + within
    late = (2 * groups - 1 - places[:, None]) * block + within - block
    return jnp.where(within < block, early, late).reshape(-1)


def row_order(owner_of, rows):
    count = owner_of.shape[0] * rows
    held = (owner_of[:, None] * rows + jnp.arange(rows, dtype=jnp.int32)[None, :]).reshape(1, count)
    return (jnp.arange(count, dtype=jnp.int32)[:, None] == held).astype(BF)


def reorder(order, blocks):
    return jnp.dot(order, blocks, preferred_element_type=jnp.float32).astype(BF)


def reorder_back(order, blocks):
    return outer_sum(order, blocks.astype(BF)).astype(BF)


def rms_back(unit, inverse, grad_scaled):
    return inverse * (grad_scaled - unit * jnp.mean(grad_scaled * unit, axis=-1, keepdims=True))


def dot_nt(left, right):
    return lax.dot_general(left, right, (((1,), (1,)), ((), ())), preferred_element_type=jnp.float32)


def dot_nn(left, right):
    return lax.dot_general(left, right, (((1,), (0,)), ((), ())), preferred_element_type=jnp.float32)


def dot_tn(left, right):
    return lax.dot_general(left, right, (((0,), (0,)), ((), ())), preferred_element_type=jnp.float32)


def unit_of(rows):
    inverse = lax.rsqrt(jnp.mean(rows * rows, axis=-1, keepdims=True) + EPS)
    return rows * inverse, inverse


def turn(rows, cosine, sine):
    half = rows.shape[1] // 2
    first, second = rows[:, :half], rows[:, half:]
    return jnp.concatenate([first * cosine - second * sine, second * cosine + first * sine], axis=1)


def turn_back(rows, cosine, sine):
    half = rows.shape[1] // 2
    first, second = rows[:, :half], rows[:, half:]
    return jnp.concatenate([first * cosine + second * sine, second * cosine - first * sine], axis=1)


def call_kernel(body, out_shapes, scratch, flops, inputs):
    whole = pl.BlockSpec(memory_space=pltpu.VMEM)
    return pl.pallas_call(
        body,
        out_shape=[jax.ShapeDtypeStruct(shape, dtype) for shape, dtype in out_shapes],
        in_specs=[whole] * len(inputs),
        out_specs=[whole] * len(out_shapes),
        scratch_shapes=[pltpu.VMEM(shape, dtype) for shape, dtype in scratch],
        compiler_params=pltpu.CompilerParams(vmem_limit_bytes=52 * 1024 * 1024),
        cost_estimate=pl.CostEstimate(flops=flops, bytes_accessed=20_000_000, transcendentals=0),
    )(*inputs)


def attend_kernel(
    unit_ref, near_ref, far_ref, own_ref, other_ref, order_q_ref, order_kv_ref, sin_scale_ref, sq_ref,
    sk_ref, cos_all_ref, sine_all_ref, key_index_ref, row_index_ref,
    wq_ref, wkv_ref, normed_ref, normed_all_ref, qraw_ref, kraw_ref, q_ref, k_ref, v_ref, attn_ref, lse_ref,
    held_q, held_kv,
):
    places, _, width = own_ref.shape
    rows_q = held_q.shape[0] // (2 * places)
    rows_kv = held_kv.shape[0] // (2 * places)
    for core, ref in enumerate((own_ref, other_ref)):
        held_q[core * places * rows_q : (core + 1) * places * rows_q, :] = ref[:, :rows_q, :].reshape(
            places * rows_q, width
        )
        held_kv[core * places * rows_kv : (core + 1) * places * rows_kv, :] = ref[
            :, rows_q : rows_q + rows_kv, :
        ].reshape(places * rows_kv, width)
    wq_ref[...] = dot_nn(order_q_ref[...], held_q[...]).astype(BF)
    wkv_ref[...] = dot_nn(order_kv_ref[...], held_kv[...]).astype(BF)
    tokens = unit_ref.shape[0]
    scale_in = 1.0 + sin_scale_ref[...]
    normed_ref[...] = (unit_ref[...] * scale_in).astype(BF)
    half = near_ref.shape[0]
    normed_all_ref[:half] = (near_ref[...].astype(jnp.float32) * scale_in).astype(BF)
    normed_all_ref[half:] = (far_ref[...].astype(jnp.float32) * scale_in).astype(BF)
    head_width = sq_ref.shape[1]
    heads = wq_ref.shape[0] // head_width
    key_raw = dot_nt(normed_all_ref[...], wkv_ref[:head_width, :])
    kraw_ref[...] = key_raw
    v_ref[...] = dot_nt(normed_all_ref[...], wkv_ref[head_width:, :]).astype(BF)
    key_unit, _ = unit_of(key_raw)
    k_ref[...] = turn(key_unit * (1.0 + sk_ref[...]), cos_all_ref[...], sine_all_ref[...]).astype(BF)
    allowed = key_index_ref[...] <= row_index_ref[...]
    cosine, sine = cos_all_ref[:tokens, :], sine_all_ref[:tokens, :]
    for head in range(heads):
        span = slice(head * head_width, (head + 1) * head_width)
        raw = dot_nt(normed_ref[...], wq_ref[span, :])
        qraw_ref[:, span] = raw
        unit, _ = unit_of(raw)
        turned = turn(unit * (1.0 + sq_ref[...]), cosine, sine)
        query = (turned * head_width ** (-0.5)).astype(BF)
        q_ref[:, span] = query
        scores = jnp.where(allowed, dot_nt(query, k_ref[...]), -1e30)
        top = jnp.max(scores, axis=1, keepdims=True)
        lse = top + jnp.log(jnp.sum(jnp.exp(scores - top), axis=1, keepdims=True))
        lse_ref[:, head : head + 1] = lse
        probs = jnp.exp(scores - lse).astype(BF)
        attn_ref[:, span] = dot_nn(probs, v_ref[...]).astype(BF)


def project_kernel(
    attn_ref, order_ref, own_ref, other_ref, resid_ref, sattn_ref, spre_ref,
    held_ref, ahead_ref, projected_ref, middle_ref, pre_ref,
):
    places, rows, width = own_ref.shape
    held_ref[: places * rows, :] = own_ref[...].reshape(places * rows, width)
    held_ref[places * rows :, :] = other_ref[...].reshape(places * rows, width)
    ahead_ref[...] = dot_nn(attn_ref[...], order_ref[...]).astype(BF)
    projected = dot_nn(ahead_ref[...], held_ref[...])
    projected_ref[...] = projected
    unit, _ = unit_of(projected)
    middle = resid_ref[...] + unit * (1.0 + sattn_ref[...])
    middle_ref[...] = middle
    unit, _ = unit_of(middle)
    pre_ref[...] = (unit * (1.0 + spre_ref[...])).astype(BF)


GELU_A = (2.0 / 3.141592653589793) ** 0.5


def feed_kernel(*refs):
    pres, weights = refs[:4], refs[4:12]
    part_refs = refs[12:16]
    gate_ref, up_ref, inner_ref, pre_ref, wg_ref, wu_ref, wd_ref = refs[16:]
    tokens = pres[0].shape[0]
    rows = weights[0].shape[0] // 3
    for number, ref in enumerate(pres):
        pre_ref[number * tokens : (number + 1) * tokens, :] = ref[...]
    for number, ref in enumerate(weights):
        span = slice(number * rows, (number + 1) * rows)
        wg_ref[span, :] = ref[:rows, :]
        wu_ref[span, :] = ref[rows : 2 * rows, :]
        wd_ref[span, :] = ref[2 * rows :, :]
    for number in range(4):
        at = slice(number * tokens, (number + 1) * tokens)
        gate = dot_nt(pre_ref[at, :], wg_ref[...])
        up = dot_nt(pre_ref[at, :], wu_ref[...])
        gate_ref[at, :] = gate
        up_ref[at, :] = up
        bent = jnp.tanh(GELU_A * (gate + 0.044715 * (gate * gate * gate)))
        inner = (0.5 * gate * (1.0 + bent) * up).astype(BF)
        inner_ref[at, :] = inner
        part_refs[number][...] = dot_nn(inner, wd_ref[...]).astype(part_refs[number].dtype)


def turning_kernel(
    own_ref, come1_ref, come2_ref, come3_ref, middle_ref, gout_ref, spost_ref,
    block_out_ref, gffn_ref, gspost_ref,
):
    ffn = own_ref[...]
    for ref in (come1_ref, come2_ref, come3_ref):
        ffn = ffn + ref[...].astype(jnp.float32)
    unit, inverse = unit_of(ffn)
    grad_out = gout_ref[...]
    block_out_ref[...] = middle_ref[...] + unit * (1.0 + spost_ref[...])
    gspost_ref[...] = jnp.sum(grad_out * unit, axis=0, keepdims=True)
    gffn_ref[...] = rms_back(unit, inverse, grad_out * (1.0 + spost_ref[...])).astype(BF)


def feed_back_kernel(*refs):
    grads = refs[:4]
    gate_ref, up_ref, inner_ref, pre_ref, wg_ref, wu_ref, wd_ref = refs[4:11]
    part_refs = refs[11:15]
    own_ref, other_ref = refs[15:17]
    gffn_scr, ggate_scr, gup_scr = refs[17:]
    tokens = grads[0].shape[0]
    for number, ref in enumerate(grads):
        at = slice(number * tokens, (number + 1) * tokens)
        gffn_scr[at, :] = ref[...]
        grad_inner = dot_nt(ref[...], wd_ref[...])
        gate = gate_ref[at, :]
        square = gate * gate
        bent = jnp.tanh(GELU_A * (gate + 0.044715 * (square * gate)))
        curve = 0.5 * gate * (1.0 + bent)
        slope = 0.5 * (1.0 + bent) + 0.5 * gate * (1.0 - bent * bent) * (
            GELU_A * (1.0 + 3.0 * 0.044715 * square)
        )
        grad_up = (grad_inner * curve).astype(BF)
        grad_gate = (grad_inner * up_ref[at, :] * slope).astype(BF)
        ggate_scr[at, :] = grad_gate
        gup_scr[at, :] = grad_up
        part_refs[number][...] = (dot_nn(grad_gate, wg_ref[...]) + dot_nn(grad_up, wu_ref[...])).astype(
            part_refs[number].dtype
        )
    places, rows, width = own_ref.shape
    rows = rows // 3
    shape = (places, rows, width)
    for core, ref in enumerate((own_ref, other_ref)):
        span = slice(core * places * rows, (core + 1) * places * rows)
        ref[:, :rows, :] = dot_tn(ggate_scr[:, span], pre_ref[...]).astype(BF).reshape(shape)
        ref[:, rows : 2 * rows, :] = dot_tn(gup_scr[:, span], pre_ref[...]).astype(BF).reshape(shape)
        ref[:, 2 * rows :, :] = dot_tn(inner_ref[:, span], gffn_scr[...]).astype(BF).reshape(shape)


def project_back_kernel(
    own_ref, come1_ref, come2_ref, come3_ref, gout_ref, projected_ref, middle_ref, held_ref, ahead_ref,
    order_ref, sattn_ref, spre_ref,
    gresid_ref, gattn_ref, gown_ref, gother_ref, gsattn_ref, gspre_ref,
):
    grad_pre = own_ref[...]
    for ref in (come1_ref, come2_ref, come3_ref):
        grad_pre = grad_pre + ref[...].astype(jnp.float32)
    unit_p, inverse_p = unit_of(middle_ref[...])
    unit_a, inverse_a = unit_of(projected_ref[...])
    gspre_ref[...] = jnp.sum(grad_pre * unit_p, axis=0, keepdims=True)
    grad_middle = gout_ref[...] + rms_back(unit_p, inverse_p, grad_pre * (1.0 + spre_ref[...]))
    gresid_ref[...] = grad_middle
    gsattn_ref[...] = jnp.sum(grad_middle * unit_a, axis=0, keepdims=True)
    grad_proj = rms_back(unit_a, inverse_a, grad_middle * (1.0 + sattn_ref[...])).astype(BF)
    grad_held = dot_nt(grad_proj, held_ref[...]).astype(BF)
    gattn_ref[...] = dot_nt(grad_held, order_ref[...]).astype(BF)
    half = held_ref.shape[0] // 2
    gown_ref[...] = dot_tn(ahead_ref[:, :half], grad_proj).astype(BF).reshape(gown_ref.shape)
    gother_ref[...] = dot_tn(ahead_ref[:, half:], grad_proj).astype(BF).reshape(gother_ref.shape)


def attend_back_kernel(
    grad_attn_ref, attn_ref, q_ref, k_ref, v_ref, lse_ref, qraw_ref, kraw_ref, wq_ref, wkv_ref,
    sq_ref, sk_ref, cos_all_ref, sine_all_ref, key_index_ref, row_index_ref,
    normed_ref, normed_all_ref, unit_ref, near_ref, far_ref, order_q_ref, order_kv_ref,
    own_ref, other_ref, gnear_ref, gfar_ref, gq_ref, gsin_ref, gsq_ref, gsk_ref,
    probs_scr, gscores_scr, grows_scr, qrows_scr, gqraw_scr, gkv_scr,
):
    head_width = sq_ref.shape[1]
    heads = wq_ref.shape[0] // head_width
    tokens = q_ref.shape[0]
    cosine, sine = cos_all_ref[:tokens, :], sine_all_ref[:tokens, :]
    allowed = key_index_ref[...] <= row_index_ref[...]
    grad_sq = jnp.zeros((1, head_width), jnp.float32)
    for head in range(heads):
        span = slice(head * head_width, (head + 1) * head_width)
        rows = slice(head * tokens, (head + 1) * tokens)
        query = q_ref[:, span]
        grad_rows = grad_attn_ref[:, span]
        delta = jnp.sum(
            grad_rows.astype(jnp.float32) * attn_ref[:, span].astype(jnp.float32),
            axis=1,
            keepdims=True,
        )
        scores = jnp.where(allowed, dot_nt(query, k_ref[...]), -1e30)
        probs = jnp.exp(scores - lse_ref[:, head : head + 1])
        grad_scores = (probs * (dot_nt(grad_rows, v_ref[...]) - delta)).astype(BF)
        probs_scr[rows, :] = probs.astype(BF)
        gscores_scr[rows, :] = grad_scores
        grows_scr[rows, :] = grad_rows
        qrows_scr[rows, :] = query
        grad_query = dot_nn(grad_scores, k_ref[...]) * head_width ** (-0.5)
        grad_query = turn_back(grad_query, cosine, sine)
        unit, inverse = unit_of(qraw_ref[:, span])
        grad_sq = grad_sq + jnp.sum(grad_query * unit, axis=0, keepdims=True)
        grad_raw = rms_back(unit, inverse, grad_query * (1.0 + sq_ref[...]))
        gqraw_scr[:, span] = grad_raw.astype(BF)
    gsq_ref[...] = grad_sq
    grad_key = dot_tn(gscores_scr[...], qrows_scr[...])
    grad_value = dot_tn(probs_scr[...], grows_scr[...]).astype(BF)
    grad_key = turn_back(grad_key, cos_all_ref[...], sine_all_ref[...])
    unit, inverse = unit_of(kraw_ref[...])
    gsk_ref[...] = jnp.sum(grad_key * unit, axis=0, keepdims=True)
    grad_kraw = rms_back(unit, inverse, grad_key * (1.0 + sk_ref[...])).astype(BF)
    half = near_ref.shape[0]
    grad_normed = dot_nn(grad_kraw, wkv_ref[:head_width, :]) + dot_nn(
        grad_value, wkv_ref[head_width:, :]
    )
    grad_q = dot_nn(gqraw_scr[...], wq_ref[...])
    gq_ref[...] = grad_q
    gsin_ref[...] = (
        jnp.sum(grad_normed[:half] * near_ref[...].astype(jnp.float32), axis=0, keepdims=True)
        + jnp.sum(grad_normed[half:] * far_ref[...].astype(jnp.float32), axis=0, keepdims=True)
        + jnp.sum(grad_q * unit_ref[...], axis=0, keepdims=True)
    )
    gnear_ref[...] = grad_normed[:half].astype(BF)
    gfar_ref[...] = grad_normed[half:].astype(BF)
    gkv_scr[:head_width, :] = dot_tn(grad_kraw, normed_all_ref[...]).astype(BF)
    gkv_scr[head_width:, :] = dot_tn(grad_value, normed_all_ref[...]).astype(BF)
    grad_wq = dot_tn(gqraw_scr[...], normed_ref[...]).astype(BF)
    held_q = dot_tn(order_q_ref[...], grad_wq).astype(BF)
    held_kv = dot_tn(order_kv_ref[...], gkv_scr[...]).astype(BF)
    places, _, width = own_ref.shape
    rows_q = held_q.shape[0] // (2 * places)
    rows_kv = held_kv.shape[0] // (2 * places)
    for core, ref in enumerate((own_ref, other_ref)):
        ref[:, :rows_q, :] = held_q[core * places * rows_q : (core + 1) * places * rows_q].reshape(
            places, rows_q, width
        )
        ref[:, rows_q : rows_q + rows_kv, :] = held_kv[
            core * places * rows_kv : (core + 1) * places * rows_kv
        ].reshape(places, rows_kv, width)
        ref[:, rows_q + rows_kv :, :] = jnp.zeros((places, 16, width), BF)


def shards_plain(
    hidden_in,
    positions,
    w_query,
    w_key,
    w_value,
    w_output,
    w_gate,
    w_up,
    w_down,
    norm_scales,
    grad_out,
):
    width = hidden_in.shape[2]
    groups = lax.axis_size("ctx")
    count_dp = lax.axis_size("dp")
    chips = groups // 2
    owners = count_dp * groups
    place = lax.axis_index("ctx")
    row = lax.axis_index("dp")
    resid = hidden_in[0]
    posit = positions[0]
    grad_nat = grad_out[0]
    tokens = resid.shape[0]
    block = tokens // 2
    head_width = w_key.shape[0] * owners
    heads = w_query.shape[0] * owners // head_width
    rows_q, rows_k = w_query.shape[0], w_key.shape[0]
    scale_part = norm_scales.shape[0]

    tie = lax.optimization_barrier
    scale_rows = jnp.zeros((8, width), BF).at[0, :scale_part].set(norm_scales)
    first = gather_over(
        jnp.concatenate([w_query, w_key, w_value, scale_rows], axis=0)[None], swap_z, chips
    )
    rows_f = w_gate.shape[0]
    group_a = jnp.concatenate([w_gate, w_output], axis=0)[None]
    group_b = jnp.concatenate([w_up, w_down], axis=0)[None]
    inverse_in = lax.rsqrt(jnp.mean(resid * resid, axis=-1, keepdims=True) + EPS)
    unit_in = resid * inverse_in
    place_rows = jnp.zeros((8, width), BF)
    place_rows = place_rows.at[0, :tokens].set((posit // 64).astype(BF))
    place_rows = place_rows.at[1, :tokens].set((posit % 64).astype(BF))
    seq_part = jnp.concatenate([unit_in.astype(BF), place_rows], axis=0)[None]
    first, group_a, group_b, seq_part = tie((first, group_a, group_b, seq_part))
    first = gather_over(first[None], swap_dp, count_dp)
    group_a = gather_over(group_a, swap_z, chips)
    group_b = gather_over(group_b, swap_z, chips)
    first, group_a, group_b, seq_part = tie((first, group_a, group_b, seq_part))
    first = first.reshape((owners // 2,) + first.shape[2:])
    group_a = double(group_a, swap_dp, 1)
    group_b = double(group_b, swap_dp, 2)
    seq_z = gather_over(seq_part, swap_z, chips)
    first = jnp.concatenate([first, swap_ctx(first, 1)], axis=0)
    first, group_a, group_b, seq_z = tie((first, group_a, group_b, seq_z))
    seq_all = jnp.concatenate([seq_z, swap_ctx(seq_z, 1)], axis=0)
    group_a = double(group_a, swap_dp, 2)
    group_b = double_inner(group_b, swap_dp, 1)
    far_core, far_dp, far_z = (
        jnp.arange(owners, dtype=jnp.int32) // (owners // 2),
        (jnp.arange(owners, dtype=jnp.int32) // chips) % count_dp,
        jnp.arange(owners, dtype=jnp.int32) % chips,
    )
    owner_of = (row ^ far_dp) * groups + (place ^ (2 * far_z + far_core))
    order_q = row_order(owner_of, rows_q)
    order_k = row_order(owner_of, rows_k)
    order_s = row_order(owner_of, 1)
    full_query = reorder(order_q, first[:, :rows_q].reshape(-1, width))
    full_key = reorder(order_k, first[:, rows_q : rows_q + rows_k].reshape(-1, width))
    full_value = reorder(order_k, first[:, rows_q + rows_k : rows_q + 2 * rows_k].reshape(-1, width))
    full_scales = reorder(order_s, first[:, rows_q + 2 * rows_k, :scale_part]).reshape(-1)
    scale_in, scale_attn, scale_pre, scale_post, scale_query, scale_key = split_scales(
        full_scales, width, head_width
    )

    seq_len = groups * tokens
    seq_core, seq_zed = (
        jnp.arange(groups, dtype=jnp.int32) // chips,
        jnp.arange(groups, dtype=jnp.int32) % chips,
    )
    key_index = natural_rows(place ^ (2 * seq_zed + seq_core), block, groups)
    row_index = natural_rows(place[None], block, groups)
    unit_all = seq_all[:, :tokens].reshape(seq_len, width).astype(jnp.float32)
    pos_all = (
        seq_all[:, tokens, :tokens].astype(jnp.int32) * 64
        + seq_all[:, tokens + 1, :tokens].astype(jnp.int32)
    ).reshape(seq_len)
    normed = (unit_in * (1.0 + scale_in)).astype(BF)
    normed_all = (unit_all * (1.0 + scale_in)).astype(BF)

    query_raw = times_wt(normed, full_query).reshape(tokens, heads, head_width)
    key_raw = times_wt(normed_all, full_key)
    value_bf = times_wt(normed_all, full_value).astype(BF)

    def query_piece(raw, scale):
        return rotate(rms_scale(raw, scale), posit) * head_width ** (-0.5)

    def key_piece(raw, scale):
        return rotate(rms_scale(raw, scale)[:, None, :], pos_all)[:, 0, :]

    query_rot, query_back = jax.vjp(query_piece, query_raw, scale_query)
    key_rot, key_back = jax.vjp(key_piece, key_raw, scale_key)
    query_bf = jnp.swapaxes(query_rot.astype(BF), 0, 1).reshape(heads * tokens, head_width)
    key_bf = key_rot.astype(BF)
    allowed = jnp.tile(key_index[None, :] <= row_index[:, None], (heads, 1))
    scores = jnp.where(allowed, times_wt(query_bf, key_bf), -1e30)
    top = jnp.max(scores, axis=1, keepdims=True)
    lse = top + jnp.log(jnp.sum(jnp.exp(scores - top), axis=1, keepdims=True))
    probs = jnp.exp(scores - lse)
    probs_bf = probs.astype(BF)
    mixed = jnp.dot(probs_bf, value_bf, preferred_element_type=jnp.float32).astype(BF)
    attn_bf = jnp.swapaxes(mixed.reshape(heads, tokens, head_width), 0, 1).reshape(tokens, -1)

    group_a, group_b, attn_bf, probs = lax.optimization_barrier((group_a, group_b, attn_bf, probs))
    halves_a = (group_a, swap_ctx(group_a, 1))
    halves_b = (group_b, swap_ctx(group_b, 1))
    gates = [half[:, :rows_f].reshape(-1, width) for half in halves_a]
    ups = [half[:, :rows_f].reshape(-1, width) for half in halves_b]
    downs = [half[:, rows_f:].reshape(-1, width) for half in halves_b]
    out_held = jnp.concatenate([half[:, rows_f:].reshape(-1, width) for half in halves_a], axis=0)
    full_output = reorder(order_q, out_held)
    projected = jnp.dot(attn_bf, full_output, preferred_element_type=jnp.float32)
    (middle, pre_ffn), mid_back = jax.vjp(mid_piece, resid, projected, scale_attn, scale_pre)
    pre_bf = pre_ffn.astype(BF)
    inners, glu_backs = [], []
    for half_no in range(2):
        inner, glu_back = jax.vjp(
            glu_piece, times_wt(pre_bf, gates[half_no]), times_wt(pre_bf, ups[half_no])
        )
        inners.append(inner.astype(BF))
        glu_backs.append(glu_back)
    ffn = sum(
        jnp.dot(inners[half_no], downs[half_no], preferred_element_type=jnp.float32)
        for half_no in range(2)
    )
    block_out, out_back = jax.vjp(out_piece, middle, ffn, scale_post)
    grad_mid, grad_ffn, grad_scale_post = out_back(grad_nat)
    grad_ffn_bf = grad_ffn.astype(BF)
    grad_pre = 0.0
    downs_grad, gates_grad, ups_grad = [], [], []
    for half_no in range(2):
        grad_gate, grad_upward = glu_backs[half_no](times_wt(grad_ffn_bf, downs[half_no]))
        gate_bf = grad_gate.astype(BF)
        upward_bf = grad_upward.astype(BF)
        grad_pre = grad_pre + (
            jnp.dot(gate_bf, gates[half_no], preferred_element_type=jnp.float32)
            + jnp.dot(upward_bf, ups[half_no], preferred_element_type=jnp.float32)
        )
        downs_grad.append(outer_sum(inners[half_no], grad_ffn_bf).astype(BF))
        gates_grad.append(outer_sum(gate_bf, pre_bf).astype(BF))
        ups_grad.append(outer_sum(upward_bf, pre_bf).astype(BF))
    grads_b = [
        jnp.concatenate(
            [
                ups_grad[half_no].reshape(-1, rows_f, width),
                downs_grad[half_no].reshape(-1, rows_f, width),
            ],
            axis=1,
        )
        for half_no in range(2)
    ]
    grads_b = add_bf16(grads_b[0], swap_ctx(grads_b[1], 1)).astype(BF)
    grad_resid_a, grad_proj, grad_scale_attn, grad_scale_pre = mid_back((grad_mid, grad_pre))
    grad_proj_bf = grad_proj.astype(BF)
    grad_attn_bf = times_wt(grad_proj_bf, full_output).astype(BF)
    out_grad = reorder_back(order_q, outer_sum(attn_bf, grad_proj_bf))
    out_grad = out_grad.reshape(2, -1, rows_q, width)
    grads_a = [
        jnp.concatenate([gates_grad[half_no].reshape(-1, rows_f, width), out_grad[half_no]], axis=1)
        for half_no in range(2)
    ]
    grads_a = add_bf16(grads_a[0], swap_ctx(grads_a[1], 1)).astype(BF)
    grads_a, grads_b, grad_attn_bf, pre_bf = lax.optimization_barrier(
        (grads_a, grads_b, grad_attn_bf, pre_bf)
    )
    grads_a = halve(grads_a, swap_dp, 2)
    grads_b = halve_inner(grads_b, swap_dp, 1)

    grad_rows = jnp.swapaxes(grad_attn_bf.reshape(tokens, heads, head_width), 0, 1).reshape(
        heads * tokens, head_width
    )
    delta = jnp.sum(
        grad_rows.astype(jnp.float32) * mixed.astype(jnp.float32), axis=1, keepdims=True
    )
    grad_scores = (probs * (times_wt(grad_rows, value_bf) - delta)).astype(BF)
    grad_query = jnp.dot(grad_scores, key_bf, preferred_element_type=jnp.float32)
    grad_query = jnp.swapaxes(grad_query.reshape(heads, tokens, head_width), 0, 1)
    grad_key = outer_sum(grad_scores, query_bf)
    grad_value_bf = outer_sum(probs_bf, grad_rows).astype(BF)
    grad_qraw, grad_scale_query = query_back(grad_query)
    grad_kraw, grad_scale_key = key_back(grad_key)
    grad_qraw_bf = grad_qraw.reshape(tokens, heads * head_width).astype(BF)
    grad_kraw_bf = grad_kraw.astype(BF)

    grad_normed_q = jnp.dot(grad_qraw_bf, full_query, preferred_element_type=jnp.float32)
    grad_normed = jnp.dot(grad_kraw_bf, full_key, preferred_element_type=jnp.float32) + jnp.dot(
        grad_value_bf, full_value, preferred_element_type=jnp.float32
    )
    grad_scale_in = jnp.sum(grad_normed * unit_all, axis=0) + jnp.sum(
        grad_normed_q * unit_in, axis=0
    )
    far = grad_normed.astype(BF).reshape(2, chips, tokens, width)
    grad_w_query = reorder_back(order_q, outer_sum(grad_qraw_bf, normed))
    grad_w_key = reorder_back(order_k, outer_sum(grad_kraw_bf, normed_all))
    grad_w_value = reorder_back(order_k, outer_sum(grad_value_bf, normed_all))
    grad_scales = jnp.concatenate(
        [
            grad_scale_in,
            grad_scale_attn,
            grad_scale_pre,
            grad_scale_post,
            grad_scale_query,
            grad_scale_key,
        ]
    ).reshape(owners, scale_part)
    scales_back = reorder_back(order_s, grad_scales)
    packed = jnp.concatenate(
        [
            grad_w_query.reshape(owners, rows_q, width),
            grad_w_key.reshape(owners, rows_k, width),
            grad_w_value.reshape(owners, rows_k, width),
            jnp.zeros((owners, 8, width), BF).at[:, 0, :scale_part].set(scales_back),
        ],
        axis=1,
    ).reshape(2, -1, width)
    far_sum = add_bf16(far[0], swap_ctx(far[1], 1)).astype(BF)
    grads_a, grads_b, packed, far_sum = tie((grads_a, grads_b, packed, far_sum))
    grads_a = halve(grads_a, swap_dp, 1)
    grads_b = halve(grads_b, swap_dp, 2)
    own_normed = scatter_over(far_sum, swap_z, chips) + grad_normed_q
    packed = add_bf16(packed[0], swap_ctx(packed[1], 1)).astype(BF)
    grads_a, grads_b, packed, own_normed = tie((grads_a, grads_b, packed, own_normed))
    own_first = scatter_chip(packed)
    sum_a = scatter_over(grads_a, swap_z, chips)
    sum_b = scatter_over(grads_b, swap_z, chips)
    own_gate, own_output = sum_a[:rows_f], sum_a[rows_f:]
    own_up, own_down = sum_b[:rows_f], sum_b[rows_f:]
    own_query = own_first[:rows_q]
    own_key = own_first[rows_q : rows_q + rows_k]
    own_value = own_first[rows_q + rows_k : rows_q + 2 * rows_k]
    own_scales = own_first[rows_q + 2 * rows_k, :scale_part]
    grad_resid = grad_resid_a + rms_back(unit_in, inverse_in, own_normed * (1.0 + scale_in))
    return (
        block_out[None],
        grad_resid[None],
        own_query,
        own_key,
        own_value,
        own_output,
        own_gate,
        own_up,
        own_down,
        own_scales,
    )


def shards(*args):
    hidden_in, w_query, w_gate = args[0], args[2], args[6]
    fits = hidden_in.shape[1] * lax.axis_size("ctx") <= 2048 and lax.axis_size("ctx") == 8
    fits = fits and lax.axis_size("dp") == 4
    if fits and w_query.shape[0] % 16 == 0 and w_gate.shape[0] % 16 == 0 and args[3].shape[0] == 8:
        return shards_kernels(*args)
    return shards_plain(*args)


def swaps(block, swap):
    return [swap(block, bits) for bits in range(1, 4)]


def shards_kernels(
    hidden_in,
    positions,
    w_query,
    w_key,
    w_value,
    w_output,
    w_gate,
    w_up,
    w_down,
    norm_scales,
    grad_out,
):
    width = hidden_in.shape[2]
    groups = lax.axis_size("ctx")
    count_dp = lax.axis_size("dp")
    chips = groups // 2
    owners = count_dp * groups
    place = lax.axis_index("ctx")
    row = lax.axis_index("dp")
    resid = hidden_in[0]
    posit = positions[0]
    tokens = resid.shape[0]
    block = tokens // 2
    seq_len = groups * tokens
    head_width = w_key.shape[0] * owners
    heads = w_query.shape[0] * owners // head_width
    rows_q, rows_k, rows_f = w_query.shape[0], w_key.shape[0], w_gate.shape[0]
    last = rows_q + 2 * rows_k
    scale_part = norm_scales.shape[0]
    f32 = jnp.float32
    tie = lax.optimization_barrier

    far_core, far_dp, far_z = (
        jnp.arange(owners, dtype=jnp.int32) // (owners // 2),
        (jnp.arange(owners, dtype=jnp.int32) // chips) % count_dp,
        jnp.arange(owners, dtype=jnp.int32) % chips,
    )
    owner_of = (row ^ far_dp) * groups + (place ^ (2 * far_z + far_core))
    order_q = row_order(owner_of, rows_q)
    order_s = row_order(owner_of, 1)
    held_row = jnp.arange(2 * rows_k * owners, dtype=jnp.int32)
    held_at = (
        (held_row % (2 * rows_k)) // rows_k * head_width
        + jnp.repeat(owner_of, 2 * rows_k) * rows_k
        + held_row % rows_k
    )
    order_kv = (held_row[:, None] == held_at[None, :]).astype(BF)
    seq_core, seq_zed = (
        jnp.arange(groups, dtype=jnp.int32) // chips,
        jnp.arange(groups, dtype=jnp.int32) % chips,
    )
    key_index = natural_rows(place ^ (2 * seq_zed + seq_core), block, groups).reshape(1, seq_len)
    row_index = natural_rows(place[None], block, groups).reshape(tokens, 1)

    last_rows = jnp.zeros((16, width), BF).at[0, :scale_part].set(norm_scales)
    last_rows = last_rows.at[1, :tokens].set((posit // 64).astype(BF))
    last_rows = last_rows.at[2, :tokens].set((posit % 64).astype(BF))
    first = jnp.concatenate([w_query, w_key, w_value, last_rows], axis=0)
    feed = jnp.concatenate([w_gate, w_up, w_down], axis=0)
    inverse_in = lax.rsqrt(jnp.mean(resid * resid, axis=-1, keepdims=True) + EPS)
    unit_in = resid * inverse_in
    unit_bf = unit_in.astype(BF)
    first = gather_over(first[None], swap_z, chips)
    first, unit_bf, feed, w_output, order_q, order_kv = tie(
        (first, unit_bf, feed, w_output, order_q, order_kv)
    )
    last_far = swap_ctx(first[:, last:], 1)
    pos_all = jnp.stack([first[:, last:], last_far], axis=0)[:, :, :, :tokens].astype(f32)
    pos_all = (pos_all[:, :, 1] * 64.0 + pos_all[:, :, 2]).reshape(seq_len)
    half = head_width // 2
    freq_table = 1000000.0 ** (-jnp.arange(half, dtype=jnp.float32) / half)
    angle = pos_all[:, None] * freq_table[None, :]
    cos_all, sine_all = jnp.cos(angle), jnp.sin(angle)
    first = gather_over(first[None], swap_dp, count_dp).reshape((owners // 2,) + first.shape[1:])
    near = gather_over(unit_bf[None], swap_z, chips).reshape(chips * tokens, width)
    first, near, feed, w_output, cos_all, sine_all = tie(
        (first, near, feed, w_output, cos_all, sine_all)
    )
    other = swap_ctx(first, 1)
    far = swap_ctx(near, 1)
    out_own = gather_over(w_output[None], swap_z, chips)
    scale_rows = jnp.concatenate([first[:, last, :scale_part], other[:, last, :scale_part]], axis=0)
    full_scales = reorder(order_s, scale_rows).reshape(-1)
    other, far, out_own, feed, full_scales = tie((other, far, out_own, feed, full_scales))
    scale_in, scale_attn, scale_pre, scale_post, scale_query, scale_key = [
        scale[None] for scale in split_scales(full_scales, width, head_width)
    ]
    feed_z2 = swap_z(feed, 2)
    out_own = gather_over(out_own[None], swap_dp, count_dp).reshape((owners // 2, rows_q, width))
    (w_q, w_kv, normed, normed_all, query_raw, key_raw, query_bf, key_bf, value_bf, attn_bf, lse) = (
        call_kernel(
            attend_kernel,
            [
                ((heads * head_width, width), BF),
                ((2 * head_width, width), BF),
                ((tokens, width), BF),
                ((seq_len, width), BF),
                ((tokens, heads * head_width), f32),
                ((seq_len, head_width), f32),
                ((tokens, heads * head_width), BF),
                ((seq_len, head_width), BF),
                ((seq_len, head_width), BF),
                ((tokens, heads * head_width), BF),
                ((tokens, heads), f32),
            ],
            [((heads * head_width, width), BF), ((2 * head_width, width), BF)],
            12_000_000_000,
            (
                unit_in, near, far, first, other, order_q, order_kv, scale_in, scale_query, scale_key,
                cos_all, sine_all, key_index, row_index,
            ),
        )
    )
    attn_bf, feed_z2, out_own, feed = tie((attn_bf, feed_z2, out_own, feed))
    out_other = swap_ctx(out_own, 1)
    feed_z1 = swap_z(feed, 1)
    feed_z3 = swap_z(feed, 3)
    feed_c0 = swap_ctx(feed, 1)
    feed_c2 = swap_ctx(feed_z2, 1)
    held_out, ahead, projected, middle, pre = call_kernel(
        project_kernel,
        [
            ((owners * rows_q, width), BF),
            ((tokens, owners * rows_q), BF),
            ((tokens, width), f32),
            ((tokens, width), f32),
            ((tokens, width), BF),
        ],
        [],
        2_000_000_000,
        (attn_bf, order_q, out_own, out_other, resid, scale_attn, scale_pre),
    )
    pres = swaps(pre, swap_dp)
    pre, pres, feed_z1, feed_z3, feed_c0, feed_c2 = tie((pre, pres, feed_z1, feed_z3, feed_c0, feed_c2))
    feed_c1 = swap_ctx(feed_z1, 1)
    feed_c3 = swap_ctx(feed_z3, 1)
    part_shapes = [((tokens, width), f32)] + [((tokens, width), BF)] * 3
    all_tokens = count_dp * tokens
    hidden = groups * rows_f
    outs = call_kernel(
        feed_kernel,
        part_shapes
        + [
            ((all_tokens, hidden), f32),
            ((all_tokens, hidden), f32),
            ((all_tokens, hidden), BF),
            ((all_tokens, width), BF),
        ]
        + [((hidden, width), BF)] * 3,
        [],
        3_000_000_000,
        [pre] + pres + [feed, feed_z1, feed_z2, feed_z3, feed_c0, feed_c1, feed_c2, feed_c3],
    )
    parts, kept = outs[:4], outs[4:]
    comes = [swap_dp(parts[bits], bits) for bits in range(1, 4)]
    block_out, grad_ffn, grad_s_post = call_kernel(
        turning_kernel,
        [((tokens, width), f32), ((tokens, width), BF), ((1, width), f32)],
        [],
        100_000_000,
        [parts[0]] + comes + [middle, grad_out[0], scale_post],
    )
    outs = call_kernel(
        feed_back_kernel,
        part_shapes + [((chips, 3 * rows_f, width), BF)] * 2,
        [((all_tokens, width), BF), ((all_tokens, hidden), BF), ((all_tokens, hidden), BF)],
        6_000_000_000,
        [grad_ffn] + swaps(grad_ffn, swap_dp) + list(kept),
    )
    parts, (g_feed, g_feed_far) = outs[:4], outs[4:]
    comes = [swap_dp(parts[bits], bits) for bits in range(1, 4)]
    g_feed = add_bf16(g_feed, swap_ctx(g_feed_far, 1)).astype(BF)
    g_feed, comes = tie((g_feed, comes))
    feed_come1 = swap_z(g_feed[1], 1)
    grad_resid_a, grad_attn, g_out, g_out_far, grad_s_attn, grad_s_pre = call_kernel(
        project_back_kernel,
        [
            ((tokens, width), f32),
            ((tokens, heads * head_width), BF),
            (out_own.shape, BF),
            (out_own.shape, BF),
            ((1, width), f32),
            ((1, width), f32),
        ],
        [],
        3_000_000_000,
        [parts[0]]
        + comes
        + [grad_out[0], projected, middle, held_out, ahead, order_q, scale_attn, scale_pre],
    )
    grad_resid_a, grad_attn, g_out, g_out_far, grad_s_attn, grad_s_pre, feed_come1, g_feed = tie(
        (grad_resid_a, grad_attn, g_out, g_out_far, grad_s_attn, grad_s_pre, feed_come1, g_feed)
    )
    g_out = add_bf16(g_out, swap_ctx(g_out_far, 1)).astype(BF).reshape(count_dp, chips, rows_q, width)
    g_out, g_feed, grad_attn = tie((g_out, g_feed, grad_attn))
    feed_come2 = swap_z(g_feed[2], 2)
    out_comes = [swap_dp(g_out[bits], bits) for bits in range(1, 4)]
    (packed, packed_far, g_near, g_far, grad_normed_q, grad_s_in, grad_s_query, grad_s_key) = call_kernel(
        attend_back_kernel,
        [
            (first.shape, BF),
            (first.shape, BF),
            (near.shape, BF),
            (far.shape, BF),
            ((tokens, width), f32),
            ((1, width), f32),
            ((1, head_width), f32),
            ((1, head_width), f32),
        ],
        [
            ((heads * tokens, seq_len), BF),
            ((heads * tokens, seq_len), BF),
            ((heads * tokens, head_width), BF),
            ((heads * tokens, head_width), BF),
            ((tokens, heads * head_width), BF),
            ((2 * head_width, width), BF),
        ],
        12_000_000_000,
        (
            grad_attn, attn_bf, query_bf, key_bf, value_bf, lse, query_raw, key_raw, w_q, w_kv,
            scale_query, scale_key, cos_all, sine_all, key_index, row_index, normed, normed_all,
            unit_in, near, far, order_q, order_kv,
        ),
    )
    back = (packed, packed_far, g_near, g_far, grad_normed_q, grad_s_in, grad_s_query, grad_s_key)
    back, feed_come2, out_comes, g_out, g_feed = tie((back, feed_come2, out_comes, g_out, g_feed))
    packed, packed_far, g_near, g_far, grad_normed_q, grad_s_in, grad_s_query, grad_s_key = back
    grad_scales = jnp.concatenate(
        [grad_s_in, grad_s_attn, grad_s_pre, grad_s_post, grad_s_query, grad_s_key], axis=1
    ).reshape(owners, scale_part)
    scales_back = reorder_back(order_s, grad_scales)
    scale_sum = add_bf16(scales_back[: owners // 2], swap_ctx(scales_back[owners // 2 :], 1))
    scale_sum = jnp.pad(
        scale_sum[:, None], ((0, 0), (last, packed.shape[1] - last - 1), (0, width - scale_part))
    )
    packed = (add_bf16(packed, swap_ctx(packed_far, 1)) + scale_sum).astype(BF)
    feed_come3 = swap_z(g_feed[3, : 3 * rows_f // 2], 3)
    far_sum = add_bf16(g_near, swap_ctx(g_far, 1)).astype(BF).reshape(chips, tokens, width)
    out_sum = add_bf16(g_out[0], *out_comes).astype(BF)
    packed, far_sum, out_sum, g_feed, feed_come3 = tie((packed, far_sum, out_sum, g_feed, feed_come3))
    packed = scatter_over(packed.reshape((count_dp, chips) + packed.shape[1:]), swap_dp, count_dp)
    own_normed = scatter_over(far_sum, swap_z, chips) + grad_normed_q
    packed, own_normed, out_sum, g_feed = tie((packed.astype(BF), own_normed, out_sum, g_feed))
    feed_come3 = jnp.concatenate([feed_come3, swap_z(g_feed[3, 3 * rows_f // 2 :], 3)], axis=0)
    own_feed = add_bf16(g_feed[0], feed_come1, feed_come2, feed_come3)
    own_output = scatter_over(out_sum, swap_z, chips)
    own_first = scatter_over(packed, swap_z, chips)
    grad_resid = grad_resid_a + rms_back(unit_in, inverse_in, own_normed * (1.0 + scale_in))
    return (
        block_out[None],
        grad_resid[None],
        own_first[:rows_q],
        own_first[rows_q : rows_q + rows_k],
        own_first[rows_q + rows_k : last],
        own_output,
        own_feed[:rows_f],
        own_feed[rows_f : 2 * rows_f],
        own_feed[2 * rows_f :],
        own_first[last, :scale_part],
    )


def solution(mesh):
    in_specs = (
        P("dp", "ctx", None),
        P("dp", "ctx"),
        P(("dp", "ctx"), None),
        P(("dp", "ctx"), None),
        P(("dp", "ctx"), None),
        P(("dp", "ctx"), None),
        P(("dp", "ctx"), None),
        P(("dp", "ctx"), None),
        P(("dp", "ctx"), None),
        P(("dp", "ctx")),
        P("dp", "ctx", None),
    )
    out_specs = (
        P("dp", "ctx", None),
        P("dp", "ctx", None),
        P(("dp", "ctx"), None),
        P(("dp", "ctx"), None),
        P(("dp", "ctx"), None),
        P(("dp", "ctx"), None),
        P(("dp", "ctx"), None),
        P(("dp", "ctx"), None),
        P(("dp", "ctx"), None),
        P(("dp", "ctx")),
    )
    return jax.shard_map(shards, mesh=mesh, in_specs=in_specs, out_specs=out_specs, check_vma=False)
```

```python
import jax
import jax.numpy as jnp
from jax import lax
from jax.experimental import pallas as pl
from jax.experimental.pallas import tpu as pltpu
from jax.sharding import PartitionSpec as P

EPS = 1e-06


def rms_scale(vector, scale):
    return (
        vector * lax.rsqrt(jnp.mean(vector * vector, axis=-1, keepdims=True) + EPS) * (1.0 + scale)
    )


def rotate(vector, position):
    half = vector.shape[-1] // 2
    freq_table = 1000000.0 ** (-jnp.arange(half, dtype=jnp.float32) / half)
    angle = position.astype(jnp.float32)[:, None] * freq_table[None, :]
    cosine = jnp.cos(angle)[:, None, :]
    sine = jnp.sin(angle)[:, None, :]
    first = vector[..., :half]
    second = vector[..., half:]
    return jnp.concatenate(
        [first * cosine - second * sine, second * cosine + first * sine], axis=-1
    )


def mid_piece(resid, projected, scale_attn, scale_pre):
    middle = resid + rms_scale(projected, scale_attn)
    return (middle, rms_scale(middle, scale_pre))


def glu_piece(gate, upward):
    return jax.nn.gelu(gate, approximate=True) * upward


def out_piece(middle, ffn, scale_post):
    return middle + rms_scale(ffn, scale_post)


def times_wt(left, weight):
    return lax.dot_general(
        left, weight, (((1,), (1,)), ((), ())), preferred_element_type=jnp.float32
    )


def outer_sum(left, right):
    return lax.dot_general(
        left, right, (((0,), (0,)), ((), ())), preferred_element_type=jnp.float32
    )


def split_scales(norm_scales, width, head_width):
    scales = norm_scales.astype(jnp.float32)
    pieces = [scales[index * width : (index + 1) * width] for index in range(4)]
    offset = 4 * width
    return pieces + [
        scales[offset : offset + head_width],
        scales[offset + head_width : offset + 2 * head_width],
    ]


BF = jnp.bfloat16


def swap_dp(block, bits):
    count = lax.axis_size("dp")
    return lax.ppermute(block, "dp", [(place, place ^ bits) for place in range(count)])


def swap_ctx(block, bits):
    count = lax.axis_size("ctx")
    return lax.ppermute(block, "ctx", [(place, place ^ bits) for place in range(count)])


def swap_z(block, bits):
    return swap_ctx(block, 2 * bits)


def gather_over(block, swap, count):
    if count <= 4:
        return jnp.concatenate([block] + [swap(block, bits) for bits in range(1, count)], axis=0)
    bits = 1
    while bits < count:
        block = jnp.concatenate([block, swap(block, bits)], axis=0)
        bits = 2 * bits
    return block


def add_bf16(first, *others):
    total = first.astype(jnp.float32)
    for other in others:
        total = total + other.astype(jnp.float32)
    return total


def scatter_over(blocks, swap, count):
    if count <= 4:
        return add_bf16(blocks[0], *[swap(blocks[bits], bits) for bits in range(1, count)])
    bits = count // 2
    while bits > 1:
        blocks = add_bf16(blocks[:bits], swap(blocks[bits:], bits)).astype(BF)
        bits = bits // 2
    return add_bf16(blocks[0], swap(blocks[1], 1))


def gather_chip(block):
    groups = lax.axis_size("ctx") // 2
    over_z = gather_over(block[None], swap_z, groups)
    over_dp = gather_over(over_z[None], swap_dp, lax.axis_size("dp"))
    return over_dp.reshape((-1,) + block.shape[1:])


def double(blocks, swap, bits):
    return jnp.concatenate([blocks, swap(blocks, bits)], axis=0)


def double_inner(blocks, swap, bits):
    pair = blocks.reshape((2, 1, -1) + blocks.shape[1:])
    return jnp.concatenate([pair, swap(pair, bits)], axis=1).reshape((-1,) + blocks.shape[1:])


def halve(blocks, swap, bits):
    half = blocks.shape[0] // 2
    return add_bf16(blocks[:half], swap(blocks[half:], bits)).astype(BF)


def halve_inner(blocks, swap, bits):
    quarters = blocks.reshape((2, 2, -1) + blocks.shape[1:])
    half = add_bf16(quarters[:, 0], swap(quarters[:, 1], bits)).astype(BF)
    return half.reshape((-1,) + blocks.shape[1:])


def scatter_chip(blocks):
    groups = lax.axis_size("ctx") // 2
    count = lax.axis_size("dp")
    shaped = blocks.reshape((count, groups, -1) + blocks.shape[1:])
    mid = scatter_over(shaped, swap_dp, count).astype(BF)
    return scatter_over(mid, swap_z, groups)


def scatter_all(first, second):
    return scatter_chip(add_bf16(first, swap_ctx(second, 1)).astype(BF))


def natural_rows(places, block, groups):
    within = jnp.arange(2 * block, dtype=jnp.int32)[None, :]
    early = places[:, None] * block + within
    late = (2 * groups - 1 - places[:, None]) * block + within - block
    return jnp.where(within < block, early, late).reshape(-1)


def row_order(owner_of, rows):
    count = owner_of.shape[0] * rows
    held = (owner_of[:, None] * rows + jnp.arange(rows, dtype=jnp.int32)[None, :]).reshape(1, count)
    return (jnp.arange(count, dtype=jnp.int32)[:, None] == held).astype(BF)


def reorder(order, blocks):
    return jnp.dot(order, blocks, preferred_element_type=jnp.float32).astype(BF)


def reorder_back(order, blocks):
    return outer_sum(order, blocks.astype(BF)).astype(BF)


def rms_back(unit, inverse, grad_scaled):
    return inverse * (grad_scaled - unit * jnp.mean(grad_scaled * unit, axis=-1, keepdims=True))


def dot_nt(left, right):
    return lax.dot_general(left, right, (((1,), (1,)), ((), ())), preferred_element_type=jnp.float32)


def dot_nn(left, right):
    return lax.dot_general(left, right, (((1,), (0,)), ((), ())), preferred_element_type=jnp.float32)


def dot_tn(left, right):
    return lax.dot_general(left, right, (((0,), (0,)), ((), ())), preferred_element_type=jnp.float32)


def unit_of(rows):
    inverse = lax.rsqrt(jnp.mean(rows * rows, axis=-1, keepdims=True) + EPS)
    return rows * inverse, inverse


def turn(rows, cosine, sine):
    half = rows.shape[1] // 2
    first, second = rows[:, :half], rows[:, half:]
    return jnp.concatenate([first * cosine - second * sine, second * cosine + first * sine], axis=1)


def turn_back(rows, cosine, sine):
    half = rows.shape[1] // 2
    first, second = rows[:, :half], rows[:, half:]
    return jnp.concatenate([first * cosine + second * sine, second * cosine - first * sine], axis=1)


def call_kernel(body, out_shapes, scratch, flops, inputs, mebibytes=24):
    whole = pl.BlockSpec(memory_space=pltpu.VMEM)
    return pl.pallas_call(
        body,
        out_shape=[jax.ShapeDtypeStruct(shape, dtype) for shape, dtype in out_shapes],
        in_specs=[whole] * len(inputs),
        out_specs=[whole] * len(out_shapes),
        scratch_shapes=[pltpu.VMEM(shape, dtype) for shape, dtype in scratch],
        compiler_params=pltpu.CompilerParams(vmem_limit_bytes=mebibytes * 1024 * 1024),
        cost_estimate=pl.CostEstimate(flops=flops, bytes_accessed=20_000_000, transcendentals=0),
    )(*inputs)


def attend_kernel(
    unit_ref, near_ref, far_ref, own_ref, other_ref, order_q_ref, order_kv_ref, sin_scale_ref, sq_ref,
    sk_ref, cos_all_ref, sine_all_ref, key_index_ref, row_index_ref,
    wq_ref, wkv_ref, normed_ref, normed_all_ref, qraw_ref, kraw_ref, q_ref, k_ref, v_ref, attn_ref, lse_ref,
    held_q, held_kv,
):
    places, _, width = own_ref.shape
    rows_q = held_q.shape[0] // (2 * places)
    rows_kv = held_kv.shape[0] // (2 * places)
    for core, ref in enumerate((own_ref, other_ref)):
        held_q[core * places * rows_q : (core + 1) * places * rows_q, :] = ref[:, :rows_q, :].reshape(
            places * rows_q, width
        )
        held_kv[core * places * rows_kv : (core + 1) * places * rows_kv, :] = ref[
            :, rows_q : rows_q + rows_kv, :
        ].reshape(places * rows_kv, width)
    wq_ref[...] = dot_nn(order_q_ref[...], held_q[...]).astype(BF)
    wkv_ref[...] = dot_nn(order_kv_ref[...], held_kv[...]).astype(BF)
    tokens = unit_ref.shape[0]
    scale_in = 1.0 + sin_scale_ref[...]
    normed_ref[...] = (unit_ref[...] * scale_in).astype(BF)
    half = near_ref.shape[0]
    normed_all_ref[:half] = (near_ref[...].astype(jnp.float32) * scale_in).astype(BF)
    normed_all_ref[half:] = (far_ref[...].astype(jnp.float32) * scale_in).astype(BF)
    head_width = sq_ref.shape[1]
    heads = wq_ref.shape[0] // head_width
    key_raw = dot_nt(normed_all_ref[...], wkv_ref[:head_width, :])
    kraw_ref[...] = key_raw
    v_ref[...] = dot_nt(normed_all_ref[...], wkv_ref[head_width:, :]).astype(BF)
    key_unit, _ = unit_of(key_raw)
    k_ref[...] = turn(key_unit * (1.0 + sk_ref[...]), cos_all_ref[...], sine_all_ref[...]).astype(BF)
    allowed = key_index_ref[...] <= row_index_ref[...]
    cosine, sine = cos_all_ref[:tokens, :], sine_all_ref[:tokens, :]
    for head in range(heads):
        span = slice(head * head_width, (head + 1) * head_width)
        raw = dot_nt(normed_ref[...], wq_ref[span, :])
        qraw_ref[:, span] = raw
        unit, _ = unit_of(raw)
        turned = turn(unit * (1.0 + sq_ref[...]), cosine, sine)
        query = (turned * head_width ** (-0.5)).astype(BF)
        q_ref[:, span] = query
        scores = jnp.where(allowed, dot_nt(query, k_ref[...]), -1e30)
        top = jnp.max(scores, axis=1, keepdims=True)
        lse = top + jnp.log(jnp.sum(jnp.exp(scores - top), axis=1, keepdims=True))
        lse_ref[:, head : head + 1] = lse
        probs = jnp.exp(scores - lse).astype(BF)
        attn_ref[:, span] = dot_nn(probs, v_ref[...]).astype(BF)


def project_kernel(
    attn_ref, order_ref, own_ref, other_ref, resid_ref, sattn_ref, spre_ref,
    held_ref, ahead_ref, projected_ref, middle_ref, pre_ref,
):
    places, rows, width = own_ref.shape
    held_ref[: places * rows, :] = own_ref[...].reshape(places * rows, width)
    held_ref[places * rows :, :] = other_ref[...].reshape(places * rows, width)
    ahead_ref[...] = dot_nn(attn_ref[...], order_ref[...]).astype(BF)
    projected = dot_nn(ahead_ref[...], held_ref[...])
    projected_ref[...] = projected
    unit, _ = unit_of(projected)
    middle = resid_ref[...] + unit * (1.0 + sattn_ref[...])
    middle_ref[...] = middle
    unit, _ = unit_of(middle)
    pre_ref[...] = (unit * (1.0 + spre_ref[...])).astype(BF)


GELU_A = (2.0 / 3.141592653589793) ** 0.5


def feed_kernel(*refs):
    pres, weights = refs[:4], refs[4:12]
    part_refs = refs[12:16]
    gate_ref, up_ref, inner_ref, pre_ref, wg_ref, wu_ref, wd_ref = refs[16:]
    tokens = pres[0].shape[0]
    rows = weights[0].shape[0] // 3
    for number, ref in enumerate(pres):
        pre_ref[number * tokens : (number + 1) * tokens, :] = ref[...]
    for number, ref in enumerate(weights):
        span = slice(number * rows, (number + 1) * rows)
        wg_ref[span, :] = ref[:rows, :]
        wu_ref[span, :] = ref[rows : 2 * rows, :]
        wd_ref[span, :] = ref[2 * rows :, :]
    for number in range(4):
        at = slice(number * tokens, (number + 1) * tokens)
        gate = dot_nt(pre_ref[at, :], wg_ref[...])
        up = dot_nt(pre_ref[at, :], wu_ref[...])
        gate_ref[at, :] = gate
        up_ref[at, :] = up
        bent = jnp.tanh(GELU_A * (gate + 0.044715 * (gate * gate * gate)))
        inner = (0.5 * gate * (1.0 + bent) * up).astype(BF)
        inner_ref[at, :] = inner
        part_refs[number][...] = dot_nn(inner, wd_ref[...]).astype(part_refs[number].dtype)


def turning_kernel(
    own_ref, come1_ref, come2_ref, come3_ref, middle_ref, gout_ref, spost_ref,
    block_out_ref, gffn_ref, gspost_ref,
):
    ffn = own_ref[...]
    for ref in (come1_ref, come2_ref, come3_ref):
        ffn = ffn + ref[...].astype(jnp.float32)
    unit, inverse = unit_of(ffn)
    grad_out = gout_ref[...]
    block_out_ref[...] = middle_ref[...] + unit * (1.0 + spost_ref[...])
    gspost_ref[...] = jnp.sum(grad_out * unit, axis=0, keepdims=True)
    gffn_ref[...] = rms_back(unit, inverse, grad_out * (1.0 + spost_ref[...])).astype(BF)


def feed_back_kernel(*refs):
    grads = refs[:4]
    gate_ref, up_ref, wg_ref, wu_ref, wd_ref = refs[4:9]
    part_refs = refs[9:13]
    gffn_ref, ggate_ref, gup_ref = refs[13:]
    tokens = grads[0].shape[0]
    for number, ref in enumerate(grads):
        at = slice(number * tokens, (number + 1) * tokens)
        gffn_ref[at, :] = ref[...]
        grad_inner = dot_nt(ref[...], wd_ref[...])
        gate = gate_ref[at, :]
        square = gate * gate
        bent = jnp.tanh(GELU_A * (gate + 0.044715 * (square * gate)))
        curve = 0.5 * gate * (1.0 + bent)
        slope = 0.5 * (1.0 + bent) + 0.5 * gate * (1.0 - bent * bent) * (
            GELU_A * (1.0 + 3.0 * 0.044715 * square)
        )
        grad_up = (grad_inner * curve).astype(BF)
        grad_gate = (grad_inner * up_ref[at, :] * slope).astype(BF)
        ggate_ref[at, :] = grad_gate
        gup_ref[at, :] = grad_up
        part_refs[number][...] = (dot_nn(grad_gate, wg_ref[...]) + dot_nn(grad_up, wu_ref[...])).astype(
            part_refs[number].dtype
        )


def feed_weights_kernel(inner_ref, pre_ref, gffn_ref, ggate_ref, gup_ref, own_ref, other_ref):
    places, rows, width = own_ref.shape
    rows = rows // 3
    shape = (places, rows, width)
    for core, ref in enumerate((own_ref, other_ref)):
        span = slice(core * places * rows, (core + 1) * places * rows)
        ref[:, :rows, :] = dot_tn(ggate_ref[:, span], pre_ref[...]).astype(BF).reshape(shape)
        ref[:, rows : 2 * rows, :] = dot_tn(gup_ref[:, span], pre_ref[...]).astype(BF).reshape(shape)
        ref[:, 2 * rows :, :] = dot_tn(inner_ref[:, span], gffn_ref[...]).astype(BF).reshape(shape)


def project_back_kernel(
    own_ref, come1_ref, come2_ref, come3_ref, gout_ref, projected_ref, middle_ref, held_ref, ahead_ref,
    order_ref, sattn_ref, spre_ref,
    gresid_ref, gattn_ref, gown_ref, gother_ref, gsattn_ref, gspre_ref,
):
    grad_pre = own_ref[...]
    for ref in (come1_ref, come2_ref, come3_ref):
        grad_pre = grad_pre + ref[...].astype(jnp.float32)
    unit_p, inverse_p = unit_of(middle_ref[...])
    unit_a, inverse_a = unit_of(projected_ref[...])
    gspre_ref[...] = jnp.sum(grad_pre * unit_p, axis=0, keepdims=True)
    grad_middle = gout_ref[...] + rms_back(unit_p, inverse_p, grad_pre * (1.0 + spre_ref[...]))
    gresid_ref[...] = grad_middle
    gsattn_ref[...] = jnp.sum(grad_middle * unit_a, axis=0, keepdims=True)
    grad_proj = rms_back(unit_a, inverse_a, grad_middle * (1.0 + sattn_ref[...])).astype(BF)
    grad_held = dot_nt(grad_proj, held_ref[...]).astype(BF)
    gattn_ref[...] = dot_nt(grad_held, order_ref[...]).astype(BF)
    half = held_ref.shape[0] // 2
    gown_ref[...] = dot_tn(ahead_ref[:, :half], grad_proj).astype(BF).reshape(gown_ref.shape)
    gother_ref[...] = dot_tn(ahead_ref[:, half:], grad_proj).astype(BF).reshape(gother_ref.shape)


def attend_back_kernel(
    grad_attn_ref, attn_ref, q_ref, k_ref, v_ref, lse_ref, qraw_ref, kraw_ref, wq_ref, wkv_ref,
    sq_ref, sk_ref, cos_all_ref, sine_all_ref, key_index_ref, row_index_ref,
    normed_ref, normed_all_ref, unit_ref, near_ref, far_ref, order_q_ref, order_kv_ref,
    own_ref, other_ref, gnear_ref, gfar_ref, gq_ref, gsin_ref, gsq_ref, gsk_ref,
    probs_scr, gscores_scr, grows_scr, qrows_scr, gqraw_scr, gkv_scr,
):
    head_width = sq_ref.shape[1]
    heads = wq_ref.shape[0] // head_width
    tokens = q_ref.shape[0]
    cosine, sine = cos_all_ref[:tokens, :], sine_all_ref[:tokens, :]
    allowed = key_index_ref[...] <= row_index_ref[...]
    grad_sq = jnp.zeros((1, head_width), jnp.float32)
    for head in range(heads):
        span = slice(head * head_width, (head + 1) * head_width)
        rows = slice(head * tokens, (head + 1) * tokens)
        query = q_ref[:, span]
        grad_rows = grad_attn_ref[:, span]
        delta = jnp.sum(
            grad_rows.astype(jnp.float32) * attn_ref[:, span].astype(jnp.float32),
            axis=1,
            keepdims=True,
        )
        scores = jnp.where(allowed, dot_nt(query, k_ref[...]), -1e30)
        probs = jnp.exp(scores - lse_ref[:, head : head + 1])
        grad_scores = (probs * (dot_nt(grad_rows, v_ref[...]) - delta)).astype(BF)
        probs_scr[rows, :] = probs.astype(BF)
        gscores_scr[rows, :] = grad_scores
        grows_scr[rows, :] = grad_rows
        qrows_scr[rows, :] = query
        grad_query = dot_nn(grad_scores, k_ref[...]) * head_width ** (-0.5)
        grad_query = turn_back(grad_query, cosine, sine)
        unit, inverse = unit_of(qraw_ref[:, span])
        grad_sq = grad_sq + jnp.sum(grad_query * unit, axis=0, keepdims=True)
        grad_raw = rms_back(unit, inverse, grad_query * (1.0 + sq_ref[...]))
        gqraw_scr[:, span] = grad_raw.astype(BF)
    gsq_ref[...] = grad_sq
    grad_key = dot_tn(gscores_scr[...], qrows_scr[...])
    grad_value = dot_tn(probs_scr[...], grows_scr[...]).astype(BF)
    grad_key = turn_back(grad_key, cos_all_ref[...], sine_all_ref[...])
    unit, inverse = unit_of(kraw_ref[...])
    gsk_ref[...] = jnp.sum(grad_key * unit, axis=0, keepdims=True)
    grad_kraw = rms_back(unit, inverse, grad_key * (1.0 + sk_ref[...])).astype(BF)
    half = near_ref.shape[0]
    grad_normed = dot_nn(grad_kraw, wkv_ref[:head_width, :]) + dot_nn(
        grad_value, wkv_ref[head_width:, :]
    )
    grad_q = dot_nn(gqraw_scr[...], wq_ref[...])
    gq_ref[...] = grad_q
    gsin_ref[...] = (
        jnp.sum(grad_normed[:half] * near_ref[...].astype(jnp.float32), axis=0, keepdims=True)
        + jnp.sum(grad_normed[half:] * far_ref[...].astype(jnp.float32), axis=0, keepdims=True)
        + jnp.sum(grad_q * unit_ref[...], axis=0, keepdims=True)
    )
    gnear_ref[:, :head_width] = grad_kraw[:half]
    gnear_ref[:, head_width:] = grad_value[:half]
    gfar_ref[:, :head_width] = grad_kraw[half:]
    gfar_ref[:, head_width:] = grad_value[half:]
    gkv_scr[:head_width, :] = dot_tn(grad_kraw, normed_all_ref[...]).astype(BF)
    gkv_scr[head_width:, :] = dot_tn(grad_value, normed_all_ref[...]).astype(BF)
    grad_wq = dot_tn(gqraw_scr[...], normed_ref[...]).astype(BF)
    held_q = dot_tn(order_q_ref[...], grad_wq).astype(BF)
    held_kv = dot_tn(order_kv_ref[...], gkv_scr[...]).astype(BF)
    places, _, width = own_ref.shape
    rows_q = held_q.shape[0] // (2 * places)
    rows_kv = held_kv.shape[0] // (2 * places)
    for core, ref in enumerate((own_ref, other_ref)):
        ref[:, :rows_q, :] = held_q[core * places * rows_q : (core + 1) * places * rows_q].reshape(
            places, rows_q, width
        )
        ref[:, rows_q : rows_q + rows_kv, :] = held_kv[
            core * places * rows_kv : (core + 1) * places * rows_kv
        ].reshape(places, rows_kv, width)


def shards_plain(
    hidden_in,
    positions,
    w_query,
    w_key,
    w_value,
    w_output,
    w_gate,
    w_up,
    w_down,
    norm_scales,
    grad_out,
):
    width = hidden_in.shape[2]
    groups = lax.axis_size("ctx")
    count_dp = lax.axis_size("dp")
    chips = groups // 2
    owners = count_dp * groups
    place = lax.axis_index("ctx")
    row = lax.axis_index("dp")
    resid = hidden_in[0]
    posit = positions[0]
    grad_nat = grad_out[0]
    tokens = resid.shape[0]
    block = tokens // 2
    head_width = w_key.shape[0] * owners
    heads = w_query.shape[0] * owners // head_width
    rows_q, rows_k = w_query.shape[0], w_key.shape[0]
    scale_part = norm_scales.shape[0]

    tie = lax.optimization_barrier
    scale_rows = jnp.zeros((8, width), BF).at[0, :scale_part].set(norm_scales)
    first = gather_over(
        jnp.concatenate([w_query, w_key, w_value, scale_rows], axis=0)[None], swap_z, chips
    )
    rows_f = w_gate.shape[0]
    group_a = jnp.concatenate([w_gate, w_output], axis=0)[None]
    group_b = jnp.concatenate([w_up, w_down], axis=0)[None]
    inverse_in = lax.rsqrt(jnp.mean(resid * resid, axis=-1, keepdims=True) + EPS)
    unit_in = resid * inverse_in
    place_rows = jnp.zeros((8, width), BF)
    place_rows = place_rows.at[0, :tokens].set((posit // 64).astype(BF))
    place_rows = place_rows.at[1, :tokens].set((posit % 64).astype(BF))
    seq_part = jnp.concatenate([unit_in.astype(BF), place_rows], axis=0)[None]
    first, group_a, group_b, seq_part = tie((first, group_a, group_b, seq_part))
    first = gather_over(first[None], swap_dp, count_dp)
    group_a = gather_over(group_a, swap_z, chips)
    group_b = gather_over(group_b, swap_z, chips)
    first, group_a, group_b, seq_part = tie((first, group_a, group_b, seq_part))
    first = first.reshape((owners // 2,) + first.shape[2:])
    group_a = double(group_a, swap_dp, 1)
    group_b = double(group_b, swap_dp, 2)
    seq_z = gather_over(seq_part, swap_z, chips)
    first = jnp.concatenate([first, swap_ctx(first, 1)], axis=0)
    first, group_a, group_b, seq_z = tie((first, group_a, group_b, seq_z))
    seq_all = jnp.concatenate([seq_z, swap_ctx(seq_z, 1)], axis=0)
    group_a = double(group_a, swap_dp, 2)
    group_b = double_inner(group_b, swap_dp, 1)
    far_core, far_dp, far_z = (
        jnp.arange(owners, dtype=jnp.int32) // (owners // 2),
        (jnp.arange(owners, dtype=jnp.int32) // chips) % count_dp,
        jnp.arange(owners, dtype=jnp.int32) % chips,
    )
    owner_of = (row ^ far_dp) * groups + (place ^ (2 * far_z + far_core))
    order_q = row_order(owner_of, rows_q)
    order_k = row_order(owner_of, rows_k)
    order_s = row_order(owner_of, 1)
    full_query = reorder(order_q, first[:, :rows_q].reshape(-1, width))
    full_key = reorder(order_k, first[:, rows_q : rows_q + rows_k].reshape(-1, width))
    full_value = reorder(order_k, first[:, rows_q + rows_k : rows_q + 2 * rows_k].reshape(-1, width))
    full_scales = reorder(order_s, first[:, rows_q + 2 * rows_k, :scale_part]).reshape(-1)
    scale_in, scale_attn, scale_pre, scale_post, scale_query, scale_key = split_scales(
        full_scales, width, head_width
    )

    seq_len = groups * tokens
    seq_core, seq_zed = (
        jnp.arange(groups, dtype=jnp.int32) // chips,
        jnp.arange(groups, dtype=jnp.int32) % chips,
    )
    key_index = natural_rows(place ^ (2 * seq_zed + seq_core), block, groups)
    row_index = natural_rows(place[None], block, groups)
    unit_all = seq_all[:, :tokens].reshape(seq_len, width).astype(jnp.float32)
    pos_all = (
        seq_all[:, tokens, :tokens].astype(jnp.int32) * 64
        + seq_all[:, tokens + 1, :tokens].astype(jnp.int32)
    ).reshape(seq_len)
    normed = (unit_in * (1.0 + scale_in)).astype(BF)
    normed_all = (unit_all * (1.0 + scale_in)).astype(BF)

    query_raw = times_wt(normed, full_query).reshape(tokens, heads, head_width)
    key_raw = times_wt(normed_all, full_key)
    value_bf = times_wt(normed_all, full_value).astype(BF)

    def query_piece(raw, scale):
        return rotate(rms_scale(raw, scale), posit) * head_width ** (-0.5)

    def key_piece(raw, scale):
        return rotate(rms_scale(raw, scale)[:, None, :], pos_all)[:, 0, :]

    query_rot, query_back = jax.vjp(query_piece, query_raw, scale_query)
    key_rot, key_back = jax.vjp(key_piece, key_raw, scale_key)
    query_bf = jnp.swapaxes(query_rot.astype(BF), 0, 1).reshape(heads * tokens, head_width)
    key_bf = key_rot.astype(BF)
    allowed = jnp.tile(key_index[None, :] <= row_index[:, None], (heads, 1))
    scores = jnp.where(allowed, times_wt(query_bf, key_bf), -1e30)
    top = jnp.max(scores, axis=1, keepdims=True)
    lse = top + jnp.log(jnp.sum(jnp.exp(scores - top), axis=1, keepdims=True))
    probs = jnp.exp(scores - lse)
    probs_bf = probs.astype(BF)
    mixed = jnp.dot(probs_bf, value_bf, preferred_element_type=jnp.float32).astype(BF)
    attn_bf = jnp.swapaxes(mixed.reshape(heads, tokens, head_width), 0, 1).reshape(tokens, -1)

    group_a, group_b, attn_bf, probs = lax.optimization_barrier((group_a, group_b, attn_bf, probs))
    halves_a = (group_a, swap_ctx(group_a, 1))
    halves_b = (group_b, swap_ctx(group_b, 1))
    gates = [half[:, :rows_f].reshape(-1, width) for half in halves_a]
    ups = [half[:, :rows_f].reshape(-1, width) for half in halves_b]
    downs = [half[:, rows_f:].reshape(-1, width) for half in halves_b]
    out_held = jnp.concatenate([half[:, rows_f:].reshape(-1, width) for half in halves_a], axis=0)
    full_output = reorder(order_q, out_held)
    projected = jnp.dot(attn_bf, full_output, preferred_element_type=jnp.float32)
    (middle, pre_ffn), mid_back = jax.vjp(mid_piece, resid, projected, scale_attn, scale_pre)
    pre_bf = pre_ffn.astype(BF)
    inners, glu_backs = [], []
    for half_no in range(2):
        inner, glu_back = jax.vjp(
            glu_piece, times_wt(pre_bf, gates[half_no]), times_wt(pre_bf, ups[half_no])
        )
        inners.append(inner.astype(BF))
        glu_backs.append(glu_back)
    ffn = sum(
        jnp.dot(inners[half_no], downs[half_no], preferred_element_type=jnp.float32)
        for half_no in range(2)
    )
    block_out, out_back = jax.vjp(out_piece, middle, ffn, scale_post)
    grad_mid, grad_ffn, grad_scale_post = out_back(grad_nat)
    grad_ffn_bf = grad_ffn.astype(BF)
    grad_pre = 0.0
    downs_grad, gates_grad, ups_grad = [], [], []
    for half_no in range(2):
        grad_gate, grad_upward = glu_backs[half_no](times_wt(grad_ffn_bf, downs[half_no]))
        gate_bf = grad_gate.astype(BF)
        upward_bf = grad_upward.astype(BF)
        grad_pre = grad_pre + (
            jnp.dot(gate_bf, gates[half_no], preferred_element_type=jnp.float32)
            + jnp.dot(upward_bf, ups[half_no], preferred_element_type=jnp.float32)
        )
        downs_grad.append(outer_sum(inners[half_no], grad_ffn_bf).astype(BF))
        gates_grad.append(outer_sum(gate_bf, pre_bf).astype(BF))
        ups_grad.append(outer_sum(upward_bf, pre_bf).astype(BF))
    grads_b = [
        jnp.concatenate(
            [
                ups_grad[half_no].reshape(-1, rows_f, width),
                downs_grad[half_no].reshape(-1, rows_f, width),
            ],
            axis=1,
        )
        for half_no in range(2)
    ]
    grads_b = add_bf16(grads_b[0], swap_ctx(grads_b[1], 1)).astype(BF)
    grad_resid_a, grad_proj, grad_scale_attn, grad_scale_pre = mid_back((grad_mid, grad_pre))
    grad_proj_bf = grad_proj.astype(BF)
    grad_attn_bf = times_wt(grad_proj_bf, full_output).astype(BF)
    out_grad = reorder_back(order_q, outer_sum(attn_bf, grad_proj_bf))
    out_grad = out_grad.reshape(2, -1, rows_q, width)
    grads_a = [
        jnp.concatenate([gates_grad[half_no].reshape(-1, rows_f, width), out_grad[half_no]], axis=1)
        for half_no in range(2)
    ]
    grads_a = add_bf16(grads_a[0], swap_ctx(grads_a[1], 1)).astype(BF)
    grads_a, grads_b, grad_attn_bf, pre_bf = lax.optimization_barrier(
        (grads_a, grads_b, grad_attn_bf, pre_bf)
    )
    grads_a = halve(grads_a, swap_dp, 2)
    grads_b = halve_inner(grads_b, swap_dp, 1)

    grad_rows = jnp.swapaxes(grad_attn_bf.reshape(tokens, heads, head_width), 0, 1).reshape(
        heads * tokens, head_width
    )
    delta = jnp.sum(
        grad_rows.astype(jnp.float32) * mixed.astype(jnp.float32), axis=1, keepdims=True
    )
    grad_scores = (probs * (times_wt(grad_rows, value_bf) - delta)).astype(BF)
    grad_query = jnp.dot(grad_scores, key_bf, preferred_element_type=jnp.float32)
    grad_query = jnp.swapaxes(grad_query.reshape(heads, tokens, head_width), 0, 1)
    grad_key = outer_sum(grad_scores, query_bf)
    grad_value_bf = outer_sum(probs_bf, grad_rows).astype(BF)
    grad_qraw, grad_scale_query = query_back(grad_query)
    grad_kraw, grad_scale_key = key_back(grad_key)
    grad_qraw_bf = grad_qraw.reshape(tokens, heads * head_width).astype(BF)
    grad_kraw_bf = grad_kraw.astype(BF)

    grad_normed_q = jnp.dot(grad_qraw_bf, full_query, preferred_element_type=jnp.float32)
    grad_normed = jnp.dot(grad_kraw_bf, full_key, preferred_element_type=jnp.float32) + jnp.dot(
        grad_value_bf, full_value, preferred_element_type=jnp.float32
    )
    grad_scale_in = jnp.sum(grad_normed * unit_all, axis=0) + jnp.sum(
        grad_normed_q * unit_in, axis=0
    )
    far = grad_normed.astype(BF).reshape(2, chips, tokens, width)
    grad_w_query = reorder_back(order_q, outer_sum(grad_qraw_bf, normed))
    grad_w_key = reorder_back(order_k, outer_sum(grad_kraw_bf, normed_all))
    grad_w_value = reorder_back(order_k, outer_sum(grad_value_bf, normed_all))
    grad_scales = jnp.concatenate(
        [
            grad_scale_in,
            grad_scale_attn,
            grad_scale_pre,
            grad_scale_post,
            grad_scale_query,
            grad_scale_key,
        ]
    ).reshape(owners, scale_part)
    scales_back = reorder_back(order_s, grad_scales)
    packed = jnp.concatenate(
        [
            grad_w_query.reshape(owners, rows_q, width),
            grad_w_key.reshape(owners, rows_k, width),
            grad_w_value.reshape(owners, rows_k, width),
            jnp.zeros((owners, 8, width), BF).at[:, 0, :scale_part].set(scales_back),
        ],
        axis=1,
    ).reshape(2, -1, width)
    far_sum = add_bf16(far[0], swap_ctx(far[1], 1)).astype(BF)
    grads_a, grads_b, packed, far_sum = tie((grads_a, grads_b, packed, far_sum))
    grads_a = halve(grads_a, swap_dp, 1)
    grads_b = halve(grads_b, swap_dp, 2)
    own_normed = scatter_over(far_sum, swap_z, chips) + grad_normed_q
    packed = add_bf16(packed[0], swap_ctx(packed[1], 1)).astype(BF)
    grads_a, grads_b, packed, own_normed = tie((grads_a, grads_b, packed, own_normed))
    own_first = scatter_chip(packed)
    sum_a = scatter_over(grads_a, swap_z, chips)
    sum_b = scatter_over(grads_b, swap_z, chips)
    own_gate, own_output = sum_a[:rows_f], sum_a[rows_f:]
    own_up, own_down = sum_b[:rows_f], sum_b[rows_f:]
    own_query = own_first[:rows_q]
    own_key = own_first[rows_q : rows_q + rows_k]
    own_value = own_first[rows_q + rows_k : rows_q + 2 * rows_k]
    own_scales = own_first[rows_q + 2 * rows_k, :scale_part]
    grad_resid = grad_resid_a + rms_back(unit_in, inverse_in, own_normed * (1.0 + scale_in))
    return (
        block_out[None],
        grad_resid[None],
        own_query,
        own_key,
        own_value,
        own_output,
        own_gate,
        own_up,
        own_down,
        own_scales,
    )


def shards(*args):
    hidden_in, w_query, w_gate = args[0], args[2], args[6]
    fits = hidden_in.shape[1] * lax.axis_size("ctx") <= 2048 and lax.axis_size("ctx") == 8
    fits = fits and lax.axis_size("dp") == 4
    if fits and w_query.shape[0] % 16 == 0 and w_gate.shape[0] % 16 == 0 and args[3].shape[0] == 8:
        return shards_kernels(*args)
    return shards_plain(*args)


def swaps(block, swap):
    return [swap(block, bits) for bits in range(1, 4)]


def shards_kernels(
    hidden_in,
    positions,
    w_query,
    w_key,
    w_value,
    w_output,
    w_gate,
    w_up,
    w_down,
    norm_scales,
    grad_out,
):
    width = hidden_in.shape[2]
    groups = lax.axis_size("ctx")
    count_dp = lax.axis_size("dp")
    chips = groups // 2
    owners = count_dp * groups
    place = lax.axis_index("ctx")
    row = lax.axis_index("dp")
    resid = hidden_in[0]
    posit = positions[0]
    tokens = resid.shape[0]
    block = tokens // 2
    seq_len = groups * tokens
    head_width = w_key.shape[0] * owners
    heads = w_query.shape[0] * owners // head_width
    rows_q, rows_k, rows_f = w_query.shape[0], w_key.shape[0], w_gate.shape[0]
    last = rows_q + 2 * rows_k
    scale_part = norm_scales.shape[0]
    f32 = jnp.float32
    tie = lax.optimization_barrier

    far_core, far_dp, far_z = (
        jnp.arange(owners, dtype=jnp.int32) // (owners // 2),
        (jnp.arange(owners, dtype=jnp.int32) // chips) % count_dp,
        jnp.arange(owners, dtype=jnp.int32) % chips,
    )
    owner_of = (row ^ far_dp) * groups + (place ^ (2 * far_z + far_core))
    order_q = row_order(owner_of, rows_q)
    order_s = row_order(owner_of, 1)
    held_row = jnp.arange(2 * rows_k * owners, dtype=jnp.int32)
    held_at = (
        (held_row % (2 * rows_k)) // rows_k * head_width
        + jnp.repeat(owner_of, 2 * rows_k) * rows_k
        + held_row % rows_k
    )
    order_kv = (held_row[:, None] == held_at[None, :]).astype(BF)
    seq_core, seq_zed = (
        jnp.arange(groups, dtype=jnp.int32) // chips,
        jnp.arange(groups, dtype=jnp.int32) % chips,
    )
    key_index = natural_rows(place ^ (2 * seq_zed + seq_core), block, groups).reshape(1, seq_len)
    row_index = natural_rows(place[None], block, groups).reshape(tokens, 1)

    last_rows = jnp.zeros((8, width), BF).at[0, :scale_part].set(norm_scales)
    last_rows = last_rows.at[1, :tokens].set((posit // 64).astype(BF))
    last_rows = last_rows.at[2, :tokens].set((posit % 64).astype(BF))
    first = jnp.concatenate([w_query, w_key, w_value, last_rows], axis=0)
    feed = jnp.concatenate([w_gate, w_up, w_down], axis=0)
    inverse_in = lax.rsqrt(jnp.mean(resid * resid, axis=-1, keepdims=True) + EPS)
    unit_in = resid * inverse_in
    unit_bf = unit_in.astype(BF)
    first = gather_over(first[None], swap_z, chips)
    first, unit_bf, feed, w_output, order_q, order_kv = tie(
        (first, unit_bf, feed, w_output, order_q, order_kv)
    )
    last_far = swap_ctx(first[:, last:], 1)
    pos_all = jnp.stack([first[:, last:], last_far], axis=0)[:, :, :, :tokens].astype(f32)
    pos_all = (pos_all[:, :, 1] * 64.0 + pos_all[:, :, 2]).reshape(seq_len)
    half = head_width // 2
    freq_table = 1000000.0 ** (-jnp.arange(half, dtype=jnp.float32) / half)
    angle = pos_all[:, None] * freq_table[None, :]
    cos_all, sine_all = jnp.cos(angle), jnp.sin(angle)
    first = gather_over(first[None], swap_dp, count_dp).reshape((owners // 2,) + first.shape[1:])
    near = gather_over(unit_bf[None], swap_z, chips).reshape(chips * tokens, width)
    first, near, feed, w_output, cos_all, sine_all = tie(
        (first, near, feed, w_output, cos_all, sine_all)
    )
    other = swap_ctx(first, 1)
    far = swap_ctx(near, 1)
    out_own = gather_over(w_output[None], swap_z, chips)
    other, far, out_own, feed = tie((other, far, out_own, feed))
    scale_rows = jnp.concatenate([first[:, last, :scale_part], other[:, last, :scale_part]], axis=0)
    full_scales = reorder(order_s, scale_rows).reshape(-1)
    scale_in, scale_attn, scale_pre, scale_post, scale_query, scale_key = [
        scale[None] for scale in split_scales(full_scales, width, head_width)
    ]
    feed_z2 = swap_z(feed, 2)
    feed_z1 = swap_z(feed, 1)
    out_own = gather_over(out_own[None], swap_dp, count_dp).reshape((owners // 2, rows_q, width))
    (w_q, w_kv, normed, normed_all, query_raw, key_raw, query_bf, key_bf, value_bf, attn_bf, lse) = (
        call_kernel(
            attend_kernel,
            [
                ((heads * head_width, width), BF),
                ((2 * head_width, width), BF),
                ((tokens, width), BF),
                ((seq_len, width), BF),
                ((tokens, heads * head_width), f32),
                ((seq_len, head_width), f32),
                ((tokens, heads * head_width), BF),
                ((seq_len, head_width), BF),
                ((seq_len, head_width), BF),
                ((tokens, heads * head_width), BF),
                ((tokens, heads), f32),
            ],
            [((heads * head_width, width), BF), ((2 * head_width, width), BF)],
            12_000_000_000,
            (
                unit_in, near, far, first, other, order_q, order_kv, scale_in, scale_query, scale_key,
                cos_all, sine_all, key_index, row_index,
            ),
            mebibytes=52,
        )
    )
    attn_bf, feed_z1, feed_z2, out_own, feed = tie((attn_bf, feed_z1, feed_z2, out_own, feed))
    out_other = swap_ctx(out_own, 1)
    feed_z3 = swap_z(feed, 3)
    feed_c0 = swap_ctx(feed, 1)
    feed_c1 = swap_ctx(feed_z1, 1)
    feed_c2 = swap_ctx(feed_z2, 1)
    held_out, ahead, projected, middle, pre = call_kernel(
        project_kernel,
        [
            ((owners * rows_q, width), BF),
            ((tokens, owners * rows_q), BF),
            ((tokens, width), f32),
            ((tokens, width), f32),
            ((tokens, width), BF),
        ],
        [],
        2_000_000_000,
        (attn_bf, order_q, out_own, out_other, resid, scale_attn, scale_pre),
    )
    pres = swaps(pre, swap_dp)
    pre, pres, feed_z3, feed_c0, feed_c1, feed_c2 = tie((pre, pres, feed_z3, feed_c0, feed_c1, feed_c2))
    feed_c3 = swap_ctx(feed_z3, 1)
    part_shapes = [((tokens, width), f32)] + [((tokens, width), BF)] * 3
    all_tokens = count_dp * tokens
    hidden = groups * rows_f
    outs = call_kernel(
        feed_kernel,
        part_shapes
        + [
            ((all_tokens, hidden), f32),
            ((all_tokens, hidden), f32),
            ((all_tokens, hidden), BF),
            ((all_tokens, width), BF),
        ]
        + [((hidden, width), BF)] * 3,
        [],
        3_000_000_000,
        [pre] + pres + [feed, feed_z1, feed_z2, feed_z3, feed_c0, feed_c1, feed_c2, feed_c3],
    )
    parts, kept = outs[:4], outs[4:]
    comes = [swap_dp(parts[bits], bits) for bits in range(1, 4)]
    block_out, grad_ffn, grad_s_post = call_kernel(
        turning_kernel,
        [((tokens, width), f32), ((tokens, width), BF), ((1, width), f32)],
        [],
        100_000_000,
        [parts[0]] + comes + [middle, grad_out[0], scale_post],
    )
    gate, up, inner, pre_all, w_g, w_u, w_d = kept
    outs = call_kernel(
        feed_back_kernel,
        part_shapes + [((all_tokens, width), BF), ((all_tokens, hidden), BF), ((all_tokens, hidden), BF)],
        [],
        3_000_000_000,
        [grad_ffn] + swaps(grad_ffn, swap_dp) + [gate, up, w_g, w_u, w_d],
    )
    parts, back = outs[:4], outs[4:]
    comes = [swap_dp(parts[bits], bits) for bits in range(1, 4)]
    g_feed, g_feed_far = call_kernel(
        feed_weights_kernel,
        [((chips, 3 * rows_f, width), BF)] * 2,
        [],
        3_000_000_000,
        [inner, pre_all] + list(back),
    )
    g_feed, g_feed_far, comes = tie((g_feed, g_feed_far, comes))
    g_feed = add_bf16(g_feed, swap_ctx(g_feed_far, 1)).astype(BF)
    grad_resid_a, grad_attn, g_out, g_out_far, grad_s_attn, grad_s_pre = call_kernel(
        project_back_kernel,
        [
            ((tokens, width), f32),
            ((tokens, heads * head_width), BF),
            (out_own.shape, BF),
            (out_own.shape, BF),
            ((1, width), f32),
            ((1, width), f32),
        ],
        [],
        3_000_000_000,
        [parts[0]]
        + comes
        + [grad_out[0], projected, middle, held_out, ahead, order_q, scale_attn, scale_pre],
    )
    g_out = add_bf16(g_out, swap_ctx(g_out_far, 1)).astype(BF).reshape(count_dp, chips, rows_q, width)
    g_out, g_feed, grad_attn = tie((g_out, g_feed, grad_attn))
    feed_come1 = swap_z(g_feed[1], 1)
    feed_come2 = swap_z(g_feed[2], 2)
    out_comes = [swap_dp(g_out[bits], bits) for bits in range(1, 4)]
    (packed, packed_far, g_near, g_far, grad_normed_q, grad_s_in, grad_s_query, grad_s_key) = call_kernel(
        attend_back_kernel,
        [
            ((owners // 2, last, width), BF),
            ((owners // 2, last, width), BF),
            ((seq_len // 2, 2 * head_width), BF),
            ((seq_len // 2, 2 * head_width), BF),
            ((tokens, width), f32),
            ((1, width), f32),
            ((1, head_width), f32),
            ((1, head_width), f32),
        ],
        [
            ((heads * tokens, seq_len), BF),
            ((heads * tokens, seq_len), BF),
            ((heads * tokens, head_width), BF),
            ((heads * tokens, head_width), BF),
            ((tokens, heads * head_width), BF),
            ((2 * head_width, width), BF),
        ],
        12_000_000_000,
        (
            grad_attn, attn_bf, query_bf, key_bf, value_bf, lse, query_raw, key_raw, w_q, w_kv,
            scale_query, scale_key, cos_all, sine_all, key_index, row_index, normed, normed_all,
            unit_in, near, far, order_q, order_kv,
        ),
        mebibytes=24,
    )
    back = (packed, packed_far, g_near, g_far, grad_normed_q, grad_s_in, grad_s_query, grad_s_key)
    back, feed_come1, feed_come2, out_comes, g_out, g_feed = tie(
        (back, feed_come1, feed_come2, out_comes, g_out, g_feed)
    )
    packed, packed_far, g_near, g_far, grad_normed_q, grad_s_in, grad_s_query, grad_s_key = back
    grad_scales = jnp.concatenate(
        [grad_s_in, grad_s_attn, grad_s_pre, grad_s_post, grad_s_query, grad_s_key], axis=1
    ).reshape(owners, scale_part)
    scales_back = reorder_back(order_s, grad_scales)
    scale_sum = add_bf16(scales_back[: owners // 2], swap_ctx(scales_back[owners // 2 :], 1))
    scale_sum = jnp.pad(scale_sum[:, None], ((0, 0), (last, 7), (0, width - scale_part)))
    packed = jnp.pad(add_bf16(packed, swap_ctx(packed_far, 1)), ((0, 0), (0, 8), (0, 0)))
    packed = (packed + scale_sum).astype(BF)
    feed_come3 = swap_z(g_feed[3, : 3 * rows_f // 2], 3)
    far_sum = add_bf16(g_near, swap_ctx(g_far, 1)).astype(BF).reshape(chips, tokens, 2 * head_width)
    out_sum = add_bf16(g_out[0], *out_comes).astype(BF)
    packed, far_sum, out_sum, g_feed, feed_come3 = tie((packed, far_sum, out_sum, g_feed, feed_come3))
    packed = scatter_over(packed.reshape((count_dp, chips) + packed.shape[1:]), swap_dp, count_dp)
    own_kv = scatter_over(far_sum, swap_z, chips).astype(BF)
    packed, own_kv, out_sum, g_feed = tie((packed.astype(BF), own_kv, out_sum, g_feed))
    own_normed = jnp.dot(own_kv, w_kv, preferred_element_type=jnp.float32) + grad_normed_q
    feed_come3 = jnp.concatenate([feed_come3, swap_z(g_feed[3, 3 * rows_f // 2 :], 3)], axis=0)
    own_feed = add_bf16(g_feed[0], feed_come1, feed_come2, feed_come3)
    own_output = scatter_over(out_sum, swap_z, chips)
    own_first = scatter_over(packed, swap_z, chips)
    grad_resid = grad_resid_a + rms_back(unit_in, inverse_in, own_normed * (1.0 + scale_in))
    return (
        block_out[None],
        grad_resid[None],
        own_first[:rows_q],
        own_first[rows_q : rows_q + rows_k],
        own_first[rows_q + rows_k : last],
        own_output,
        own_feed[:rows_f],
        own_feed[rows_f : 2 * rows_f],
        own_feed[2 * rows_f :],
        own_first[last, :scale_part],
    )


def solution(mesh):
    in_specs = (
        P("dp", "ctx", None),
        P("dp", "ctx"),
        P(("dp", "ctx"), None),
        P(("dp", "ctx"), None),
        P(("dp", "ctx"), None),
        P(("dp", "ctx"), None),
        P(("dp", "ctx"), None),
        P(("dp", "ctx"), None),
        P(("dp", "ctx"), None),
        P(("dp", "ctx")),
        P("dp", "ctx", None),
    )
    out_specs = (
        P("dp", "ctx", None),
        P("dp", "ctx", None),
        P(("dp", "ctx"), None),
        P(("dp", "ctx"), None),
        P(("dp", "ctx"), None),
        P(("dp", "ctx"), None),
        P(("dp", "ctx"), None),
        P(("dp", "ctx"), None),
        P(("dp", "ctx"), None),
        P(("dp", "ctx")),
    )
    return jax.shard_map(shards, mesh=mesh, in_specs=in_specs, out_specs=out_specs, check_vma=False)
```

```python
import jax
import jax.numpy as jnp
from jax import lax
from jax.experimental import pallas as pl
from jax.experimental.pallas import tpu as pltpu
from jax.sharding import PartitionSpec as P

EPS = 1e-06


def rms_scale(vector, scale):
    return (
        vector * lax.rsqrt(jnp.mean(vector * vector, axis=-1, keepdims=True) + EPS) * (1.0 + scale)
    )


def rotate(vector, position):
    half = vector.shape[-1] // 2
    freq_table = 1000000.0 ** (-jnp.arange(half, dtype=jnp.float32) / half)
    angle = position.astype(jnp.float32)[:, None] * freq_table[None, :]
    cosine = jnp.cos(angle)[:, None, :]
    sine = jnp.sin(angle)[:, None, :]
    first = vector[..., :half]
    second = vector[..., half:]
    return jnp.concatenate(
        [first * cosine - second * sine, second * cosine + first * sine], axis=-1
    )


def mid_piece(resid, projected, scale_attn, scale_pre):
    middle = resid + rms_scale(projected, scale_attn)
    return (middle, rms_scale(middle, scale_pre))


def glu_piece(gate, upward):
    return jax.nn.gelu(gate, approximate=True) * upward


def out_piece(middle, ffn, scale_post):
    return middle + rms_scale(ffn, scale_post)


def times_wt(left, weight):
    return lax.dot_general(
        left, weight, (((1,), (1,)), ((), ())), preferred_element_type=jnp.float32
    )


def outer_sum(left, right):
    return lax.dot_general(
        left, right, (((0,), (0,)), ((), ())), preferred_element_type=jnp.float32
    )


def split_scales(norm_scales, width, head_width):
    scales = norm_scales.astype(jnp.float32)
    pieces = [scales[index * width : (index + 1) * width] for index in range(4)]
    offset = 4 * width
    return pieces + [
        scales[offset : offset + head_width],
        scales[offset + head_width : offset + 2 * head_width],
    ]


BF = jnp.bfloat16


def swap_dp(block, bits):
    count = lax.axis_size("dp")
    return lax.ppermute(block, "dp", [(place, place ^ bits) for place in range(count)])


def swap_ctx(block, bits):
    count = lax.axis_size("ctx")
    return lax.ppermute(block, "ctx", [(place, place ^ bits) for place in range(count)])


def swap_z(block, bits):
    return swap_ctx(block, 2 * bits)


def gather_over(block, swap, count):
    if count <= 4:
        return jnp.concatenate([block] + [swap(block, bits) for bits in range(1, count)], axis=0)
    bits = 1
    while bits < count:
        block = jnp.concatenate([block, swap(block, bits)], axis=0)
        bits = 2 * bits
    return block


def add_bf16(first, *others):
    total = first.astype(jnp.float32)
    for other in others:
        total = total + other.astype(jnp.float32)
    return total


def scatter_over(blocks, swap, count):
    if count <= 4:
        return add_bf16(blocks[0], *[swap(blocks[bits], bits) for bits in range(1, count)])
    bits = count // 2
    while bits > 1:
        blocks = add_bf16(blocks[:bits], swap(blocks[bits:], bits)).astype(BF)
        bits = bits // 2
    return add_bf16(blocks[0], swap(blocks[1], 1))


def gather_chip(block):
    groups = lax.axis_size("ctx") // 2
    over_z = gather_over(block[None], swap_z, groups)
    over_dp = gather_over(over_z[None], swap_dp, lax.axis_size("dp"))
    return over_dp.reshape((-1,) + block.shape[1:])


def double(blocks, swap, bits):
    return jnp.concatenate([blocks, swap(blocks, bits)], axis=0)


def double_inner(blocks, swap, bits):
    pair = blocks.reshape((2, 1, -1) + blocks.shape[1:])
    return jnp.concatenate([pair, swap(pair, bits)], axis=1).reshape((-1,) + blocks.shape[1:])


def halve(blocks, swap, bits):
    half = blocks.shape[0] // 2
    return add_bf16(blocks[:half], swap(blocks[half:], bits)).astype(BF)


def halve_inner(blocks, swap, bits):
    quarters = blocks.reshape((2, 2, -1) + blocks.shape[1:])
    half = add_bf16(quarters[:, 0], swap(quarters[:, 1], bits)).astype(BF)
    return half.reshape((-1,) + blocks.shape[1:])


def scatter_chip(blocks):
    groups = lax.axis_size("ctx") // 2
    count = lax.axis_size("dp")
    shaped = blocks.reshape((count, groups, -1) + blocks.shape[1:])
    mid = scatter_over(shaped, swap_dp, count).astype(BF)
    return scatter_over(mid, swap_z, groups)


def scatter_all(first, second):
    return scatter_chip(add_bf16(first, swap_ctx(second, 1)).astype(BF))


def natural_rows(places, block, groups):
    within = jnp.arange(2 * block, dtype=jnp.int32)[None, :]
    early = places[:, None] * block + within
    late = (2 * groups - 1 - places[:, None]) * block + within - block
    return jnp.where(within < block, early, late).reshape(-1)


def row_order(owner_of, rows):
    count = owner_of.shape[0] * rows
    held = (owner_of[:, None] * rows + jnp.arange(rows, dtype=jnp.int32)[None, :]).reshape(1, count)
    return (jnp.arange(count, dtype=jnp.int32)[:, None] == held).astype(BF)


def reorder(order, blocks):
    return jnp.dot(order, blocks, preferred_element_type=jnp.float32).astype(BF)


def reorder_back(order, blocks):
    return outer_sum(order, blocks.astype(BF)).astype(BF)


def rms_back(unit, inverse, grad_scaled):
    return inverse * (grad_scaled - unit * jnp.mean(grad_scaled * unit, axis=-1, keepdims=True))


def dot_nt(left, right):
    return lax.dot_general(left, right, (((1,), (1,)), ((), ())), preferred_element_type=jnp.float32)


def dot_nn(left, right):
    return lax.dot_general(left, right, (((1,), (0,)), ((), ())), preferred_element_type=jnp.float32)


def dot_tn(left, right):
    return lax.dot_general(left, right, (((0,), (0,)), ((), ())), preferred_element_type=jnp.float32)


def unit_of(rows):
    inverse = lax.rsqrt(jnp.mean(rows * rows, axis=-1, keepdims=True) + EPS)
    return rows * inverse, inverse


def turn(rows, cosine, sine):
    half = rows.shape[1] // 2
    first, second = rows[:, :half], rows[:, half:]
    return jnp.concatenate([first * cosine - second * sine, second * cosine + first * sine], axis=1)


def turn_back(rows, cosine, sine):
    half = rows.shape[1] // 2
    first, second = rows[:, :half], rows[:, half:]
    return jnp.concatenate([first * cosine + second * sine, second * cosine - first * sine], axis=1)


def call_kernel(body, out_shapes, scratch, flops, inputs, mebibytes=24):
    whole = pl.BlockSpec(memory_space=pltpu.VMEM)
    return pl.pallas_call(
        body,
        out_shape=[jax.ShapeDtypeStruct(shape, dtype) for shape, dtype in out_shapes],
        in_specs=[
            pl.BlockSpec(memory_space=pltpu.SMEM) if entry.ndim == 1 else whole for entry in inputs
        ],
        out_specs=[whole] * len(out_shapes),
        scratch_shapes=[pltpu.VMEM(shape, dtype) for shape, dtype in scratch],
        compiler_params=pltpu.CompilerParams(vmem_limit_bytes=mebibytes * 1024 * 1024),
        cost_estimate=pl.CostEstimate(flops=flops, bytes_accessed=20_000_000, transcendentals=0),
    )(*inputs)


def owner_rows(owner_ref, entry, rows):
    return pl.ds(pl.multiple_of(owner_ref[entry] * rows, rows), rows)


def attend_kernel(
    unit_ref, near_ref, far_ref, own_ref, other_ref, owner_ref, order_kv_ref, sin_scale_ref, sq_ref,
    sk_ref, cos_all_ref, sine_all_ref, key_index_ref, row_index_ref,
    wq_ref, wkv_ref, normed_ref, normed_all_ref, qraw_ref, kraw_ref, q_ref, k_ref, v_ref, attn_ref, lse_ref,
    held_kv,
):
    places, _, width = own_ref.shape
    rows_q = wq_ref.shape[0] // (2 * places)
    rows_kv = held_kv.shape[0] // (2 * places)
    for core, ref in enumerate((own_ref, other_ref)):
        for at in range(places):
            wq_ref[owner_rows(owner_ref, core * places + at, rows_q), :] = ref[at, :rows_q, :]
        held_kv[core * places * rows_kv : (core + 1) * places * rows_kv, :] = ref[
            :, rows_q : rows_q + rows_kv, :
        ].reshape(places * rows_kv, width)
    wkv_ref[...] = dot_nn(order_kv_ref[...], held_kv[...]).astype(BF)
    tokens = unit_ref.shape[0]
    scale_in = 1.0 + sin_scale_ref[...]
    normed_ref[...] = (unit_ref[...] * scale_in).astype(BF)
    half = near_ref.shape[0]
    normed_all_ref[:half] = (near_ref[...].astype(jnp.float32) * scale_in).astype(BF)
    normed_all_ref[half:] = (far_ref[...].astype(jnp.float32) * scale_in).astype(BF)
    head_width = sq_ref.shape[1]
    heads = wq_ref.shape[0] // head_width
    key_raw = dot_nt(normed_all_ref[...], wkv_ref[:head_width, :])
    kraw_ref[...] = key_raw
    v_ref[...] = dot_nt(normed_all_ref[...], wkv_ref[head_width:, :]).astype(BF)
    key_unit, _ = unit_of(key_raw)
    k_ref[...] = turn(key_unit * (1.0 + sk_ref[...]), cos_all_ref[...], sine_all_ref[...]).astype(BF)
    allowed = key_index_ref[...] <= row_index_ref[...]
    cosine, sine = cos_all_ref[:tokens, :], sine_all_ref[:tokens, :]
    for head in range(heads):
        span = slice(head * head_width, (head + 1) * head_width)
        raw = dot_nt(normed_ref[...], wq_ref[span, :])
        qraw_ref[:, span] = raw
        unit, _ = unit_of(raw)
        turned = turn(unit * (1.0 + sq_ref[...]), cosine, sine)
        query = (turned * head_width ** (-0.5)).astype(BF)
        q_ref[:, span] = query
        scores = jnp.where(allowed, dot_nt(query, k_ref[...]), -1e30)
        top = jnp.max(scores, axis=1, keepdims=True)
        lse = top + jnp.log(jnp.sum(jnp.exp(scores - top), axis=1, keepdims=True))
        lse_ref[:, head : head + 1] = lse
        probs = jnp.exp(scores - lse).astype(BF)
        attn_ref[:, span] = dot_nn(probs, v_ref[...]).astype(BF)


def project_kernel(
    attn_ref, owner_ref, own_ref, other_ref, resid_ref, sattn_ref, spre_ref,
    wo_ref, projected_ref, middle_ref, pre_ref,
):
    places, rows, _ = own_ref.shape
    for core, ref in enumerate((own_ref, other_ref)):
        for at in range(places):
            wo_ref[owner_rows(owner_ref, core * places + at, rows), :] = ref[at]
    projected = dot_nn(attn_ref[...], wo_ref[...])
    projected_ref[...] = projected
    unit, _ = unit_of(projected)
    middle = resid_ref[...] + unit * (1.0 + sattn_ref[...])
    middle_ref[...] = middle
    unit, _ = unit_of(middle)
    pre_ref[...] = (unit * (1.0 + spre_ref[...])).astype(BF)


GELU_A = (2.0 / 3.141592653589793) ** 0.5


def feed_kernel(*refs):
    pres, weights = refs[:4], refs[4:12]
    part_refs = refs[12:16]
    gate_ref, up_ref, inner_ref, pre_ref, wg_ref, wu_ref, wd_ref = refs[16:]
    tokens = pres[0].shape[0]
    rows = weights[0].shape[0] // 3
    for number, ref in enumerate(pres):
        pre_ref[number * tokens : (number + 1) * tokens, :] = ref[...]
    for number, ref in enumerate(weights):
        span = slice(number * rows, (number + 1) * rows)
        wg_ref[span, :] = ref[:rows, :]
        wu_ref[span, :] = ref[rows : 2 * rows, :]
        wd_ref[span, :] = ref[2 * rows :, :]
    for number in range(4):
        at = slice(number * tokens, (number + 1) * tokens)
        gate = dot_nt(pre_ref[at, :], wg_ref[...])
        up = dot_nt(pre_ref[at, :], wu_ref[...])
        gate_ref[at, :] = gate
        up_ref[at, :] = up
        bent = jnp.tanh(GELU_A * (gate + 0.044715 * (gate * gate * gate)))
        inner = (0.5 * gate * (1.0 + bent) * up).astype(BF)
        inner_ref[at, :] = inner
        part_refs[number][...] = dot_nn(inner, wd_ref[...]).astype(part_refs[number].dtype)


def turning_kernel(
    own_ref, come1_ref, come2_ref, come3_ref, middle_ref, gout_ref, spost_ref,
    block_out_ref, gffn_ref, gspost_ref,
):
    ffn = own_ref[...]
    for ref in (come1_ref, come2_ref, come3_ref):
        ffn = ffn + ref[...].astype(jnp.float32)
    unit, inverse = unit_of(ffn)
    grad_out = gout_ref[...]
    block_out_ref[...] = middle_ref[...] + unit * (1.0 + spost_ref[...])
    gspost_ref[...] = jnp.sum(grad_out * unit, axis=0, keepdims=True)
    gffn_ref[...] = rms_back(unit, inverse, grad_out * (1.0 + spost_ref[...])).astype(BF)


def feed_back_kernel(*refs):
    grads = refs[:4]
    gate_ref, up_ref, wg_ref, wu_ref, wd_ref = refs[4:9]
    part_refs = refs[9:13]
    gffn_ref, ggate_ref, gup_ref = refs[13:]
    tokens = grads[0].shape[0]
    for number, ref in enumerate(grads):
        at = slice(number * tokens, (number + 1) * tokens)
        gffn_ref[at, :] = ref[...]
        grad_inner = dot_nt(ref[...], wd_ref[...])
        gate = gate_ref[at, :]
        square = gate * gate
        bent = jnp.tanh(GELU_A * (gate + 0.044715 * (square * gate)))
        curve = 0.5 * gate * (1.0 + bent)
        slope = 0.5 * (1.0 + bent) + 0.5 * gate * (1.0 - bent * bent) * (
            GELU_A * (1.0 + 3.0 * 0.044715 * square)
        )
        grad_up = (grad_inner * curve).astype(BF)
        grad_gate = (grad_inner * up_ref[at, :] * slope).astype(BF)
        ggate_ref[at, :] = grad_gate
        gup_ref[at, :] = grad_up
        part_refs[number][...] = (dot_nn(grad_gate, wg_ref[...]) + dot_nn(grad_up, wu_ref[...])).astype(
            part_refs[number].dtype
        )


def feed_weights_kernel(inner_ref, pre_ref, gffn_ref, ggate_ref, gup_ref, own_ref, other_ref):
    places, rows, width = own_ref.shape
    rows = rows // 3
    shape = (places, rows, width)
    for core, ref in enumerate((own_ref, other_ref)):
        span = slice(core * places * rows, (core + 1) * places * rows)
        ref[:, :rows, :] = dot_tn(ggate_ref[:, span], pre_ref[...]).astype(BF).reshape(shape)
        ref[:, rows : 2 * rows, :] = dot_tn(gup_ref[:, span], pre_ref[...]).astype(BF).reshape(shape)
        ref[:, 2 * rows :, :] = dot_tn(inner_ref[:, span], gffn_ref[...]).astype(BF).reshape(shape)


def project_back_kernel(
    own_ref, come1_ref, come2_ref, come3_ref, gout_ref, projected_ref, middle_ref, wo_ref, attn_ref,
    owner_ref, sattn_ref, spre_ref,
    gresid_ref, gattn_ref, gown_ref, gother_ref, gsattn_ref, gspre_ref,
    gwo_scr,
):
    grad_pre = own_ref[...]
    for ref in (come1_ref, come2_ref, come3_ref):
        grad_pre = grad_pre + ref[...].astype(jnp.float32)
    unit_p, inverse_p = unit_of(middle_ref[...])
    unit_a, inverse_a = unit_of(projected_ref[...])
    gspre_ref[...] = jnp.sum(grad_pre * unit_p, axis=0, keepdims=True)
    grad_middle = gout_ref[...] + rms_back(unit_p, inverse_p, grad_pre * (1.0 + spre_ref[...]))
    gresid_ref[...] = grad_middle
    gsattn_ref[...] = jnp.sum(grad_middle * unit_a, axis=0, keepdims=True)
    grad_proj = rms_back(unit_a, inverse_a, grad_middle * (1.0 + sattn_ref[...])).astype(BF)
    gattn_ref[...] = dot_nt(grad_proj, wo_ref[...]).astype(BF)
    gwo_scr[...] = dot_tn(attn_ref[...], grad_proj).astype(BF)
    places, rows, _ = gown_ref.shape
    for core, ref in enumerate((gown_ref, gother_ref)):
        for at in range(places):
            ref[at] = gwo_scr[owner_rows(owner_ref, core * places + at, rows), :]


def attend_back_kernel(
    grad_attn_ref, attn_ref, q_ref, k_ref, v_ref, lse_ref, qraw_ref, kraw_ref, wq_ref, wkv_ref,
    sq_ref, sk_ref, cos_all_ref, sine_all_ref, key_index_ref, row_index_ref,
    normed_ref, normed_all_ref, unit_ref, near_ref, far_ref, owner_ref, order_kv_ref,
    own_ref, other_ref, gnear_ref, gfar_ref, gq_ref, gsin_ref, gsq_ref, gsk_ref,
    probs_scr, gscores_scr, grows_scr, qrows_scr, gqraw_scr, gkv_scr, gwq_scr,
):
    head_width = sq_ref.shape[1]
    heads = wq_ref.shape[0] // head_width
    tokens = q_ref.shape[0]
    cosine, sine = cos_all_ref[:tokens, :], sine_all_ref[:tokens, :]
    allowed = key_index_ref[...] <= row_index_ref[...]
    grad_sq = jnp.zeros((1, head_width), jnp.float32)
    for head in range(heads):
        span = slice(head * head_width, (head + 1) * head_width)
        rows = slice(head * tokens, (head + 1) * tokens)
        query = q_ref[:, span]
        grad_rows = grad_attn_ref[:, span]
        delta = jnp.sum(
            grad_rows.astype(jnp.float32) * attn_ref[:, span].astype(jnp.float32),
            axis=1,
            keepdims=True,
        )
        scores = jnp.where(allowed, dot_nt(query, k_ref[...]), -1e30)
        probs = jnp.exp(scores - lse_ref[:, head : head + 1])
        grad_scores = (probs * (dot_nt(grad_rows, v_ref[...]) - delta)).astype(BF)
        probs_scr[rows, :] = probs.astype(BF)
        gscores_scr[rows, :] = grad_scores
        grows_scr[rows, :] = grad_rows
        qrows_scr[rows, :] = query
        grad_query = dot_nn(grad_scores, k_ref[...]) * head_width ** (-0.5)
        grad_query = turn_back(grad_query, cosine, sine)
        unit, inverse = unit_of(qraw_ref[:, span])
        grad_sq = grad_sq + jnp.sum(grad_query * unit, axis=0, keepdims=True)
        grad_raw = rms_back(unit, inverse, grad_query * (1.0 + sq_ref[...]))
        gqraw_scr[:, span] = grad_raw.astype(BF)
    gsq_ref[...] = grad_sq
    grad_key = dot_tn(gscores_scr[...], qrows_scr[...])
    grad_value = dot_tn(probs_scr[...], grows_scr[...]).astype(BF)
    grad_key = turn_back(grad_key, cos_all_ref[...], sine_all_ref[...])
    unit, inverse = unit_of(kraw_ref[...])
    gsk_ref[...] = jnp.sum(grad_key * unit, axis=0, keepdims=True)
    grad_kraw = rms_back(unit, inverse, grad_key * (1.0 + sk_ref[...])).astype(BF)
    half = near_ref.shape[0]
    grad_normed = dot_nn(grad_kraw, wkv_ref[:head_width, :]) + dot_nn(
        grad_value, wkv_ref[head_width:, :]
    )
    grad_q = dot_nn(gqraw_scr[...], wq_ref[...])
    gq_ref[...] = grad_q
    gsin_ref[...] = (
        jnp.sum(grad_normed[:half] * near_ref[...].astype(jnp.float32), axis=0, keepdims=True)
        + jnp.sum(grad_normed[half:] * far_ref[...].astype(jnp.float32), axis=0, keepdims=True)
        + jnp.sum(grad_q * unit_ref[...], axis=0, keepdims=True)
    )
    gnear_ref[:, :head_width] = grad_kraw[:half]
    gnear_ref[:, head_width:] = grad_value[:half]
    gfar_ref[:, :head_width] = grad_kraw[half:]
    gfar_ref[:, head_width:] = grad_value[half:]
    gkv_scr[:head_width, :] = dot_tn(grad_kraw, normed_all_ref[...]).astype(BF)
    gkv_scr[head_width:, :] = dot_tn(grad_value, normed_all_ref[...]).astype(BF)
    gwq_scr[...] = dot_tn(gqraw_scr[...], normed_ref[...]).astype(BF)
    held_kv = dot_tn(order_kv_ref[...], gkv_scr[...]).astype(BF)
    places, _, width = own_ref.shape
    rows_q = gwq_scr.shape[0] // (2 * places)
    rows_kv = held_kv.shape[0] // (2 * places)
    for core, ref in enumerate((own_ref, other_ref)):
        for at in range(places):
            ref[at, :rows_q, :] = gwq_scr[owner_rows(owner_ref, core * places + at, rows_q), :]
        ref[:, rows_q : rows_q + rows_kv, :] = held_kv[
            core * places * rows_kv : (core + 1) * places * rows_kv
        ].reshape(places, rows_kv, width)


def ending_kernel(*refs):
    firsts, outs, feeds, results = refs[:4], refs[4:8], refs[8:13], refs[13:]
    total = add_bf16(*[ref[...] for ref in firsts])
    row = 0
    for ref in results[:4]:
        ref[...] = total[row : row + ref.shape[0]]
        row = row + ref.shape[0]
    results[4][...] = add_bf16(*[ref[...] for ref in outs])
    total = add_bf16(*[ref[...] for ref in feeds[:3]]) + jnp.concatenate(
        [ref[...].astype(jnp.float32) for ref in feeds[3:]], axis=0
    )
    row = 0
    for ref in results[5:]:
        ref[...] = total[row : row + ref.shape[0]]
        row = row + ref.shape[0]


def shards_plain(
    hidden_in,
    positions,
    w_query,
    w_key,
    w_value,
    w_output,
    w_gate,
    w_up,
    w_down,
    norm_scales,
    grad_out,
):
    width = hidden_in.shape[2]
    groups = lax.axis_size("ctx")
    count_dp = lax.axis_size("dp")
    chips = groups // 2
    owners = count_dp * groups
    place = lax.axis_index("ctx")
    row = lax.axis_index("dp")
    resid = hidden_in[0]
    posit = positions[0]
    grad_nat = grad_out[0]
    tokens = resid.shape[0]
    block = tokens // 2
    head_width = w_key.shape[0] * owners
    heads = w_query.shape[0] * owners // head_width
    rows_q, rows_k = w_query.shape[0], w_key.shape[0]
    scale_part = norm_scales.shape[0]

    tie = lax.optimization_barrier
    scale_rows = jnp.zeros((8, width), BF).at[0, :scale_part].set(norm_scales)
    first = gather_over(
        jnp.concatenate([w_query, w_key, w_value, scale_rows], axis=0)[None], swap_z, chips
    )
    rows_f = w_gate.shape[0]
    group_a = jnp.concatenate([w_gate, w_output], axis=0)[None]
    group_b = jnp.concatenate([w_up, w_down], axis=0)[None]
    inverse_in = lax.rsqrt(jnp.mean(resid * resid, axis=-1, keepdims=True) + EPS)
    unit_in = resid * inverse_in
    place_rows = jnp.zeros((8, width), BF)
    place_rows = place_rows.at[0, :tokens].set((posit // 64).astype(BF))
    place_rows = place_rows.at[1, :tokens].set((posit % 64).astype(BF))
    seq_part = jnp.concatenate([unit_in.astype(BF), place_rows], axis=0)[None]
    first, group_a, group_b, seq_part = tie((first, group_a, group_b, seq_part))
    first = gather_over(first[None], swap_dp, count_dp)
    group_a = gather_over(group_a, swap_z, chips)
    group_b = gather_over(group_b, swap_z, chips)
    first, group_a, group_b, seq_part = tie((first, group_a, group_b, seq_part))
    first = first.reshape((owners // 2,) + first.shape[2:])
    group_a = double(group_a, swap_dp, 1)
    group_b = double(group_b, swap_dp, 2)
    seq_z = gather_over(seq_part, swap_z, chips)
    first = jnp.concatenate([first, swap_ctx(first, 1)], axis=0)
    first, group_a, group_b, seq_z = tie((first, group_a, group_b, seq_z))
    seq_all = jnp.concatenate([seq_z, swap_ctx(seq_z, 1)], axis=0)
    group_a = double(group_a, swap_dp, 2)
    group_b = double_inner(group_b, swap_dp, 1)
    far_core, far_dp, far_z = (
        jnp.arange(owners, dtype=jnp.int32) // (owners // 2),
        (jnp.arange(owners, dtype=jnp.int32) // chips) % count_dp,
        jnp.arange(owners, dtype=jnp.int32) % chips,
    )
    owner_of = (row ^ far_dp) * groups + (place ^ (2 * far_z + far_core))
    order_q = row_order(owner_of, rows_q)
    order_k = row_order(owner_of, rows_k)
    order_s = row_order(owner_of, 1)
    full_query = reorder(order_q, first[:, :rows_q].reshape(-1, width))
    full_key = reorder(order_k, first[:, rows_q : rows_q + rows_k].reshape(-1, width))
    full_value = reorder(order_k, first[:, rows_q + rows_k : rows_q + 2 * rows_k].reshape(-1, width))
    full_scales = reorder(order_s, first[:, rows_q + 2 * rows_k, :scale_part]).reshape(-1)
    scale_in, scale_attn, scale_pre, scale_post, scale_query, scale_key = split_scales(
        full_scales, width, head_width
    )

    seq_len = groups * tokens
    seq_core, seq_zed = (
        jnp.arange(groups, dtype=jnp.int32) // chips,
        jnp.arange(groups, dtype=jnp.int32) % chips,
    )
    key_index = natural_rows(place ^ (2 * seq_zed + seq_core), block, groups)
    row_index = natural_rows(place[None], block, groups)
    unit_all = seq_all[:, :tokens].reshape(seq_len, width).astype(jnp.float32)
    pos_all = (
        seq_all[:, tokens, :tokens].astype(jnp.int32) * 64
        + seq_all[:, tokens + 1, :tokens].astype(jnp.int32)
    ).reshape(seq_len)
    normed = (unit_in * (1.0 + scale_in)).astype(BF)
    normed_all = (unit_all * (1.0 + scale_in)).astype(BF)

    query_raw = times_wt(normed, full_query).reshape(tokens, heads, head_width)
    key_raw = times_wt(normed_all, full_key)
    value_bf = times_wt(normed_all, full_value).astype(BF)

    def query_piece(raw, scale):
        return rotate(rms_scale(raw, scale), posit) * head_width ** (-0.5)

    def key_piece(raw, scale):
        return rotate(rms_scale(raw, scale)[:, None, :], pos_all)[:, 0, :]

    query_rot, query_back = jax.vjp(query_piece, query_raw, scale_query)
    key_rot, key_back = jax.vjp(key_piece, key_raw, scale_key)
    query_bf = jnp.swapaxes(query_rot.astype(BF), 0, 1).reshape(heads * tokens, head_width)
    key_bf = key_rot.astype(BF)
    allowed = jnp.tile(key_index[None, :] <= row_index[:, None], (heads, 1))
    scores = jnp.where(allowed, times_wt(query_bf, key_bf), -1e30)
    top = jnp.max(scores, axis=1, keepdims=True)
    lse = top + jnp.log(jnp.sum(jnp.exp(scores - top), axis=1, keepdims=True))
    probs = jnp.exp(scores - lse)
    probs_bf = probs.astype(BF)
    mixed = jnp.dot(probs_bf, value_bf, preferred_element_type=jnp.float32).astype(BF)
    attn_bf = jnp.swapaxes(mixed.reshape(heads, tokens, head_width), 0, 1).reshape(tokens, -1)

    group_a, group_b, attn_bf, probs = lax.optimization_barrier((group_a, group_b, attn_bf, probs))
    halves_a = (group_a, swap_ctx(group_a, 1))
    halves_b = (group_b, swap_ctx(group_b, 1))
    gates = [half[:, :rows_f].reshape(-1, width) for half in halves_a]
    ups = [half[:, :rows_f].reshape(-1, width) for half in halves_b]
    downs = [half[:, rows_f:].reshape(-1, width) for half in halves_b]
    out_held = jnp.concatenate([half[:, rows_f:].reshape(-1, width) for half in halves_a], axis=0)
    full_output = reorder(order_q, out_held)
    projected = jnp.dot(attn_bf, full_output, preferred_element_type=jnp.float32)
    (middle, pre_ffn), mid_back = jax.vjp(mid_piece, resid, projected, scale_attn, scale_pre)
    pre_bf = pre_ffn.astype(BF)
    inners, glu_backs = [], []
    for half_no in range(2):
        inner, glu_back = jax.vjp(
            glu_piece, times_wt(pre_bf, gates[half_no]), times_wt(pre_bf, ups[half_no])
        )
        inners.append(inner.astype(BF))
        glu_backs.append(glu_back)
    ffn = sum(
        jnp.dot(inners[half_no], downs[half_no], preferred_element_type=jnp.float32)
        for half_no in range(2)
    )
    block_out, out_back = jax.vjp(out_piece, middle, ffn, scale_post)
    grad_mid, grad_ffn, grad_scale_post = out_back(grad_nat)
    grad_ffn_bf = grad_ffn.astype(BF)
    grad_pre = 0.0
    downs_grad, gates_grad, ups_grad = [], [], []
    for half_no in range(2):
        grad_gate, grad_upward = glu_backs[half_no](times_wt(grad_ffn_bf, downs[half_no]))
        gate_bf = grad_gate.astype(BF)
        upward_bf = grad_upward.astype(BF)
        grad_pre = grad_pre + (
            jnp.dot(gate_bf, gates[half_no], preferred_element_type=jnp.float32)
            + jnp.dot(upward_bf, ups[half_no], preferred_element_type=jnp.float32)
        )
        downs_grad.append(outer_sum(inners[half_no], grad_ffn_bf).astype(BF))
        gates_grad.append(outer_sum(gate_bf, pre_bf).astype(BF))
        ups_grad.append(outer_sum(upward_bf, pre_bf).astype(BF))
    grads_b = [
        jnp.concatenate(
            [
                ups_grad[half_no].reshape(-1, rows_f, width),
                downs_grad[half_no].reshape(-1, rows_f, width),
            ],
            axis=1,
        )
        for half_no in range(2)
    ]
    grads_b = add_bf16(grads_b[0], swap_ctx(grads_b[1], 1)).astype(BF)
    grad_resid_a, grad_proj, grad_scale_attn, grad_scale_pre = mid_back((grad_mid, grad_pre))
    grad_proj_bf = grad_proj.astype(BF)
    grad_attn_bf = times_wt(grad_proj_bf, full_output).astype(BF)
    out_grad = reorder_back(order_q, outer_sum(attn_bf, grad_proj_bf))
    out_grad = out_grad.reshape(2, -1, rows_q, width)
    grads_a = [
        jnp.concatenate([gates_grad[half_no].reshape(-1, rows_f, width), out_grad[half_no]], axis=1)
        for half_no in range(2)
    ]
    grads_a = add_bf16(grads_a[0], swap_ctx(grads_a[1], 1)).astype(BF)
    grads_a, grads_b, grad_attn_bf, pre_bf = lax.optimization_barrier(
        (grads_a, grads_b, grad_attn_bf, pre_bf)
    )
    grads_a = halve(grads_a, swap_dp, 2)
    grads_b = halve_inner(grads_b, swap_dp, 1)

    grad_rows = jnp.swapaxes(grad_attn_bf.reshape(tokens, heads, head_width), 0, 1).reshape(
        heads * tokens, head_width
    )
    delta = jnp.sum(
        grad_rows.astype(jnp.float32) * mixed.astype(jnp.float32), axis=1, keepdims=True
    )
    grad_scores = (probs * (times_wt(grad_rows, value_bf) - delta)).astype(BF)
    grad_query = jnp.dot(grad_scores, key_bf, preferred_element_type=jnp.float32)
    grad_query = jnp.swapaxes(grad_query.reshape(heads, tokens, head_width), 0, 1)
    grad_key = outer_sum(grad_scores, query_bf)
    grad_value_bf = outer_sum(probs_bf, grad_rows).astype(BF)
    grad_qraw, grad_scale_query = query_back(grad_query)
    grad_kraw, grad_scale_key = key_back(grad_key)
    grad_qraw_bf = grad_qraw.reshape(tokens, heads * head_width).astype(BF)
    grad_kraw_bf = grad_kraw.astype(BF)

    grad_normed_q = jnp.dot(grad_qraw_bf, full_query, preferred_element_type=jnp.float32)
    grad_normed = jnp.dot(grad_kraw_bf, full_key, preferred_element_type=jnp.float32) + jnp.dot(
        grad_value_bf, full_value, preferred_element_type=jnp.float32
    )
    grad_scale_in = jnp.sum(grad_normed * unit_all, axis=0) + jnp.sum(
        grad_normed_q * unit_in, axis=0
    )
    far = grad_normed.astype(BF).reshape(2, chips, tokens, width)
    grad_w_query = reorder_back(order_q, outer_sum(grad_qraw_bf, normed))
    grad_w_key = reorder_back(order_k, outer_sum(grad_kraw_bf, normed_all))
    grad_w_value = reorder_back(order_k, outer_sum(grad_value_bf, normed_all))
    grad_scales = jnp.concatenate(
        [
            grad_scale_in,
            grad_scale_attn,
            grad_scale_pre,
            grad_scale_post,
            grad_scale_query,
            grad_scale_key,
        ]
    ).reshape(owners, scale_part)
    scales_back = reorder_back(order_s, grad_scales)
    packed = jnp.concatenate(
        [
            grad_w_query.reshape(owners, rows_q, width),
            grad_w_key.reshape(owners, rows_k, width),
            grad_w_value.reshape(owners, rows_k, width),
            jnp.zeros((owners, 8, width), BF).at[:, 0, :scale_part].set(scales_back),
        ],
        axis=1,
    ).reshape(2, -1, width)
    far_sum = add_bf16(far[0], swap_ctx(far[1], 1)).astype(BF)
    grads_a, grads_b, packed, far_sum = tie((grads_a, grads_b, packed, far_sum))
    grads_a = halve(grads_a, swap_dp, 1)
    grads_b = halve(grads_b, swap_dp, 2)
    own_normed = scatter_over(far_sum, swap_z, chips) + grad_normed_q
    packed = add_bf16(packed[0], swap_ctx(packed[1], 1)).astype(BF)
    grads_a, grads_b, packed, own_normed = tie((grads_a, grads_b, packed, own_normed))
    own_first = scatter_chip(packed)
    sum_a = scatter_over(grads_a, swap_z, chips)
    sum_b = scatter_over(grads_b, swap_z, chips)
    own_gate, own_output = sum_a[:rows_f], sum_a[rows_f:]
    own_up, own_down = sum_b[:rows_f], sum_b[rows_f:]
    own_query = own_first[:rows_q]
    own_key = own_first[rows_q : rows_q + rows_k]
    own_value = own_first[rows_q + rows_k : rows_q + 2 * rows_k]
    own_scales = own_first[rows_q + 2 * rows_k, :scale_part]
    grad_resid = grad_resid_a + rms_back(unit_in, inverse_in, own_normed * (1.0 + scale_in))
    return (
        block_out[None],
        grad_resid[None],
        own_query,
        own_key,
        own_value,
        own_output,
        own_gate,
        own_up,
        own_down,
        own_scales,
    )


def shards(*args):
    hidden_in, w_query, w_gate = args[0], args[2], args[6]
    fits = hidden_in.shape[1] * lax.axis_size("ctx") <= 2048 and lax.axis_size("ctx") == 8
    fits = fits and lax.axis_size("dp") == 4
    if fits and w_query.shape[0] % 16 == 0 and w_gate.shape[0] % 16 == 0 and args[3].shape[0] == 8:
        return shards_kernels(*args)
    return shards_plain(*args)


def swaps(block, swap):
    return [swap(block, bits) for bits in range(1, 4)]


def shards_kernels(
    hidden_in,
    positions,
    w_query,
    w_key,
    w_value,
    w_output,
    w_gate,
    w_up,
    w_down,
    norm_scales,
    grad_out,
):
    width = hidden_in.shape[2]
    groups = lax.axis_size("ctx")
    count_dp = lax.axis_size("dp")
    chips = groups // 2
    owners = count_dp * groups
    place = lax.axis_index("ctx")
    row = lax.axis_index("dp")
    resid = hidden_in[0]
    posit = positions[0]
    tokens = resid.shape[0]
    block = tokens // 2
    seq_len = groups * tokens
    head_width = w_key.shape[0] * owners
    heads = w_query.shape[0] * owners // head_width
    rows_q, rows_k, rows_f = w_query.shape[0], w_key.shape[0], w_gate.shape[0]
    last = rows_q + 2 * rows_k
    scale_part = norm_scales.shape[0]
    f32 = jnp.float32
    tie = lax.optimization_barrier

    far_core, far_dp, far_z = (
        jnp.arange(owners, dtype=jnp.int32) // (owners // 2),
        (jnp.arange(owners, dtype=jnp.int32) // chips) % count_dp,
        jnp.arange(owners, dtype=jnp.int32) % chips,
    )
    owner_of = (row ^ far_dp) * groups + (place ^ (2 * far_z + far_core))
    order_s = row_order(owner_of, 1)
    held_row = jnp.arange(2 * rows_k * owners, dtype=jnp.int32)
    held_at = (
        (held_row % (2 * rows_k)) // rows_k * head_width
        + jnp.repeat(owner_of, 2 * rows_k) * rows_k
        + held_row % rows_k
    )
    order_kv = (held_row[:, None] == held_at[None, :]).astype(BF)
    seq_core, seq_zed = (
        jnp.arange(groups, dtype=jnp.int32) // chips,
        jnp.arange(groups, dtype=jnp.int32) % chips,
    )
    key_index = natural_rows(place ^ (2 * seq_zed + seq_core), block, groups).reshape(1, seq_len)
    row_index = natural_rows(place[None], block, groups).reshape(tokens, 1)

    last_rows = jnp.concatenate(
        [
            jnp.pad(values[None], ((0, 0), (0, width - values.shape[0])))
            for values in (norm_scales, (posit // 64).astype(BF), (posit % 64).astype(BF))
        ]
        + [jnp.zeros((5, width), BF)],
        axis=0,
    )
    first = jnp.concatenate([w_query, w_key, w_value, last_rows], axis=0)
    feed = jnp.concatenate([w_gate, w_up, w_down], axis=0)
    inverse_in = lax.rsqrt(jnp.mean(resid * resid, axis=-1, keepdims=True) + EPS)
    unit_in = resid * inverse_in
    unit_bf = unit_in.astype(BF)
    first = gather_over(first[None], swap_z, chips)
    first, unit_bf, feed, w_output, order_kv = tie((first, unit_bf, feed, w_output, order_kv))
    last_far = swap_ctx(first[:, last:], 1)
    pos_all = jnp.stack([first[:, last:], last_far], axis=0)[:, :, :, :tokens].astype(f32)
    pos_all = (pos_all[:, :, 1] * 64.0 + pos_all[:, :, 2]).reshape(seq_len)
    half = head_width // 2
    freq_table = 1000000.0 ** (-jnp.arange(half, dtype=jnp.float32) / half)
    angle = pos_all[:, None] * freq_table[None, :]
    cos_all, sine_all = jnp.cos(angle), jnp.sin(angle)
    first = gather_over(first[None], swap_dp, count_dp).reshape((owners // 2,) + first.shape[1:])
    near = gather_over(unit_bf[None], swap_z, chips).reshape(chips * tokens, width)
    first, near, feed, w_output, cos_all, sine_all = tie(
        (first, near, feed, w_output, cos_all, sine_all)
    )
    other = swap_ctx(first, 1)
    far = swap_ctx(near, 1)
    out_own = gather_over(w_output[None], swap_z, chips)
    other, far, out_own, feed = tie((other, far, out_own, feed))
    scale_rows = jnp.concatenate([first[:, last, :scale_part], other[:, last, :scale_part]], axis=0)
    full_scales = reorder(order_s, scale_rows).reshape(-1)
    scale_in, scale_attn, scale_pre, scale_post, scale_query, scale_key = [
        scale[None] for scale in split_scales(full_scales, width, head_width)
    ]
    feed_z2 = swap_z(feed, 2)
    feed_z1 = swap_z(feed, 1)
    out_own = gather_over(out_own[None], swap_dp, count_dp).reshape((owners // 2, rows_q, width))
    (w_q, w_kv, normed, normed_all, query_raw, key_raw, query_bf, key_bf, value_bf, attn_bf, lse) = (
        call_kernel(
            attend_kernel,
            [
                ((heads * head_width, width), BF),
                ((2 * head_width, width), BF),
                ((tokens, width), BF),
                ((seq_len, width), BF),
                ((tokens, heads * head_width), f32),
                ((seq_len, head_width), f32),
                ((tokens, heads * head_width), BF),
                ((seq_len, head_width), BF),
                ((seq_len, head_width), BF),
                ((tokens, heads * head_width), BF),
                ((tokens, heads), f32),
            ],
            [((2 * head_width, width), BF)],
            12_000_000_000,
            (
                unit_in, near, far, first, other, owner_of, order_kv, scale_in, scale_query, scale_key,
                cos_all, sine_all, key_index, row_index,
            ),
            mebibytes=52,
        )
    )
    attn_bf, feed_z1, feed_z2, out_own, feed = tie((attn_bf, feed_z1, feed_z2, out_own, feed))
    out_other = swap_ctx(out_own, 1)
    feed_z3 = swap_z(feed, 3)
    feed_c0 = swap_ctx(feed, 1)
    feed_c1 = swap_ctx(feed_z1, 1)
    feed_c2 = swap_ctx(feed_z2, 1)
    full_output, projected, middle, pre = call_kernel(
        project_kernel,
        [
            ((owners * rows_q, width), BF),
            ((tokens, width), f32),
            ((tokens, width), f32),
            ((tokens, width), BF),
        ],
        [],
        2_000_000_000,
        (attn_bf, owner_of, out_own, out_other, resid, scale_attn, scale_pre),
    )
    pres = swaps(pre, swap_dp)
    pre, pres, feed_z3, feed_c0, feed_c1, feed_c2 = tie((pre, pres, feed_z3, feed_c0, feed_c1, feed_c2))
    feed_c3 = swap_ctx(feed_z3, 1)
    part_shapes = [((tokens, width), f32)] + [((tokens, width), BF)] * 3
    all_tokens = count_dp * tokens
    hidden = groups * rows_f
    outs = call_kernel(
        feed_kernel,
        part_shapes
        + [
            ((all_tokens, hidden), f32),
            ((all_tokens, hidden), f32),
            ((all_tokens, hidden), BF),
            ((all_tokens, width), BF),
        ]
        + [((hidden, width), BF)] * 3,
        [],
        3_000_000_000,
        [pre] + pres + [feed, feed_z1, feed_z2, feed_z3, feed_c0, feed_c1, feed_c2, feed_c3],
    )
    parts, kept = outs[:4], outs[4:]
    comes = [swap_dp(parts[bits], bits) for bits in range(1, 4)]
    block_out, grad_ffn, grad_s_post = call_kernel(
        turning_kernel,
        [((tokens, width), f32), ((tokens, width), BF), ((1, width), f32)],
        [],
        100_000_000,
        [parts[0]] + comes + [middle, grad_out[0], scale_post],
    )
    gate, up, inner, pre_all, w_g, w_u, w_d = kept
    outs = call_kernel(
        feed_back_kernel,
        part_shapes + [((all_tokens, width), BF), ((all_tokens, hidden), BF), ((all_tokens, hidden), BF)],
        [],
        3_000_000_000,
        [grad_ffn] + swaps(grad_ffn, swap_dp) + [gate, up, w_g, w_u, w_d],
    )
    parts, back = outs[:4], outs[4:]
    comes = [swap_dp(parts[bits], bits) for bits in range(1, 4)]
    g_feed, g_feed_far = call_kernel(
        feed_weights_kernel,
        [((chips, 3 * rows_f, width), BF)] * 2,
        [],
        3_000_000_000,
        [inner, pre_all] + list(back),
    )
    g_feed, g_feed_far, comes = tie((g_feed, g_feed_far, comes))
    g_feed = add_bf16(g_feed, swap_ctx(g_feed_far, 1)).astype(BF)
    grad_resid_a, grad_attn, g_out, g_out_far, grad_s_attn, grad_s_pre = call_kernel(
        project_back_kernel,
        [
            ((tokens, width), f32),
            ((tokens, heads * head_width), BF),
            (out_own.shape, BF),
            (out_own.shape, BF),
            ((1, width), f32),
            ((1, width), f32),
        ],
        [((owners * rows_q, width), BF)],
        3_000_000_000,
        [parts[0]]
        + comes
        + [grad_out[0], projected, middle, full_output, attn_bf, owner_of, scale_attn, scale_pre],
    )
    g_out = add_bf16(g_out, swap_ctx(g_out_far, 1)).astype(BF).reshape(count_dp, chips, rows_q, width)
    g_out, g_feed, grad_attn = tie((g_out, g_feed, grad_attn))
    feed_come1 = swap_z(g_feed[1], 1)
    feed_come2 = swap_z(g_feed[2], 2)
    out_comes = [swap_dp(g_out[bits], bits) for bits in range(1, 4)]
    (packed, packed_far, g_near, g_far, grad_normed_q, grad_s_in, grad_s_query, grad_s_key) = call_kernel(
        attend_back_kernel,
        [
            ((owners // 2, last, width), BF),
            ((owners // 2, last, width), BF),
            ((seq_len // 2, 2 * head_width), BF),
            ((seq_len // 2, 2 * head_width), BF),
            ((tokens, width), f32),
            ((1, width), f32),
            ((1, head_width), f32),
            ((1, head_width), f32),
        ],
        [
            ((heads * tokens, seq_len), BF),
            ((heads * tokens, seq_len), BF),
            ((heads * tokens, head_width), BF),
            ((heads * tokens, head_width), BF),
            ((tokens, heads * head_width), BF),
            ((2 * head_width, width), BF),
            ((heads * head_width, width), BF),
        ],
        12_000_000_000,
        (
            grad_attn, attn_bf, query_bf, key_bf, value_bf, lse, query_raw, key_raw, w_q, w_kv,
            scale_query, scale_key, cos_all, sine_all, key_index, row_index, normed, normed_all,
            unit_in, near, far, owner_of, order_kv,
        ),
        mebibytes=36,
    )
    back = (packed, packed_far, g_near, g_far, grad_normed_q, grad_s_in, grad_s_query, grad_s_key)
    back, feed_come1, feed_come2, out_comes, g_out, g_feed = tie(
        (back, feed_come1, feed_come2, out_comes, g_out, g_feed)
    )
    packed, packed_far, g_near, g_far, grad_normed_q, grad_s_in, grad_s_query, grad_s_key = back
    grad_scales = jnp.concatenate(
        [grad_s_in, grad_s_attn, grad_s_pre, grad_s_post, grad_s_query, grad_s_key], axis=1
    ).reshape(owners, scale_part)
    scales_back = reorder_back(order_s, grad_scales)
    scale_sum = add_bf16(scales_back[: owners // 2], swap_ctx(scales_back[owners // 2 :], 1))
    scale_sum = jnp.pad(scale_sum[:, None], ((0, 0), (last, 7), (0, width - scale_part)))
    packed = jnp.pad(add_bf16(packed, swap_ctx(packed_far, 1)), ((0, 0), (0, 8), (0, 0)))
    packed = (packed + scale_sum).astype(BF)
    feed_come3 = swap_z(g_feed[3, : 3 * rows_f // 2], 3)
    far_sum = add_bf16(g_near, swap_ctx(g_far, 1)).astype(BF).reshape(chips, tokens, 2 * head_width)
    out_sum = add_bf16(g_out[0], *out_comes).astype(BF)
    packed, far_sum, out_sum, g_feed, feed_come3 = tie((packed, far_sum, out_sum, g_feed, feed_come3))
    packed = scatter_over(packed.reshape((count_dp, chips) + packed.shape[1:]), swap_dp, count_dp)
    own_kv = scatter_over(far_sum, swap_z, chips).astype(BF)
    packed, own_kv, out_sum, g_feed = tie((packed.astype(BF), own_kv, out_sum, g_feed))
    own_normed = jnp.dot(own_kv, w_kv, preferred_element_type=jnp.float32) + grad_normed_q
    half_rows = 3 * rows_f // 2
    feed_end3 = swap_z(g_feed[3, half_rows:], 3)
    out_comes = [swap_z(out_sum[bits], bits) for bits in range(1, 4)]
    first_comes = [swap_z(packed[bits], bits) for bits in range(1, 4)]
    own_query, own_key, own_value, own_last, own_output, own_gate, own_up, own_down = call_kernel(
        ending_kernel,
        [
            ((rows_q, width), f32),
            ((rows_k, width), f32),
            ((rows_k, width), f32),
            ((8, width), f32),
            ((rows_q, width), f32),
            ((rows_f, width), f32),
            ((rows_f, width), f32),
            ((rows_f, width), f32),
        ],
        [],
        10_000_000,
        [packed[0]]
        + first_comes
        + [out_sum[0]]
        + out_comes
        + [g_feed[0], feed_come1, feed_come2, feed_come3, feed_end3],
    )
    grad_resid = grad_resid_a + rms_back(unit_in, inverse_in, own_normed * (1.0 + scale_in))
    return (
        block_out[None],
        grad_resid[None],
        own_query,
        own_key,
        own_value,
        own_output,
        own_gate,
        own_up,
        own_down,
        own_last[0, :scale_part],
    )


def solution(mesh):
    in_specs = (
        P("dp", "ctx", None),
        P("dp", "ctx"),
        P(("dp", "ctx"), None),
        P(("dp", "ctx"), None),
        P(("dp", "ctx"), None),
        P(("dp", "ctx"), None),
        P(("dp", "ctx"), None),
        P(("dp", "ctx"), None),
        P(("dp", "ctx"), None),
        P(("dp", "ctx")),
        P("dp", "ctx", None),
    )
    out_specs = (
        P("dp", "ctx", None),
        P("dp", "ctx", None),
        P(("dp", "ctx"), None),
        P(("dp", "ctx"), None),
        P(("dp", "ctx"), None),
        P(("dp", "ctx"), None),
        P(("dp", "ctx"), None),
        P(("dp", "ctx"), None),
        P(("dp", "ctx"), None),
        P(("dp", "ctx")),
    )
    return jax.shard_map(shards, mesh=mesh, in_specs=in_specs, out_specs=out_specs, check_vma=False)
```

```python
import jax
import jax.numpy as jnp
from jax import lax
from jax.experimental import pallas as pl
from jax.experimental.pallas import tpu as pltpu
from jax.sharding import PartitionSpec as P

EPS = 1e-06


def rms_scale(vector, scale):
    return (
        vector * lax.rsqrt(jnp.mean(vector * vector, axis=-1, keepdims=True) + EPS) * (1.0 + scale)
    )


def rotate(vector, position):
    half = vector.shape[-1] // 2
    freq_table = 1000000.0 ** (-jnp.arange(half, dtype=jnp.float32) / half)
    angle = position.astype(jnp.float32)[:, None] * freq_table[None, :]
    cosine = jnp.cos(angle)[:, None, :]
    sine = jnp.sin(angle)[:, None, :]
    first = vector[..., :half]
    second = vector[..., half:]
    return jnp.concatenate(
        [first * cosine - second * sine, second * cosine + first * sine], axis=-1
    )


def mid_piece(resid, projected, scale_attn, scale_pre):
    middle = resid + rms_scale(projected, scale_attn)
    return (middle, rms_scale(middle, scale_pre))


def glu_piece(gate, upward):
    return jax.nn.gelu(gate, approximate=True) * upward


def out_piece(middle, ffn, scale_post):
    return middle + rms_scale(ffn, scale_post)


def times_wt(left, weight):
    return lax.dot_general(
        left, weight, (((1,), (1,)), ((), ())), preferred_element_type=jnp.float32
    )


def outer_sum(left, right):
    return lax.dot_general(
        left, right, (((0,), (0,)), ((), ())), preferred_element_type=jnp.float32
    )


def split_scales(norm_scales, width, head_width):
    scales = norm_scales.astype(jnp.float32)
    pieces = [scales[index * width : (index + 1) * width] for index in range(4)]
    offset = 4 * width
    return pieces + [
        scales[offset : offset + head_width],
        scales[offset + head_width : offset + 2 * head_width],
    ]


BF = jnp.bfloat16


def swap_dp(block, bits):
    count = lax.axis_size("dp")
    return lax.ppermute(block, "dp", [(place, place ^ bits) for place in range(count)])


def swap_ctx(block, bits):
    count = lax.axis_size("ctx")
    return lax.ppermute(block, "ctx", [(place, place ^ bits) for place in range(count)])


def swap_z(block, bits):
    return swap_ctx(block, 2 * bits)


def gather_over(block, swap, count):
    if count <= 4:
        return jnp.concatenate([block] + [swap(block, bits) for bits in range(1, count)], axis=0)
    bits = 1
    while bits < count:
        block = jnp.concatenate([block, swap(block, bits)], axis=0)
        bits = 2 * bits
    return block


def add_bf16(first, *others):
    total = first.astype(jnp.float32)
    for other in others:
        total = total + other.astype(jnp.float32)
    return total


def scatter_over(blocks, swap, count):
    if count <= 4:
        return add_bf16(blocks[0], *[swap(blocks[bits], bits) for bits in range(1, count)])
    bits = count // 2
    while bits > 1:
        blocks = add_bf16(blocks[:bits], swap(blocks[bits:], bits)).astype(BF)
        bits = bits // 2
    return add_bf16(blocks[0], swap(blocks[1], 1))


def gather_chip(block):
    groups = lax.axis_size("ctx") // 2
    over_z = gather_over(block[None], swap_z, groups)
    over_dp = gather_over(over_z[None], swap_dp, lax.axis_size("dp"))
    return over_dp.reshape((-1,) + block.shape[1:])


def double(blocks, swap, bits):
    return jnp.concatenate([blocks, swap(blocks, bits)], axis=0)


def double_inner(blocks, swap, bits):
    pair = blocks.reshape((2, 1, -1) + blocks.shape[1:])
    return jnp.concatenate([pair, swap(pair, bits)], axis=1).reshape((-1,) + blocks.shape[1:])


def halve(blocks, swap, bits):
    half = blocks.shape[0] // 2
    return add_bf16(blocks[:half], swap(blocks[half:], bits)).astype(BF)


def halve_inner(blocks, swap, bits):
    quarters = blocks.reshape((2, 2, -1) + blocks.shape[1:])
    half = add_bf16(quarters[:, 0], swap(quarters[:, 1], bits)).astype(BF)
    return half.reshape((-1,) + blocks.shape[1:])


def scatter_chip(blocks):
    groups = lax.axis_size("ctx") // 2
    count = lax.axis_size("dp")
    shaped = blocks.reshape((count, groups, -1) + blocks.shape[1:])
    mid = scatter_over(shaped, swap_dp, count).astype(BF)
    return scatter_over(mid, swap_z, groups)


def scatter_all(first, second):
    return scatter_chip(add_bf16(first, swap_ctx(second, 1)).astype(BF))


def natural_rows(places, block, groups):
    within = jnp.arange(2 * block, dtype=jnp.int32)[None, :]
    early = places[:, None] * block + within
    late = (2 * groups - 1 - places[:, None]) * block + within - block
    return jnp.where(within < block, early, late).reshape(-1)


def row_order(owner_of, rows):
    count = owner_of.shape[0] * rows
    held = (owner_of[:, None] * rows + jnp.arange(rows, dtype=jnp.int32)[None, :]).reshape(1, count)
    return (jnp.arange(count, dtype=jnp.int32)[:, None] == held).astype(BF)


def reorder(order, blocks):
    return jnp.dot(order, blocks, preferred_element_type=jnp.float32).astype(BF)


def reorder_back(order, blocks):
    return outer_sum(order, blocks.astype(BF)).astype(BF)


def rms_back(unit, inverse, grad_scaled):
    return inverse * (grad_scaled - unit * jnp.mean(grad_scaled * unit, axis=-1, keepdims=True))


def dot_nt(left, right):
    return lax.dot_general(left, right, (((1,), (1,)), ((), ())), preferred_element_type=jnp.float32)


def dot_nn(left, right):
    return lax.dot_general(left, right, (((1,), (0,)), ((), ())), preferred_element_type=jnp.float32)


def dot_tn(left, right):
    return lax.dot_general(left, right, (((0,), (0,)), ((), ())), preferred_element_type=jnp.float32)


def unit_of(rows):
    inverse = lax.rsqrt(jnp.mean(rows * rows, axis=-1, keepdims=True) + EPS)
    return rows * inverse, inverse


def turn(rows, cosine, sine):
    half = rows.shape[1] // 2
    first, second = rows[:, :half], rows[:, half:]
    return jnp.concatenate([first * cosine - second * sine, second * cosine + first * sine], axis=1)


def turn_back(rows, cosine, sine):
    half = rows.shape[1] // 2
    first, second = rows[:, :half], rows[:, half:]
    return jnp.concatenate([first * cosine + second * sine, second * cosine - first * sine], axis=1)


def call_kernel(body, out_shapes, scratch, flops, inputs, mebibytes=24):
    whole = pl.BlockSpec(memory_space=pltpu.VMEM)
    return pl.pallas_call(
        body,
        out_shape=[jax.ShapeDtypeStruct(shape, dtype) for shape, dtype in out_shapes],
        in_specs=[
            pl.BlockSpec(memory_space=pltpu.SMEM) if entry.ndim == 1 else whole for entry in inputs
        ],
        out_specs=[whole] * len(out_shapes),
        scratch_shapes=[pltpu.VMEM(shape, dtype) for shape, dtype in scratch],
        compiler_params=pltpu.CompilerParams(vmem_limit_bytes=mebibytes * 1024 * 1024),
        cost_estimate=pl.CostEstimate(flops=flops, bytes_accessed=20_000_000, transcendentals=0),
    )(*inputs)


def owner_rows(owner_ref, entry, rows):
    return pl.ds(pl.multiple_of(owner_ref[entry] * rows, rows), rows)


def attend_kernel(
    unit_ref, near_ref, far_ref, own_ref, other_ref, owner_ref, order_kv_ref, sin_scale_ref, sq_ref,
    sk_ref, cos_all_ref, sine_all_ref, key_index_ref, row_index_ref,
    wq_ref, wkv_ref, normed_ref, normed_all_ref, qraw_ref, kraw_ref, q_ref, k_ref, v_ref, attn_ref, lse_ref,
    held_kv,
):
    places, _, width = own_ref.shape
    rows_q = wq_ref.shape[0] // (2 * places)
    rows_kv = held_kv.shape[0] // (2 * places)
    for core, ref in enumerate((own_ref, other_ref)):
        for at in range(places):
            wq_ref[owner_rows(owner_ref, core * places + at, rows_q), :] = ref[at, :rows_q, :]
        held_kv[core * places * rows_kv : (core + 1) * places * rows_kv, :] = ref[
            :, rows_q : rows_q + rows_kv, :
        ].reshape(places * rows_kv, width)
    wkv_ref[...] = dot_nn(order_kv_ref[...], held_kv[...]).astype(BF)
    tokens = unit_ref.shape[0]
    scale_in = 1.0 + sin_scale_ref[...]
    normed_ref[...] = (unit_ref[...] * scale_in).astype(BF)
    half = near_ref.shape[0]
    normed_all_ref[:half] = (near_ref[...].astype(jnp.float32) * scale_in).astype(BF)
    normed_all_ref[half:] = (far_ref[...].astype(jnp.float32) * scale_in).astype(BF)
    head_width = sq_ref.shape[1]
    heads = wq_ref.shape[0] // head_width
    key_raw = dot_nt(normed_all_ref[...], wkv_ref[:head_width, :])
    kraw_ref[...] = key_raw
    v_ref[...] = dot_nt(normed_all_ref[...], wkv_ref[head_width:, :]).astype(BF)
    key_unit, _ = unit_of(key_raw)
    k_ref[...] = turn(key_unit * (1.0 + sk_ref[...]), cos_all_ref[...], sine_all_ref[...]).astype(BF)
    allowed = key_index_ref[...] <= row_index_ref[...]
    cosine, sine = cos_all_ref[:tokens, :], sine_all_ref[:tokens, :]
    for head in range(heads):
        span = slice(head * head_width, (head + 1) * head_width)
        raw = dot_nt(normed_ref[...], wq_ref[span, :])
        qraw_ref[:, span] = raw
        unit, _ = unit_of(raw)
        turned = turn(unit * (1.0 + sq_ref[...]), cosine, sine)
        query = (turned * head_width ** (-0.5)).astype(BF)
        q_ref[:, span] = query
        scores = jnp.where(allowed, dot_nt(query, k_ref[...]), -1e30)
        top = jnp.max(scores, axis=1, keepdims=True)
        lse = top + jnp.log(jnp.sum(jnp.exp(scores - top), axis=1, keepdims=True))
        lse_ref[:, head : head + 1] = lse
        probs = jnp.exp(scores - lse).astype(BF)
        attn_ref[:, span] = dot_nn(probs, v_ref[...]).astype(BF)


def project_kernel(
    attn_ref, owner_ref, own_ref, other_ref, resid_ref, sattn_ref, spre_ref,
    wo_ref, projected_ref, middle_ref, pre_ref,
):
    places, rows, _ = own_ref.shape
    for core, ref in enumerate((own_ref, other_ref)):
        for at in range(places):
            wo_ref[owner_rows(owner_ref, core * places + at, rows), :] = ref[at]
    projected = dot_nn(attn_ref[...], wo_ref[...])
    projected_ref[...] = projected
    unit, _ = unit_of(projected)
    middle = resid_ref[...] + unit * (1.0 + sattn_ref[...])
    middle_ref[...] = middle
    unit, _ = unit_of(middle)
    pre_ref[...] = (unit * (1.0 + spre_ref[...])).astype(BF)


GELU_A = (2.0 / 3.141592653589793) ** 0.5


def feed_kernel(*refs):
    pres, weights = refs[:4], refs[4:12]
    part_refs = refs[12:16]
    gate_ref, up_ref, inner_ref, pre_ref, wg_ref, wu_ref, wd_ref = refs[16:]
    tokens = pres[0].shape[0]
    rows = weights[0].shape[0] // 3
    for number, ref in enumerate(pres):
        pre_ref[number * tokens : (number + 1) * tokens, :] = ref[...]
    for number, ref in enumerate(weights):
        span = slice(number * rows, (number + 1) * rows)
        wg_ref[span, :] = ref[:rows, :]
        wu_ref[span, :] = ref[rows : 2 * rows, :]
        wd_ref[span, :] = ref[2 * rows :, :]
    for number in range(4):
        at = slice(number * tokens, (number + 1) * tokens)
        gate = dot_nt(pre_ref[at, :], wg_ref[...])
        up = dot_nt(pre_ref[at, :], wu_ref[...])
        gate_ref[at, :] = gate
        up_ref[at, :] = up
        bent = jnp.tanh(GELU_A * (gate + 0.044715 * (gate * gate * gate)))
        inner = (0.5 * gate * (1.0 + bent) * up).astype(BF)
        inner_ref[at, :] = inner
        part_refs[number][...] = dot_nn(inner, wd_ref[...]).astype(part_refs[number].dtype)


def turning_kernel(
    own_ref, come1_ref, come2_ref, come3_ref, middle_ref, gout_ref, spost_ref,
    block_out_ref, gffn_ref, gspost_ref,
):
    ffn = own_ref[...]
    for ref in (come1_ref, come2_ref, come3_ref):
        ffn = ffn + ref[...].astype(jnp.float32)
    unit, inverse = unit_of(ffn)
    grad_out = gout_ref[...]
    block_out_ref[...] = middle_ref[...] + unit * (1.0 + spost_ref[...])
    gspost_ref[...] = jnp.sum(grad_out * unit, axis=0, keepdims=True)
    gffn_ref[...] = rms_back(unit, inverse, grad_out * (1.0 + spost_ref[...])).astype(BF)


def feed_back_kernel(*refs):
    grads = refs[:4]
    gate_ref, up_ref, wg_ref, wu_ref, wd_ref = refs[4:9]
    part_refs = refs[9:13]
    gffn_ref, ggate_ref, gup_ref = refs[13:]
    tokens = grads[0].shape[0]
    for number, ref in enumerate(grads):
        at = slice(number * tokens, (number + 1) * tokens)
        gffn_ref[at, :] = ref[...]
        grad_inner = dot_nt(ref[...], wd_ref[...])
        gate = gate_ref[at, :]
        square = gate * gate
        bent = jnp.tanh(GELU_A * (gate + 0.044715 * (square * gate)))
        curve = 0.5 * gate * (1.0 + bent)
        slope = 0.5 * (1.0 + bent) + 0.5 * gate * (1.0 - bent * bent) * (
            GELU_A * (1.0 + 3.0 * 0.044715 * square)
        )
        grad_up = (grad_inner * curve).astype(BF)
        grad_gate = (grad_inner * up_ref[at, :] * slope).astype(BF)
        ggate_ref[at, :] = grad_gate
        gup_ref[at, :] = grad_up
        part_refs[number][...] = (dot_nn(grad_gate, wg_ref[...]) + dot_nn(grad_up, wu_ref[...])).astype(
            part_refs[number].dtype
        )


def feed_weights_kernel(inner_ref, pre_ref, gffn_ref, ggate_ref, gup_ref, own_ref, other_ref):
    places, rows, width = own_ref.shape
    rows = rows // 3
    shape = (places, rows, width)
    for core, ref in enumerate((own_ref, other_ref)):
        span = slice(core * places * rows, (core + 1) * places * rows)
        ref[:, :rows, :] = dot_tn(ggate_ref[:, span], pre_ref[...]).astype(BF).reshape(shape)
        ref[:, rows : 2 * rows, :] = dot_tn(gup_ref[:, span], pre_ref[...]).astype(BF).reshape(shape)
        ref[:, 2 * rows :, :] = dot_tn(inner_ref[:, span], gffn_ref[...]).astype(BF).reshape(shape)


def project_back_kernel(
    own_ref, come1_ref, come2_ref, come3_ref, gout_ref, projected_ref, middle_ref, wo_ref, attn_ref,
    owner_ref, sattn_ref, spre_ref,
    gresid_ref, gattn_ref, gown_ref, gother_ref, gsattn_ref, gspre_ref,
    gwo_scr,
):
    grad_pre = own_ref[...]
    for ref in (come1_ref, come2_ref, come3_ref):
        grad_pre = grad_pre + ref[...].astype(jnp.float32)
    unit_p, inverse_p = unit_of(middle_ref[...])
    unit_a, inverse_a = unit_of(projected_ref[...])
    gspre_ref[...] = jnp.sum(grad_pre * unit_p, axis=0, keepdims=True)
    grad_middle = gout_ref[...] + rms_back(unit_p, inverse_p, grad_pre * (1.0 + spre_ref[...]))
    gresid_ref[...] = grad_middle
    gsattn_ref[...] = jnp.sum(grad_middle * unit_a, axis=0, keepdims=True)
    grad_proj = rms_back(unit_a, inverse_a, grad_middle * (1.0 + sattn_ref[...])).astype(BF)
    gattn_ref[...] = dot_nt(grad_proj, wo_ref[...]).astype(BF)
    gwo_scr[...] = dot_tn(attn_ref[...], grad_proj).astype(BF)
    places, rows, _ = gown_ref.shape
    for core, ref in enumerate((gown_ref, gother_ref)):
        for at in range(places):
            ref[at] = gwo_scr[owner_rows(owner_ref, core * places + at, rows), :]


def attend_back_kernel(
    grad_attn_ref, attn_ref, q_ref, k_ref, v_ref, lse_ref, qraw_ref, kraw_ref, wq_ref, wkv_ref,
    sq_ref, sk_ref, cos_all_ref, sine_all_ref, key_index_ref, row_index_ref,
    normed_ref, normed_all_ref, unit_ref, near_ref, far_ref, owner_ref, order_kv_ref,
    own_ref, other_ref, gnear_ref, gfar_ref, gq_ref, gsin_ref, gsq_ref, gsk_ref,
    probs_scr, gscores_scr, grows_scr, qrows_scr, gqraw_scr, gkv_scr, gwq_scr,
):
    head_width = sq_ref.shape[1]
    heads = wq_ref.shape[0] // head_width
    tokens = q_ref.shape[0]
    cosine, sine = cos_all_ref[:tokens, :], sine_all_ref[:tokens, :]
    allowed = key_index_ref[...] <= row_index_ref[...]
    grad_sq = jnp.zeros((1, head_width), jnp.float32)
    for head in range(heads):
        span = slice(head * head_width, (head + 1) * head_width)
        rows = slice(head * tokens, (head + 1) * tokens)
        query = q_ref[:, span]
        grad_rows = grad_attn_ref[:, span]
        delta = jnp.sum(
            grad_rows.astype(jnp.float32) * attn_ref[:, span].astype(jnp.float32),
            axis=1,
            keepdims=True,
        )
        scores = jnp.where(allowed, dot_nt(query, k_ref[...]), -1e30)
        probs = jnp.exp(scores - lse_ref[:, head : head + 1])
        grad_scores = (probs * (dot_nt(grad_rows, v_ref[...]) - delta)).astype(BF)
        probs_scr[rows, :] = probs.astype(BF)
        gscores_scr[rows, :] = grad_scores
        grows_scr[rows, :] = grad_rows
        qrows_scr[rows, :] = query
        grad_query = dot_nn(grad_scores, k_ref[...]) * head_width ** (-0.5)
        grad_query = turn_back(grad_query, cosine, sine)
        unit, inverse = unit_of(qraw_ref[:, span])
        grad_sq = grad_sq + jnp.sum(grad_query * unit, axis=0, keepdims=True)
        grad_raw = rms_back(unit, inverse, grad_query * (1.0 + sq_ref[...]))
        gqraw_scr[:, span] = grad_raw.astype(BF)
    gsq_ref[...] = grad_sq
    grad_key = dot_tn(gscores_scr[...], qrows_scr[...])
    grad_value = dot_tn(probs_scr[...], grows_scr[...]).astype(BF)
    grad_key = turn_back(grad_key, cos_all_ref[...], sine_all_ref[...])
    unit, inverse = unit_of(kraw_ref[...])
    gsk_ref[...] = jnp.sum(grad_key * unit, axis=0, keepdims=True)
    grad_kraw = rms_back(unit, inverse, grad_key * (1.0 + sk_ref[...])).astype(BF)
    half = near_ref.shape[0]
    grad_normed = dot_nn(grad_kraw, wkv_ref[:head_width, :]) + dot_nn(
        grad_value, wkv_ref[head_width:, :]
    )
    grad_q = dot_nn(gqraw_scr[...], wq_ref[...])
    gq_ref[...] = grad_q
    gsin_ref[...] = (
        jnp.sum(grad_normed[:half] * near_ref[...].astype(jnp.float32), axis=0, keepdims=True)
        + jnp.sum(grad_normed[half:] * far_ref[...].astype(jnp.float32), axis=0, keepdims=True)
        + jnp.sum(grad_q * unit_ref[...], axis=0, keepdims=True)
    )
    gnear_ref[:, :head_width] = grad_kraw[:half]
    gnear_ref[:, head_width:] = grad_value[:half]
    gfar_ref[:, :head_width] = grad_kraw[half:]
    gfar_ref[:, head_width:] = grad_value[half:]
    gkv_scr[:head_width, :] = dot_tn(grad_kraw, normed_all_ref[...]).astype(BF)
    gkv_scr[head_width:, :] = dot_tn(grad_value, normed_all_ref[...]).astype(BF)
    gwq_scr[...] = dot_tn(gqraw_scr[...], normed_ref[...]).astype(BF)
    held_kv = dot_tn(order_kv_ref[...], gkv_scr[...]).astype(BF)
    places, _, width = own_ref.shape
    rows_q = gwq_scr.shape[0] // (2 * places)
    rows_kv = held_kv.shape[0] // (2 * places)
    for core, ref in enumerate((own_ref, other_ref)):
        for at in range(places):
            ref[at, :rows_q, :] = gwq_scr[owner_rows(owner_ref, core * places + at, rows_q), :]
        ref[:, rows_q : rows_q + rows_kv, :] = held_kv[
            core * places * rows_kv : (core + 1) * places * rows_kv
        ].reshape(places, rows_kv, width)


def ending_kernel(*refs):
    first_ref, out_ref = refs[:2]
    comes = [ref[...].astype(jnp.float32) for ref in refs[2:5]]
    feeds, results = refs[5:9], refs[9:]
    rows_q = out_ref.shape[0]
    rows = rows_q + first_ref.shape[0]
    total = first_ref[...].astype(jnp.float32)
    for come in comes:
        total = total + come[rows_q:rows]
    row = 0
    for ref in results[:4]:
        ref[...] = total[row : row + ref.shape[0]]
        row = row + ref.shape[0]
    total = out_ref[...].astype(jnp.float32)
    for come in comes:
        total = total + come[:rows_q]
    results[4][...] = total
    total = add_bf16(*[ref[...] for ref in feeds[:3]]) + jnp.concatenate(
        [feeds[3][...].astype(jnp.float32), comes[2][rows:]], axis=0
    )
    row = 0
    for ref in results[5:]:
        ref[...] = total[row : row + ref.shape[0]]
        row = row + ref.shape[0]


def shards_plain(
    hidden_in,
    positions,
    w_query,
    w_key,
    w_value,
    w_output,
    w_gate,
    w_up,
    w_down,
    norm_scales,
    grad_out,
):
    width = hidden_in.shape[2]
    groups = lax.axis_size("ctx")
    count_dp = lax.axis_size("dp")
    chips = groups // 2
    owners = count_dp * groups
    place = lax.axis_index("ctx")
    row = lax.axis_index("dp")
    resid = hidden_in[0]
    posit = positions[0]
    grad_nat = grad_out[0]
    tokens = resid.shape[0]
    block = tokens // 2
    head_width = w_key.shape[0] * owners
    heads = w_query.shape[0] * owners // head_width
    rows_q, rows_k = w_query.shape[0], w_key.shape[0]
    scale_part = norm_scales.shape[0]

    tie = lax.optimization_barrier
    scale_rows = jnp.zeros((8, width), BF).at[0, :scale_part].set(norm_scales)
    first = gather_over(
        jnp.concatenate([w_query, w_key, w_value, scale_rows], axis=0)[None], swap_z, chips
    )
    rows_f = w_gate.shape[0]
    group_a = jnp.concatenate([w_gate, w_output], axis=0)[None]
    group_b = jnp.concatenate([w_up, w_down], axis=0)[None]
    inverse_in = lax.rsqrt(jnp.mean(resid * resid, axis=-1, keepdims=True) + EPS)
    unit_in = resid * inverse_in
    place_rows = jnp.zeros((8, width), BF)
    place_rows = place_rows.at[0, :tokens].set((posit // 64).astype(BF))
    place_rows = place_rows.at[1, :tokens].set((posit % 64).astype(BF))
    seq_part = jnp.concatenate([unit_in.astype(BF), place_rows], axis=0)[None]
    first, group_a, group_b, seq_part = tie((first, group_a, group_b, seq_part))
    first = gather_over(first[None], swap_dp, count_dp)
    group_a = gather_over(group_a, swap_z, chips)
    group_b = gather_over(group_b, swap_z, chips)
    first, group_a, group_b, seq_part = tie((first, group_a, group_b, seq_part))
    first = first.reshape((owners // 2,) + first.shape[2:])
    group_a = double(group_a, swap_dp, 1)
    group_b = double(group_b, swap_dp, 2)
    seq_z = gather_over(seq_part, swap_z, chips)
    first = jnp.concatenate([first, swap_ctx(first, 1)], axis=0)
    first, group_a, group_b, seq_z = tie((first, group_a, group_b, seq_z))
    seq_all = jnp.concatenate([seq_z, swap_ctx(seq_z, 1)], axis=0)
    group_a = double(group_a, swap_dp, 2)
    group_b = double_inner(group_b, swap_dp, 1)
    far_core, far_dp, far_z = (
        jnp.arange(owners, dtype=jnp.int32) // (owners // 2),
        (jnp.arange(owners, dtype=jnp.int32) // chips) % count_dp,
        jnp.arange(owners, dtype=jnp.int32) % chips,
    )
    owner_of = (row ^ far_dp) * groups + (place ^ (2 * far_z + far_core))
    order_q = row_order(owner_of, rows_q)
    order_k = row_order(owner_of, rows_k)
    order_s = row_order(owner_of, 1)
    full_query = reorder(order_q, first[:, :rows_q].reshape(-1, width))
    full_key = reorder(order_k, first[:, rows_q : rows_q + rows_k].reshape(-1, width))
    full_value = reorder(order_k, first[:, rows_q + rows_k : rows_q + 2 * rows_k].reshape(-1, width))
    full_scales = reorder(order_s, first[:, rows_q + 2 * rows_k, :scale_part]).reshape(-1)
    scale_in, scale_attn, scale_pre, scale_post, scale_query, scale_key = split_scales(
        full_scales, width, head_width
    )

    seq_len = groups * tokens
    seq_core, seq_zed = (
        jnp.arange(groups, dtype=jnp.int32) // chips,
        jnp.arange(groups, dtype=jnp.int32) % chips,
    )
    key_index = natural_rows(place ^ (2 * seq_zed + seq_core), block, groups)
    row_index = natural_rows(place[None], block, groups)
    unit_all = seq_all[:, :tokens].reshape(seq_len, width).astype(jnp.float32)
    pos_all = (
        seq_all[:, tokens, :tokens].astype(jnp.int32) * 64
        + seq_all[:, tokens + 1, :tokens].astype(jnp.int32)
    ).reshape(seq_len)
    normed = (unit_in * (1.0 + scale_in)).astype(BF)
    normed_all = (unit_all * (1.0 + scale_in)).astype(BF)

    query_raw = times_wt(normed, full_query).reshape(tokens, heads, head_width)
    key_raw = times_wt(normed_all, full_key)
    value_bf = times_wt(normed_all, full_value).astype(BF)

    def query_piece(raw, scale):
        return rotate(rms_scale(raw, scale), posit) * head_width ** (-0.5)

    def key_piece(raw, scale):
        return rotate(rms_scale(raw, scale)[:, None, :], pos_all)[:, 0, :]

    query_rot, query_back = jax.vjp(query_piece, query_raw, scale_query)
    key_rot, key_back = jax.vjp(key_piece, key_raw, scale_key)
    query_bf = jnp.swapaxes(query_rot.astype(BF), 0, 1).reshape(heads * tokens, head_width)
    key_bf = key_rot.astype(BF)
    allowed = jnp.tile(key_index[None, :] <= row_index[:, None], (heads, 1))
    scores = jnp.where(allowed, times_wt(query_bf, key_bf), -1e30)
    top = jnp.max(scores, axis=1, keepdims=True)
    lse = top + jnp.log(jnp.sum(jnp.exp(scores - top), axis=1, keepdims=True))
    probs = jnp.exp(scores - lse)
    probs_bf = probs.astype(BF)
    mixed = jnp.dot(probs_bf, value_bf, preferred_element_type=jnp.float32).astype(BF)
    attn_bf = jnp.swapaxes(mixed.reshape(heads, tokens, head_width), 0, 1).reshape(tokens, -1)

    group_a, group_b, attn_bf, probs = lax.optimization_barrier((group_a, group_b, attn_bf, probs))
    halves_a = (group_a, swap_ctx(group_a, 1))
    halves_b = (group_b, swap_ctx(group_b, 1))
    gates = [half[:, :rows_f].reshape(-1, width) for half in halves_a]
    ups = [half[:, :rows_f].reshape(-1, width) for half in halves_b]
    downs = [half[:, rows_f:].reshape(-1, width) for half in halves_b]
    out_held = jnp.concatenate([half[:, rows_f:].reshape(-1, width) for half in halves_a], axis=0)
    full_output = reorder(order_q, out_held)
    projected = jnp.dot(attn_bf, full_output, preferred_element_type=jnp.float32)
    (middle, pre_ffn), mid_back = jax.vjp(mid_piece, resid, projected, scale_attn, scale_pre)
    pre_bf = pre_ffn.astype(BF)
    inners, glu_backs = [], []
    for half_no in range(2):
        inner, glu_back = jax.vjp(
            glu_piece, times_wt(pre_bf, gates[half_no]), times_wt(pre_bf, ups[half_no])
        )
        inners.append(inner.astype(BF))
        glu_backs.append(glu_back)
    ffn = sum(
        jnp.dot(inners[half_no], downs[half_no], preferred_element_type=jnp.float32)
        for half_no in range(2)
    )
    block_out, out_back = jax.vjp(out_piece, middle, ffn, scale_post)
    grad_mid, grad_ffn, grad_scale_post = out_back(grad_nat)
    grad_ffn_bf = grad_ffn.astype(BF)
    grad_pre = 0.0
    downs_grad, gates_grad, ups_grad = [], [], []
    for half_no in range(2):
        grad_gate, grad_upward = glu_backs[half_no](times_wt(grad_ffn_bf, downs[half_no]))
        gate_bf = grad_gate.astype(BF)
        upward_bf = grad_upward.astype(BF)
        grad_pre = grad_pre + (
            jnp.dot(gate_bf, gates[half_no], preferred_element_type=jnp.float32)
            + jnp.dot(upward_bf, ups[half_no], preferred_element_type=jnp.float32)
        )
        downs_grad.append(outer_sum(inners[half_no], grad_ffn_bf).astype(BF))
        gates_grad.append(outer_sum(gate_bf, pre_bf).astype(BF))
        ups_grad.append(outer_sum(upward_bf, pre_bf).astype(BF))
    grads_b = [
        jnp.concatenate(
            [
                ups_grad[half_no].reshape(-1, rows_f, width),
                downs_grad[half_no].reshape(-1, rows_f, width),
            ],
            axis=1,
        )
        for half_no in range(2)
    ]
    grads_b = add_bf16(grads_b[0], swap_ctx(grads_b[1], 1)).astype(BF)
    grad_resid_a, grad_proj, grad_scale_attn, grad_scale_pre = mid_back((grad_mid, grad_pre))
    grad_proj_bf = grad_proj.astype(BF)
    grad_attn_bf = times_wt(grad_proj_bf, full_output).astype(BF)
    out_grad = reorder_back(order_q, outer_sum(attn_bf, grad_proj_bf))
    out_grad = out_grad.reshape(2, -1, rows_q, width)
    grads_a = [
        jnp.concatenate([gates_grad[half_no].reshape(-1, rows_f, width), out_grad[half_no]], axis=1)
        for half_no in range(2)
    ]
    grads_a = add_bf16(grads_a[0], swap_ctx(grads_a[1], 1)).astype(BF)
    grads_a, grads_b, grad_attn_bf, pre_bf = lax.optimization_barrier(
        (grads_a, grads_b, grad_attn_bf, pre_bf)
    )
    grads_a = halve(grads_a, swap_dp, 2)
    grads_b = halve_inner(grads_b, swap_dp, 1)

    grad_rows = jnp.swapaxes(grad_attn_bf.reshape(tokens, heads, head_width), 0, 1).reshape(
        heads * tokens, head_width
    )
    delta = jnp.sum(
        grad_rows.astype(jnp.float32) * mixed.astype(jnp.float32), axis=1, keepdims=True
    )
    grad_scores = (probs * (times_wt(grad_rows, value_bf) - delta)).astype(BF)
    grad_query = jnp.dot(grad_scores, key_bf, preferred_element_type=jnp.float32)
    grad_query = jnp.swapaxes(grad_query.reshape(heads, tokens, head_width), 0, 1)
    grad_key = outer_sum(grad_scores, query_bf)
    grad_value_bf = outer_sum(probs_bf, grad_rows).astype(BF)
    grad_qraw, grad_scale_query = query_back(grad_query)
    grad_kraw, grad_scale_key = key_back(grad_key)
    grad_qraw_bf = grad_qraw.reshape(tokens, heads * head_width).astype(BF)
    grad_kraw_bf = grad_kraw.astype(BF)

    grad_normed_q = jnp.dot(grad_qraw_bf, full_query, preferred_element_type=jnp.float32)
    grad_normed = jnp.dot(grad_kraw_bf, full_key, preferred_element_type=jnp.float32) + jnp.dot(
        grad_value_bf, full_value, preferred_element_type=jnp.float32
    )
    grad_scale_in = jnp.sum(grad_normed * unit_all, axis=0) + jnp.sum(
        grad_normed_q * unit_in, axis=0
    )
    far = grad_normed.astype(BF).reshape(2, chips, tokens, width)
    grad_w_query = reorder_back(order_q, outer_sum(grad_qraw_bf, normed))
    grad_w_key = reorder_back(order_k, outer_sum(grad_kraw_bf, normed_all))
    grad_w_value = reorder_back(order_k, outer_sum(grad_value_bf, normed_all))
    grad_scales = jnp.concatenate(
        [
            grad_scale_in,
            grad_scale_attn,
            grad_scale_pre,
            grad_scale_post,
            grad_scale_query,
            grad_scale_key,
        ]
    ).reshape(owners, scale_part)
    scales_back = reorder_back(order_s, grad_scales)
    packed = jnp.concatenate(
        [
            grad_w_query.reshape(owners, rows_q, width),
            grad_w_key.reshape(owners, rows_k, width),
            grad_w_value.reshape(owners, rows_k, width),
            jnp.zeros((owners, 8, width), BF).at[:, 0, :scale_part].set(scales_back),
        ],
        axis=1,
    ).reshape(2, -1, width)
    far_sum = add_bf16(far[0], swap_ctx(far[1], 1)).astype(BF)
    grads_a, grads_b, packed, far_sum = tie((grads_a, grads_b, packed, far_sum))
    grads_a = halve(grads_a, swap_dp, 1)
    grads_b = halve(grads_b, swap_dp, 2)
    own_normed = scatter_over(far_sum, swap_z, chips) + grad_normed_q
    packed = add_bf16(packed[0], swap_ctx(packed[1], 1)).astype(BF)
    grads_a, grads_b, packed, own_normed = tie((grads_a, grads_b, packed, own_normed))
    own_first = scatter_chip(packed)
    sum_a = scatter_over(grads_a, swap_z, chips)
    sum_b = scatter_over(grads_b, swap_z, chips)
    own_gate, own_output = sum_a[:rows_f], sum_a[rows_f:]
    own_up, own_down = sum_b[:rows_f], sum_b[rows_f:]
    own_query = own_first[:rows_q]
    own_key = own_first[rows_q : rows_q + rows_k]
    own_value = own_first[rows_q + rows_k : rows_q + 2 * rows_k]
    own_scales = own_first[rows_q + 2 * rows_k, :scale_part]
    grad_resid = grad_resid_a + rms_back(unit_in, inverse_in, own_normed * (1.0 + scale_in))
    return (
        block_out[None],
        grad_resid[None],
        own_query,
        own_key,
        own_value,
        own_output,
        own_gate,
        own_up,
        own_down,
        own_scales,
    )


def shards(*args):
    hidden_in, w_query, w_gate = args[0], args[2], args[6]
    fits = hidden_in.shape[1] * lax.axis_size("ctx") <= 2048 and lax.axis_size("ctx") == 8
    fits = fits and lax.axis_size("dp") == 4
    if fits and w_query.shape[0] % 16 == 0 and w_gate.shape[0] % 16 == 0 and args[3].shape[0] == 8:
        return shards_kernels(*args)
    return shards_plain(*args)


def swaps(block, swap):
    return [swap(block, bits) for bits in range(1, 4)]


def shards_kernels(
    hidden_in,
    positions,
    w_query,
    w_key,
    w_value,
    w_output,
    w_gate,
    w_up,
    w_down,
    norm_scales,
    grad_out,
):
    width = hidden_in.shape[2]
    groups = lax.axis_size("ctx")
    count_dp = lax.axis_size("dp")
    chips = groups // 2
    owners = count_dp * groups
    place = lax.axis_index("ctx")
    row = lax.axis_index("dp")
    resid = hidden_in[0]
    posit = positions[0]
    tokens = resid.shape[0]
    block = tokens // 2
    seq_len = groups * tokens
    head_width = w_key.shape[0] * owners
    heads = w_query.shape[0] * owners // head_width
    rows_q, rows_k, rows_f = w_query.shape[0], w_key.shape[0], w_gate.shape[0]
    last = rows_q + 2 * rows_k
    scale_part = norm_scales.shape[0]
    f32 = jnp.float32
    tie = lax.optimization_barrier

    far_core, far_dp, far_z = (
        jnp.arange(owners, dtype=jnp.int32) // (owners // 2),
        (jnp.arange(owners, dtype=jnp.int32) // chips) % count_dp,
        jnp.arange(owners, dtype=jnp.int32) % chips,
    )
    owner_of = (row ^ far_dp) * groups + (place ^ (2 * far_z + far_core))
    order_s = row_order(owner_of, 1)
    held_row = jnp.arange(2 * rows_k * owners, dtype=jnp.int32)
    held_at = (
        (held_row % (2 * rows_k)) // rows_k * head_width
        + jnp.repeat(owner_of, 2 * rows_k) * rows_k
        + held_row % rows_k
    )
    order_kv = (held_row[:, None] == held_at[None, :]).astype(BF)
    seq_core, seq_zed = (
        jnp.arange(groups, dtype=jnp.int32) // chips,
        jnp.arange(groups, dtype=jnp.int32) % chips,
    )
    key_index = natural_rows(place ^ (2 * seq_zed + seq_core), block, groups).reshape(1, seq_len)
    row_index = natural_rows(place[None], block, groups).reshape(tokens, 1)

    last_rows = jnp.concatenate(
        [
            jnp.pad(values[None], ((0, 0), (0, width - values.shape[0])))
            for values in (norm_scales, (posit // 64).astype(BF), (posit % 64).astype(BF))
        ]
        + [jnp.zeros((5, width), BF)],
        axis=0,
    )
    first = jnp.concatenate([w_query, w_key, w_value, last_rows], axis=0)
    feed = jnp.concatenate([w_gate, w_up, w_down], axis=0)
    inverse_in = lax.rsqrt(jnp.mean(resid * resid, axis=-1, keepdims=True) + EPS)
    unit_in = resid * inverse_in
    unit_bf = unit_in.astype(BF)
    first = gather_over(first[None], swap_z, chips)
    first, unit_bf, feed, w_output, order_kv = tie((first, unit_bf, feed, w_output, order_kv))
    last_far = swap_ctx(first[:, last:], 1)
    pos_all = jnp.stack([first[:, last:], last_far], axis=0)[:, :, :, :tokens].astype(f32)
    pos_all = (pos_all[:, :, 1] * 64.0 + pos_all[:, :, 2]).reshape(seq_len)
    half = head_width // 2
    freq_table = 1000000.0 ** (-jnp.arange(half, dtype=jnp.float32) / half)
    angle = pos_all[:, None] * freq_table[None, :]
    cos_all, sine_all = jnp.cos(angle), jnp.sin(angle)
    first = gather_over(first[None], swap_dp, count_dp).reshape((owners // 2,) + first.shape[1:])
    near = gather_over(unit_bf[None], swap_z, chips).reshape(chips * tokens, width)
    first, near, feed, w_output, cos_all, sine_all = tie(
        (first, near, feed, w_output, cos_all, sine_all)
    )
    other = swap_ctx(first, 1)
    far = swap_ctx(near, 1)
    out_own = gather_over(w_output[None], swap_z, chips)
    other, far, out_own, feed = tie((other, far, out_own, feed))
    scale_rows = jnp.concatenate([first[:, last, :scale_part], other[:, last, :scale_part]], axis=0)
    full_scales = reorder(order_s, scale_rows).reshape(-1)
    scale_in, scale_attn, scale_pre, scale_post, scale_query, scale_key = [
        scale[None] for scale in split_scales(full_scales, width, head_width)
    ]
    feed_z2 = swap_z(feed, 2)
    feed_z1 = swap_z(feed, 1)
    out_own = gather_over(out_own[None], swap_dp, count_dp).reshape((owners // 2, rows_q, width))
    (w_q, w_kv, normed, normed_all, query_raw, key_raw, query_bf, key_bf, value_bf, attn_bf, lse) = (
        call_kernel(
            attend_kernel,
            [
                ((heads * head_width, width), BF),
                ((2 * head_width, width), BF),
                ((tokens, width), BF),
                ((seq_len, width), BF),
                ((tokens, heads * head_width), f32),
                ((seq_len, head_width), f32),
                ((tokens, heads * head_width), BF),
                ((seq_len, head_width), BF),
                ((seq_len, head_width), BF),
                ((tokens, heads * head_width), BF),
                ((tokens, heads), f32),
            ],
            [((2 * head_width, width), BF)],
            12_000_000_000,
            (
                unit_in, near, far, first, other, owner_of, order_kv, scale_in, scale_query, scale_key,
                cos_all, sine_all, key_index, row_index,
            ),
            mebibytes=52,
        )
    )
    attn_bf, feed_z1, feed_z2, out_own, feed = tie((attn_bf, feed_z1, feed_z2, out_own, feed))
    out_other = swap_ctx(out_own, 1)
    feed_z3 = swap_z(feed, 3)
    feed_c0 = swap_ctx(feed, 1)
    feed_c1 = swap_ctx(feed_z1, 1)
    feed_c2 = swap_ctx(feed_z2, 1)
    full_output, projected, middle, pre = call_kernel(
        project_kernel,
        [
            ((owners * rows_q, width), BF),
            ((tokens, width), f32),
            ((tokens, width), f32),
            ((tokens, width), BF),
        ],
        [],
        2_000_000_000,
        (attn_bf, owner_of, out_own, out_other, resid, scale_attn, scale_pre),
    )
    pres = swaps(pre, swap_dp)
    pre, pres, feed_z3, feed_c0, feed_c1, feed_c2 = tie((pre, pres, feed_z3, feed_c0, feed_c1, feed_c2))
    feed_c3 = swap_ctx(feed_z3, 1)
    part_shapes = [((tokens, width), f32)] + [((tokens, width), BF)] * 3
    all_tokens = count_dp * tokens
    hidden = groups * rows_f
    outs = call_kernel(
        feed_kernel,
        part_shapes
        + [
            ((all_tokens, hidden), f32),
            ((all_tokens, hidden), f32),
            ((all_tokens, hidden), BF),
            ((all_tokens, width), BF),
        ]
        + [((hidden, width), BF)] * 3,
        [],
        3_000_000_000,
        [pre] + pres + [feed, feed_z1, feed_z2, feed_z3, feed_c0, feed_c1, feed_c2, feed_c3],
    )
    parts, kept = outs[:4], outs[4:]
    comes = [swap_dp(parts[bits], bits) for bits in range(1, 4)]
    block_out, grad_ffn, grad_s_post = call_kernel(
        turning_kernel,
        [((tokens, width), f32), ((tokens, width), BF), ((1, width), f32)],
        [],
        100_000_000,
        [parts[0]] + comes + [middle, grad_out[0], scale_post],
    )
    gate, up, inner, pre_all, w_g, w_u, w_d = kept
    outs = call_kernel(
        feed_back_kernel,
        part_shapes + [((all_tokens, width), BF), ((all_tokens, hidden), BF), ((all_tokens, hidden), BF)],
        [],
        3_000_000_000,
        [grad_ffn] + swaps(grad_ffn, swap_dp) + [gate, up, w_g, w_u, w_d],
    )
    parts, back = outs[:4], outs[4:]
    comes = [swap_dp(parts[bits], bits) for bits in range(1, 4)]
    g_feed, g_feed_far = call_kernel(
        feed_weights_kernel,
        [((chips, 3 * rows_f, width), BF)] * 2,
        [],
        3_000_000_000,
        [inner, pre_all] + list(back),
    )
    g_feed, g_feed_far, comes = tie((g_feed, g_feed_far, comes))
    g_feed = add_bf16(g_feed, swap_ctx(g_feed_far, 1)).astype(BF)
    grad_resid_a, grad_attn, g_out, g_out_far, grad_s_attn, grad_s_pre = call_kernel(
        project_back_kernel,
        [
            ((tokens, width), f32),
            ((tokens, heads * head_width), BF),
            (out_own.shape, BF),
            (out_own.shape, BF),
            ((1, width), f32),
            ((1, width), f32),
        ],
        [((owners * rows_q, width), BF)],
        3_000_000_000,
        [parts[0]]
        + comes
        + [grad_out[0], projected, middle, full_output, attn_bf, owner_of, scale_attn, scale_pre],
    )
    g_out = add_bf16(g_out, swap_ctx(g_out_far, 1)).astype(BF).reshape(count_dp, chips, rows_q, width)
    g_out, g_feed, grad_attn = tie((g_out, g_feed, grad_attn))
    feed_come1 = swap_z(g_feed[1], 1)
    feed_come2 = swap_z(g_feed[2], 2)
    out_comes = [swap_dp(g_out[bits], bits) for bits in range(1, 4)]
    (packed, packed_far, g_near, g_far, grad_normed_q, grad_s_in, grad_s_query, grad_s_key) = call_kernel(
        attend_back_kernel,
        [
            ((owners // 2, last, width), BF),
            ((owners // 2, last, width), BF),
            ((seq_len // 2, 2 * head_width), BF),
            ((seq_len // 2, 2 * head_width), BF),
            ((tokens, width), f32),
            ((1, width), f32),
            ((1, head_width), f32),
            ((1, head_width), f32),
        ],
        [
            ((heads * tokens, seq_len), BF),
            ((heads * tokens, seq_len), BF),
            ((heads * tokens, head_width), BF),
            ((heads * tokens, head_width), BF),
            ((tokens, heads * head_width), BF),
            ((2 * head_width, width), BF),
            ((heads * head_width, width), BF),
        ],
        12_000_000_000,
        (
            grad_attn, attn_bf, query_bf, key_bf, value_bf, lse, query_raw, key_raw, w_q, w_kv,
            scale_query, scale_key, cos_all, sine_all, key_index, row_index, normed, normed_all,
            unit_in, near, far, owner_of, order_kv,
        ),
        mebibytes=36,
    )
    back = (packed, packed_far, g_near, g_far, grad_normed_q, grad_s_in, grad_s_query, grad_s_key)
    back, feed_come1, feed_come2, out_comes, g_out, g_feed = tie(
        (back, feed_come1, feed_come2, out_comes, g_out, g_feed)
    )
    packed, packed_far, g_near, g_far, grad_normed_q, grad_s_in, grad_s_query, grad_s_key = back
    grad_scales = jnp.concatenate(
        [grad_s_in, grad_s_attn, grad_s_pre, grad_s_post, grad_s_query, grad_s_key], axis=1
    ).reshape(owners, scale_part)
    scales_back = reorder_back(order_s, grad_scales)
    scale_sum = add_bf16(scales_back[: owners // 2], swap_ctx(scales_back[owners // 2 :], 1))
    scale_sum = jnp.pad(scale_sum[:, None], ((0, 0), (last, 7), (0, width - scale_part)))
    packed = jnp.pad(add_bf16(packed, swap_ctx(packed_far, 1)), ((0, 0), (0, 8), (0, 0)))
    packed = (packed + scale_sum).astype(BF)
    feed_come3 = swap_z(g_feed[3, : 3 * rows_f // 2], 3)
    far_sum = add_bf16(g_near, swap_ctx(g_far, 1)).astype(BF).reshape(chips, tokens, 2 * head_width)
    out_sum = add_bf16(g_out[0], *out_comes).astype(BF)
    packed, far_sum, out_sum, g_feed, feed_come3 = tie((packed, far_sum, out_sum, g_feed, feed_come3))
    packed = scatter_over(packed.reshape((count_dp, chips) + packed.shape[1:]), swap_dp, count_dp)
    own_kv = scatter_over(far_sum, swap_z, chips).astype(BF)
    packed, own_kv, out_sum, g_feed = tie((packed.astype(BF), own_kv, out_sum, g_feed))
    own_normed = jnp.dot(own_kv, w_kv, preferred_element_type=jnp.float32) + grad_normed_q
    half_rows = 3 * rows_f // 2
    last_comes = []
    for bits in range(1, 4):
        blocks = [out_sum[bits], packed[bits]] + ([g_feed[3, half_rows:]] if bits == 3 else [])
        last_comes.append(swap_z(jnp.concatenate(blocks, axis=0), bits))
    own_query, own_key, own_value, own_last, own_output, own_gate, own_up, own_down = call_kernel(
        ending_kernel,
        [
            ((rows_q, width), f32),
            ((rows_k, width), f32),
            ((rows_k, width), f32),
            ((8, width), f32),
            ((rows_q, width), f32),
            ((rows_f, width), f32),
            ((rows_f, width), f32),
            ((rows_f, width), f32),
        ],
        [],
        10_000_000,
        [packed[0], out_sum[0]]
        + last_comes
        + [g_feed[0], feed_come1, feed_come2, feed_come3],
    )
    grad_resid = grad_resid_a + rms_back(unit_in, inverse_in, own_normed * (1.0 + scale_in))
    return (
        block_out[None],
        grad_resid[None],
        own_query,
        own_key,
        own_value,
        own_output,
        own_gate,
        own_up,
        own_down,
        own_last[0, :scale_part],
    )


def solution(mesh):
    in_specs = (
        P("dp", "ctx", None),
        P("dp", "ctx"),
        P(("dp", "ctx"), None),
        P(("dp", "ctx"), None),
        P(("dp", "ctx"), None),
        P(("dp", "ctx"), None),
        P(("dp", "ctx"), None),
        P(("dp", "ctx"), None),
        P(("dp", "ctx"), None),
        P(("dp", "ctx")),
        P("dp", "ctx", None),
    )
    out_specs = (
        P("dp", "ctx", None),
        P("dp", "ctx", None),
        P(("dp", "ctx"), None),
        P(("dp", "ctx"), None),
        P(("dp", "ctx"), None),
        P(("dp", "ctx"), None),
        P(("dp", "ctx"), None),
        P(("dp", "ctx"), None),
        P(("dp", "ctx"), None),
        P(("dp", "ctx")),
    )
    return jax.shard_map(shards, mesh=mesh, in_specs=in_specs, out_specs=out_specs, check_vma=False)
```

```python
import jax
import jax.numpy as jnp
from jax import lax
from jax.experimental import pallas as pl
from jax.experimental.pallas import tpu as pltpu
from jax.sharding import PartitionSpec as P

EPS = 1e-06


def rms_scale(vector, scale):
    return (
        vector * lax.rsqrt(jnp.mean(vector * vector, axis=-1, keepdims=True) + EPS) * (1.0 + scale)
    )


def rotate(vector, position):
    half = vector.shape[-1] // 2
    freq_table = 1000000.0 ** (-jnp.arange(half, dtype=jnp.float32) / half)
    angle = position.astype(jnp.float32)[:, None] * freq_table[None, :]
    cosine = jnp.cos(angle)[:, None, :]
    sine = jnp.sin(angle)[:, None, :]
    first = vector[..., :half]
    second = vector[..., half:]
    return jnp.concatenate(
        [first * cosine - second * sine, second * cosine + first * sine], axis=-1
    )


def mid_piece(resid, projected, scale_attn, scale_pre):
    middle = resid + rms_scale(projected, scale_attn)
    return (middle, rms_scale(middle, scale_pre))


def glu_piece(gate, upward):
    return jax.nn.gelu(gate, approximate=True) * upward


def out_piece(middle, ffn, scale_post):
    return middle + rms_scale(ffn, scale_post)


def times_wt(left, weight):
    return lax.dot_general(
        left, weight, (((1,), (1,)), ((), ())), preferred_element_type=jnp.float32
    )


def outer_sum(left, right):
    return lax.dot_general(
        left, right, (((0,), (0,)), ((), ())), preferred_element_type=jnp.float32
    )


def split_scales(norm_scales, width, head_width):
    scales = norm_scales.astype(jnp.float32)
    pieces = [scales[index * width : (index + 1) * width] for index in range(4)]
    offset = 4 * width
    return pieces + [
        scales[offset : offset + head_width],
        scales[offset + head_width : offset + 2 * head_width],
    ]


BF = jnp.bfloat16


def swap_dp(block, bits):
    count = lax.axis_size("dp")
    return lax.ppermute(block, "dp", [(place, place ^ bits) for place in range(count)])


def swap_ctx(block, bits):
    count = lax.axis_size("ctx")
    return lax.ppermute(block, "ctx", [(place, place ^ bits) for place in range(count)])


def swap_z(block, bits):
    return swap_ctx(block, 2 * bits)


def gather_over(block, swap, count):
    if count <= 4:
        return jnp.concatenate([block] + [swap(block, bits) for bits in range(1, count)], axis=0)
    bits = 1
    while bits < count:
        block = jnp.concatenate([block, swap(block, bits)], axis=0)
        bits = 2 * bits
    return block


def add_bf16(first, *others):
    total = first.astype(jnp.float32)
    for other in others:
        total = total + other.astype(jnp.float32)
    return total


def scatter_over(blocks, swap, count):
    if count <= 4:
        return add_bf16(blocks[0], *[swap(blocks[bits], bits) for bits in range(1, count)])
    bits = count // 2
    while bits > 1:
        blocks = add_bf16(blocks[:bits], swap(blocks[bits:], bits)).astype(BF)
        bits = bits // 2
    return add_bf16(blocks[0], swap(blocks[1], 1))


def gather_chip(block):
    groups = lax.axis_size("ctx") // 2
    over_z = gather_over(block[None], swap_z, groups)
    over_dp = gather_over(over_z[None], swap_dp, lax.axis_size("dp"))
    return over_dp.reshape((-1,) + block.shape[1:])


def double(blocks, swap, bits):
    return jnp.concatenate([blocks, swap(blocks, bits)], axis=0)


def double_inner(blocks, swap, bits):
    pair = blocks.reshape((2, 1, -1) + blocks.shape[1:])
    return jnp.concatenate([pair, swap(pair, bits)], axis=1).reshape((-1,) + blocks.shape[1:])


def halve(blocks, swap, bits):
    half = blocks.shape[0] // 2
    return add_bf16(blocks[:half], swap(blocks[half:], bits)).astype(BF)


def halve_inner(blocks, swap, bits):
    quarters = blocks.reshape((2, 2, -1) + blocks.shape[1:])
    half = add_bf16(quarters[:, 0], swap(quarters[:, 1], bits)).astype(BF)
    return half.reshape((-1,) + blocks.shape[1:])


def scatter_chip(blocks):
    groups = lax.axis_size("ctx") // 2
    count = lax.axis_size("dp")
    shaped = blocks.reshape((count, groups, -1) + blocks.shape[1:])
    mid = scatter_over(shaped, swap_dp, count).astype(BF)
    return scatter_over(mid, swap_z, groups)


def scatter_all(first, second):
    return scatter_chip(add_bf16(first, swap_ctx(second, 1)).astype(BF))


def natural_rows(places, block, groups):
    within = jnp.arange(2 * block, dtype=jnp.int32)[None, :]
    early = places[:, None] * block + within
    late = (2 * groups - 1 - places[:, None]) * block + within - block
    return jnp.where(within < block, early, late).reshape(-1)


def row_order(owner_of, rows):
    count = owner_of.shape[0] * rows
    held = (owner_of[:, None] * rows + jnp.arange(rows, dtype=jnp.int32)[None, :]).reshape(1, count)
    return (jnp.arange(count, dtype=jnp.int32)[:, None] == held).astype(BF)


def reorder(order, blocks):
    return jnp.dot(order, blocks, preferred_element_type=jnp.float32).astype(BF)


def reorder_back(order, blocks):
    return outer_sum(order, blocks.astype(BF)).astype(BF)


def rms_back(unit, inverse, grad_scaled):
    return inverse * (grad_scaled - unit * jnp.mean(grad_scaled * unit, axis=-1, keepdims=True))


def dot_nt(left, right):
    return lax.dot_general(left, right, (((1,), (1,)), ((), ())), preferred_element_type=jnp.float32)


def dot_nn(left, right):
    return lax.dot_general(left, right, (((1,), (0,)), ((), ())), preferred_element_type=jnp.float32)


def dot_tn(left, right):
    return lax.dot_general(left, right, (((0,), (0,)), ((), ())), preferred_element_type=jnp.float32)


def unit_of(rows):
    inverse = lax.rsqrt(jnp.mean(rows * rows, axis=-1, keepdims=True) + EPS)
    return rows * inverse, inverse


def turn(rows, cosine, sine):
    half = rows.shape[1] // 2
    first, second = rows[:, :half], rows[:, half:]
    return jnp.concatenate([first * cosine - second * sine, second * cosine + first * sine], axis=1)


def turn_back(rows, cosine, sine):
    half = rows.shape[1] // 2
    first, second = rows[:, :half], rows[:, half:]
    return jnp.concatenate([first * cosine + second * sine, second * cosine - first * sine], axis=1)


def call_kernel(body, out_shapes, scratch, flops, inputs, mebibytes=24):
    whole = pl.BlockSpec(memory_space=pltpu.VMEM)
    return pl.pallas_call(
        body,
        out_shape=[jax.ShapeDtypeStruct(shape, dtype) for shape, dtype in out_shapes],
        in_specs=[
            pl.BlockSpec(memory_space=pltpu.SMEM) if entry.ndim == 1 else whole for entry in inputs
        ],
        out_specs=[whole] * len(out_shapes),
        scratch_shapes=[pltpu.VMEM(shape, dtype) for shape, dtype in scratch],
        compiler_params=pltpu.CompilerParams(vmem_limit_bytes=mebibytes * 1024 * 1024),
        cost_estimate=pl.CostEstimate(flops=flops, bytes_accessed=20_000_000, transcendentals=0),
    )(*inputs)


def owner_rows(owner_ref, entry, rows):
    return pl.ds(pl.multiple_of(owner_ref[entry] * rows, rows), rows)


def attend_kernel(
    unit_ref, near_ref, far_ref, own_ref, other_ref, owner_ref, order_kv_ref, sin_scale_ref, sq_ref,
    sk_ref, cos_all_ref, sine_all_ref, key_index_ref, row_index_ref,
    wq_ref, wkv_ref, normed_ref, normed_all_ref, qraw_ref, kraw_ref, q_ref, k_ref, v_ref, attn_ref, lse_ref,
    held_kv,
):
    places, _, width = own_ref.shape
    rows_q = wq_ref.shape[0] // (2 * places)
    rows_kv = held_kv.shape[0] // (2 * places)
    for core, ref in enumerate((own_ref, other_ref)):
        for at in range(places):
            wq_ref[owner_rows(owner_ref, core * places + at, rows_q), :] = ref[at, :rows_q, :]
        held_kv[core * places * rows_kv : (core + 1) * places * rows_kv, :] = ref[
            :, rows_q : rows_q + rows_kv, :
        ].reshape(places * rows_kv, width)
    wkv_ref[...] = dot_nn(order_kv_ref[...], held_kv[...]).astype(BF)
    tokens = unit_ref.shape[0]
    scale_in = 1.0 + sin_scale_ref[...]
    normed_ref[...] = (unit_ref[...] * scale_in).astype(BF)
    half = near_ref.shape[0]
    normed_all_ref[:half] = (near_ref[...].astype(jnp.float32) * scale_in).astype(BF)
    normed_all_ref[half:] = (far_ref[...].astype(jnp.float32) * scale_in).astype(BF)
    head_width = sq_ref.shape[1]
    heads = wq_ref.shape[0] // head_width
    key_raw = dot_nt(normed_all_ref[...], wkv_ref[:head_width, :])
    kraw_ref[...] = key_raw
    v_ref[...] = dot_nt(normed_all_ref[...], wkv_ref[head_width:, :]).astype(BF)
    key_unit, _ = unit_of(key_raw)
    k_ref[...] = turn(key_unit * (1.0 + sk_ref[...]), cos_all_ref[...], sine_all_ref[...]).astype(BF)
    allowed = key_index_ref[...] <= row_index_ref[...]
    cosine, sine = cos_all_ref[:tokens, :], sine_all_ref[:tokens, :]
    for head in range(heads):
        span = slice(head * head_width, (head + 1) * head_width)
        raw = dot_nt(normed_ref[...], wq_ref[span, :])
        qraw_ref[:, span] = raw
        unit, _ = unit_of(raw)
        turned = turn(unit * (1.0 + sq_ref[...]), cosine, sine)
        query = (turned * head_width ** (-0.5)).astype(BF)
        q_ref[:, span] = query
        scores = jnp.where(allowed, dot_nt(query, k_ref[...]), -1e30)
        top = jnp.max(scores, axis=1, keepdims=True)
        lse = top + jnp.log(jnp.sum(jnp.exp(scores - top), axis=1, keepdims=True))
        lse_ref[:, head : head + 1] = lse
        probs = jnp.exp(scores - lse).astype(BF)
        attn_ref[:, span] = dot_nn(probs, v_ref[...]).astype(BF)


def project_kernel(
    attn_ref, owner_ref, own_ref, other_ref, resid_ref, sattn_ref, spre_ref,
    wo_ref, projected_ref, middle_ref, pre_ref,
):
    places, rows, _ = own_ref.shape
    for core, ref in enumerate((own_ref, other_ref)):
        for at in range(places):
            wo_ref[owner_rows(owner_ref, core * places + at, rows), :] = ref[at]
    projected = dot_nn(attn_ref[...], wo_ref[...])
    projected_ref[...] = projected
    unit, _ = unit_of(projected)
    middle = resid_ref[...] + unit * (1.0 + sattn_ref[...])
    middle_ref[...] = middle
    unit, _ = unit_of(middle)
    pre_ref[...] = (unit * (1.0 + spre_ref[...])).astype(BF)


GELU_A = (2.0 / 3.141592653589793) ** 0.5


def feed_kernel(*refs):
    pres, weights = refs[:4], refs[4:12]
    part_refs = refs[12:16]
    gate_ref, up_ref, inner_ref, pre_ref, wg_ref, wu_ref, wd_ref = refs[16:]
    tokens = pres[0].shape[0]
    rows = weights[0].shape[0] // 3
    for number, ref in enumerate(pres):
        pre_ref[number * tokens : (number + 1) * tokens, :] = ref[...]
    for number, ref in enumerate(weights):
        span = slice(number * rows, (number + 1) * rows)
        wg_ref[span, :] = ref[:rows, :]
        wu_ref[span, :] = ref[rows : 2 * rows, :]
        wd_ref[span, :] = ref[2 * rows :, :]
    for number in range(4):
        at = slice(number * tokens, (number + 1) * tokens)
        gate = dot_nt(pre_ref[at, :], wg_ref[...])
        up = dot_nt(pre_ref[at, :], wu_ref[...])
        gate_ref[at, :] = gate
        up_ref[at, :] = up
        bent = jnp.tanh(GELU_A * (gate + 0.044715 * (gate * gate * gate)))
        inner = (0.5 * gate * (1.0 + bent) * up).astype(BF)
        inner_ref[at, :] = inner
        part_refs[number][...] = dot_nn(inner, wd_ref[...]).astype(part_refs[number].dtype)


def turning_kernel(
    own_ref, come1_ref, come2_ref, come3_ref, middle_ref, gout_ref, spost_ref,
    block_out_ref, gffn_ref, gspost_ref,
):
    ffn = own_ref[...]
    for ref in (come1_ref, come2_ref, come3_ref):
        ffn = ffn + ref[...].astype(jnp.float32)
    unit, inverse = unit_of(ffn)
    grad_out = gout_ref[...]
    block_out_ref[...] = middle_ref[...] + unit * (1.0 + spost_ref[...])
    gspost_ref[...] = jnp.sum(grad_out * unit, axis=0, keepdims=True)
    gffn_ref[...] = rms_back(unit, inverse, grad_out * (1.0 + spost_ref[...])).astype(BF)


def feed_back_kernel(*refs):
    grads = refs[:4]
    gate_ref, up_ref, wg_ref, wu_ref, wd_ref = refs[4:9]
    part_refs = refs[9:13]
    gffn_ref, ggate_ref, gup_ref = refs[13:]
    tokens = grads[0].shape[0]
    for number, ref in enumerate(grads):
        at = slice(number * tokens, (number + 1) * tokens)
        gffn_ref[at, :] = ref[...]
        grad_inner = dot_nt(ref[...], wd_ref[...])
        gate = gate_ref[at, :]
        square = gate * gate
        bent = jnp.tanh(GELU_A * (gate + 0.044715 * (square * gate)))
        curve = 0.5 * gate * (1.0 + bent)
        slope = 0.5 * (1.0 + bent) + 0.5 * gate * (1.0 - bent * bent) * (
            GELU_A * (1.0 + 3.0 * 0.044715 * square)
        )
        grad_up = (grad_inner * curve).astype(BF)
        grad_gate = (grad_inner * up_ref[at, :] * slope).astype(BF)
        ggate_ref[at, :] = grad_gate
        gup_ref[at, :] = grad_up
        part_refs[number][...] = (dot_nn(grad_gate, wg_ref[...]) + dot_nn(grad_up, wu_ref[...])).astype(
            part_refs[number].dtype
        )


def feed_weights_kernel(inner_ref, pre_ref, gffn_ref, ggate_ref, gup_ref, own_ref, other_ref):
    places, rows, width = own_ref.shape
    rows = rows // 3
    shape = (places, rows, width)
    for core, ref in enumerate((own_ref, other_ref)):
        span = slice(core * places * rows, (core + 1) * places * rows)
        ref[:, :rows, :] = dot_tn(ggate_ref[:, span], pre_ref[...]).astype(BF).reshape(shape)
        ref[:, rows : 2 * rows, :] = dot_tn(gup_ref[:, span], pre_ref[...]).astype(BF).reshape(shape)
        ref[:, 2 * rows :, :] = dot_tn(inner_ref[:, span], gffn_ref[...]).astype(BF).reshape(shape)


def project_back_kernel(
    own_ref, come1_ref, come2_ref, come3_ref, gout_ref, projected_ref, middle_ref, wo_ref, attn_ref,
    owner_ref, sattn_ref, spre_ref,
    gresid_ref, gattn_ref, gown_ref, gother_ref, gsattn_ref, gspre_ref,
    gwo_scr,
):
    grad_pre = own_ref[...]
    for ref in (come1_ref, come2_ref, come3_ref):
        grad_pre = grad_pre + ref[...].astype(jnp.float32)
    unit_p, inverse_p = unit_of(middle_ref[...])
    unit_a, inverse_a = unit_of(projected_ref[...])
    gspre_ref[...] = jnp.sum(grad_pre * unit_p, axis=0, keepdims=True)
    grad_middle = gout_ref[...] + rms_back(unit_p, inverse_p, grad_pre * (1.0 + spre_ref[...]))
    gresid_ref[...] = grad_middle
    gsattn_ref[...] = jnp.sum(grad_middle * unit_a, axis=0, keepdims=True)
    grad_proj = rms_back(unit_a, inverse_a, grad_middle * (1.0 + sattn_ref[...])).astype(BF)
    gattn_ref[...] = dot_nt(grad_proj, wo_ref[...]).astype(BF)
    gwo_scr[...] = dot_tn(attn_ref[...], grad_proj).astype(BF)
    places, rows, _ = gown_ref.shape
    for core, ref in enumerate((gown_ref, gother_ref)):
        for at in range(places):
            ref[at] = gwo_scr[owner_rows(owner_ref, core * places + at, rows), :]


def attend_back_kernel(
    grad_attn_ref, attn_ref, q_ref, k_ref, v_ref, lse_ref, qraw_ref, kraw_ref, wq_ref, wkv_ref,
    sq_ref, sk_ref, cos_all_ref, sine_all_ref, key_index_ref, row_index_ref,
    normed_ref, normed_all_ref, unit_ref, near_ref, far_ref, owner_ref, order_kv_ref,
    own_ref, other_ref, gnear_ref, gfar_ref, gq_ref, gsin_ref, gsq_ref, gsk_ref,
    probs_scr, gscores_scr, grows_scr, qrows_scr, gqraw_scr, gkv_scr, gwq_scr,
):
    head_width = sq_ref.shape[1]
    heads = wq_ref.shape[0] // head_width
    tokens = q_ref.shape[0]
    cosine, sine = cos_all_ref[:tokens, :], sine_all_ref[:tokens, :]
    allowed = key_index_ref[...] <= row_index_ref[...]
    grad_sq = jnp.zeros((1, head_width), jnp.float32)
    for head in range(heads):
        span = slice(head * head_width, (head + 1) * head_width)
        rows = slice(head * tokens, (head + 1) * tokens)
        query = q_ref[:, span]
        grad_rows = grad_attn_ref[:, span]
        delta = jnp.sum(
            grad_rows.astype(jnp.float32) * attn_ref[:, span].astype(jnp.float32),
            axis=1,
            keepdims=True,
        )
        scores = jnp.where(allowed, dot_nt(query, k_ref[...]), -1e30)
        probs = jnp.exp(scores - lse_ref[:, head : head + 1])
        grad_scores = (probs * (dot_nt(grad_rows, v_ref[...]) - delta)).astype(BF)
        probs_scr[rows, :] = probs.astype(BF)
        gscores_scr[rows, :] = grad_scores
        grows_scr[rows, :] = grad_rows
        qrows_scr[rows, :] = query
        grad_query = dot_nn(grad_scores, k_ref[...]) * head_width ** (-0.5)
        grad_query = turn_back(grad_query, cosine, sine)
        unit, inverse = unit_of(qraw_ref[:, span])
        grad_sq = grad_sq + jnp.sum(grad_query * unit, axis=0, keepdims=True)
        grad_raw = rms_back(unit, inverse, grad_query * (1.0 + sq_ref[...]))
        gqraw_scr[:, span] = grad_raw.astype(BF)
    gsq_ref[...] = grad_sq
    grad_key = dot_tn(gscores_scr[...], qrows_scr[...])
    grad_value = dot_tn(probs_scr[...], grows_scr[...]).astype(BF)
    grad_key = turn_back(grad_key, cos_all_ref[...], sine_all_ref[...])
    unit, inverse = unit_of(kraw_ref[...])
    gsk_ref[...] = jnp.sum(grad_key * unit, axis=0, keepdims=True)
    grad_kraw = rms_back(unit, inverse, grad_key * (1.0 + sk_ref[...])).astype(BF)
    half = near_ref.shape[0]
    grad_normed = dot_nn(grad_kraw, wkv_ref[:head_width, :]) + dot_nn(
        grad_value, wkv_ref[head_width:, :]
    )
    grad_q = dot_nn(gqraw_scr[...], wq_ref[...])
    gq_ref[...] = grad_q
    gsin_ref[...] = (
        jnp.sum(grad_normed[:half] * near_ref[...].astype(jnp.float32), axis=0, keepdims=True)
        + jnp.sum(grad_normed[half:] * far_ref[...].astype(jnp.float32), axis=0, keepdims=True)
        + jnp.sum(grad_q * unit_ref[...], axis=0, keepdims=True)
    )
    gnear_ref[:, :head_width] = grad_kraw[:half]
    gnear_ref[:, head_width:] = grad_value[:half]
    gfar_ref[:, :head_width] = grad_kraw[half:]
    gfar_ref[:, head_width:] = grad_value[half:]
    gkv_scr[:head_width, :] = dot_tn(grad_kraw, normed_all_ref[...]).astype(BF)
    gkv_scr[head_width:, :] = dot_tn(grad_value, normed_all_ref[...]).astype(BF)
    gwq_scr[...] = dot_tn(gqraw_scr[...], normed_ref[...]).astype(BF)
    held_kv = dot_tn(order_kv_ref[...], gkv_scr[...]).astype(BF)
    places, _, width = own_ref.shape
    rows_q = gwq_scr.shape[0] // (2 * places)
    rows_kv = held_kv.shape[0] // (2 * places)
    for core, ref in enumerate((own_ref, other_ref)):
        for at in range(places):
            ref[at, :rows_q, :] = gwq_scr[owner_rows(owner_ref, core * places + at, rows_q), :]
        ref[:, rows_q : rows_q + rows_kv, :] = held_kv[
            core * places * rows_kv : (core + 1) * places * rows_kv
        ].reshape(places, rows_kv, width)


def ending_kernel(*refs):
    first_ref, out_ref = refs[:2]
    comes = [ref[...].astype(jnp.float32) for ref in refs[2:5]]
    feeds, results = refs[5:9], refs[9:]
    rows_q = out_ref.shape[0]
    rows = rows_q + first_ref.shape[0]
    total = first_ref[...].astype(jnp.float32)
    for come in comes:
        total = total + come[rows_q:rows]
    row = 0
    for ref in results[:4]:
        ref[...] = total[row : row + ref.shape[0]]
        row = row + ref.shape[0]
    total = out_ref[...].astype(jnp.float32)
    for come in comes:
        total = total + come[:rows_q]
    results[4][...] = total
    total = add_bf16(*[ref[...] for ref in feeds[:3]]) + jnp.concatenate(
        [feeds[3][...].astype(jnp.float32), comes[2][rows:]], axis=0
    )
    row = 0
    for ref in results[5:]:
        ref[...] = total[row : row + ref.shape[0]]
        row = row + ref.shape[0]


def shards_plain(
    hidden_in,
    positions,
    w_query,
    w_key,
    w_value,
    w_output,
    w_gate,
    w_up,
    w_down,
    norm_scales,
    grad_out,
):
    width = hidden_in.shape[2]
    groups = lax.axis_size("ctx")
    count_dp = lax.axis_size("dp")
    chips = groups // 2
    owners = count_dp * groups
    place = lax.axis_index("ctx")
    row = lax.axis_index("dp")
    resid = hidden_in[0]
    posit = positions[0]
    grad_nat = grad_out[0]
    tokens = resid.shape[0]
    block = tokens // 2
    head_width = w_key.shape[0] * owners
    heads = w_query.shape[0] * owners // head_width
    rows_q, rows_k = w_query.shape[0], w_key.shape[0]
    scale_part = norm_scales.shape[0]

    tie = lax.optimization_barrier
    scale_rows = jnp.zeros((8, width), BF).at[0, :scale_part].set(norm_scales)
    first = gather_over(
        jnp.concatenate([w_query, w_key, w_value, scale_rows], axis=0)[None], swap_z, chips
    )
    rows_f = w_gate.shape[0]
    group_a = jnp.concatenate([w_gate, w_output], axis=0)[None]
    group_b = jnp.concatenate([w_up, w_down], axis=0)[None]
    inverse_in = lax.rsqrt(jnp.mean(resid * resid, axis=-1, keepdims=True) + EPS)
    unit_in = resid * inverse_in
    place_rows = jnp.zeros((8, width), BF)
    place_rows = place_rows.at[0, :tokens].set((posit // 64).astype(BF))
    place_rows = place_rows.at[1, :tokens].set((posit % 64).astype(BF))
    seq_part = jnp.concatenate([unit_in.astype(BF), place_rows], axis=0)[None]
    first, group_a, group_b, seq_part = tie((first, group_a, group_b, seq_part))
    first = gather_over(first[None], swap_dp, count_dp)
    group_a = gather_over(group_a, swap_z, chips)
    group_b = gather_over(group_b, swap_z, chips)
    first, group_a, group_b, seq_part = tie((first, group_a, group_b, seq_part))
    first = first.reshape((owners // 2,) + first.shape[2:])
    group_a = double(group_a, swap_dp, 1)
    group_b = double(group_b, swap_dp, 2)
    seq_z = gather_over(seq_part, swap_z, chips)
    first = jnp.concatenate([first, swap_ctx(first, 1)], axis=0)
    first, group_a, group_b, seq_z = tie((first, group_a, group_b, seq_z))
    seq_all = jnp.concatenate([seq_z, swap_ctx(seq_z, 1)], axis=0)
    group_a = double(group_a, swap_dp, 2)
    group_b = double_inner(group_b, swap_dp, 1)
    far_core, far_dp, far_z = (
        jnp.arange(owners, dtype=jnp.int32) // (owners // 2),
        (jnp.arange(owners, dtype=jnp.int32) // chips) % count_dp,
        jnp.arange(owners, dtype=jnp.int32) % chips,
    )
    owner_of = (row ^ far_dp) * groups + (place ^ (2 * far_z + far_core))
    order_q = row_order(owner_of, rows_q)
    order_k = row_order(owner_of, rows_k)
    order_s = row_order(owner_of, 1)
    full_query = reorder(order_q, first[:, :rows_q].reshape(-1, width))
    full_key = reorder(order_k, first[:, rows_q : rows_q + rows_k].reshape(-1, width))
    full_value = reorder(order_k, first[:, rows_q + rows_k : rows_q + 2 * rows_k].reshape(-1, width))
    full_scales = reorder(order_s, first[:, rows_q + 2 * rows_k, :scale_part]).reshape(-1)
    scale_in, scale_attn, scale_pre, scale_post, scale_query, scale_key = split_scales(
        full_scales, width, head_width
    )

    seq_len = groups * tokens
    seq_core, seq_zed = (
        jnp.arange(groups, dtype=jnp.int32) // chips,
        jnp.arange(groups, dtype=jnp.int32) % chips,
    )
    key_index = natural_rows(place ^ (2 * seq_zed + seq_core), block, groups)
    row_index = natural_rows(place[None], block, groups)
    unit_all = seq_all[:, :tokens].reshape(seq_len, width).astype(jnp.float32)
    pos_all = (
        seq_all[:, tokens, :tokens].astype(jnp.int32) * 64
        + seq_all[:, tokens + 1, :tokens].astype(jnp.int32)
    ).reshape(seq_len)
    normed = (unit_in * (1.0 + scale_in)).astype(BF)
    normed_all = (unit_all * (1.0 + scale_in)).astype(BF)

    query_raw = times_wt(normed, full_query).reshape(tokens, heads, head_width)
    key_raw = times_wt(normed_all, full_key)
    value_bf = times_wt(normed_all, full_value).astype(BF)

    def query_piece(raw, scale):
        return rotate(rms_scale(raw, scale), posit) * head_width ** (-0.5)

    def key_piece(raw, scale):
        return rotate(rms_scale(raw, scale)[:, None, :], pos_all)[:, 0, :]

    query_rot, query_back = jax.vjp(query_piece, query_raw, scale_query)
    key_rot, key_back = jax.vjp(key_piece, key_raw, scale_key)
    query_bf = jnp.swapaxes(query_rot.astype(BF), 0, 1).reshape(heads * tokens, head_width)
    key_bf = key_rot.astype(BF)
    allowed = jnp.tile(key_index[None, :] <= row_index[:, None], (heads, 1))
    scores = jnp.where(allowed, times_wt(query_bf, key_bf), -1e30)
    top = jnp.max(scores, axis=1, keepdims=True)
    lse = top + jnp.log(jnp.sum(jnp.exp(scores - top), axis=1, keepdims=True))
    probs = jnp.exp(scores - lse)
    probs_bf = probs.astype(BF)
    mixed = jnp.dot(probs_bf, value_bf, preferred_element_type=jnp.float32).astype(BF)
    attn_bf = jnp.swapaxes(mixed.reshape(heads, tokens, head_width), 0, 1).reshape(tokens, -1)

    group_a, group_b, attn_bf, probs = lax.optimization_barrier((group_a, group_b, attn_bf, probs))
    halves_a = (group_a, swap_ctx(group_a, 1))
    halves_b = (group_b, swap_ctx(group_b, 1))
    gates = [half[:, :rows_f].reshape(-1, width) for half in halves_a]
    ups = [half[:, :rows_f].reshape(-1, width) for half in halves_b]
    downs = [half[:, rows_f:].reshape(-1, width) for half in halves_b]
    out_held = jnp.concatenate([half[:, rows_f:].reshape(-1, width) for half in halves_a], axis=0)
    full_output = reorder(order_q, out_held)
    projected = jnp.dot(attn_bf, full_output, preferred_element_type=jnp.float32)
    (middle, pre_ffn), mid_back = jax.vjp(mid_piece, resid, projected, scale_attn, scale_pre)
    pre_bf = pre_ffn.astype(BF)
    inners, glu_backs = [], []
    for half_no in range(2):
        inner, glu_back = jax.vjp(
            glu_piece, times_wt(pre_bf, gates[half_no]), times_wt(pre_bf, ups[half_no])
        )
        inners.append(inner.astype(BF))
        glu_backs.append(glu_back)
    ffn = sum(
        jnp.dot(inners[half_no], downs[half_no], preferred_element_type=jnp.float32)
        for half_no in range(2)
    )
    block_out, out_back = jax.vjp(out_piece, middle, ffn, scale_post)
    grad_mid, grad_ffn, grad_scale_post = out_back(grad_nat)
    grad_ffn_bf = grad_ffn.astype(BF)
    grad_pre = 0.0
    downs_grad, gates_grad, ups_grad = [], [], []
    for half_no in range(2):
        grad_gate, grad_upward = glu_backs[half_no](times_wt(grad_ffn_bf, downs[half_no]))
        gate_bf = grad_gate.astype(BF)
        upward_bf = grad_upward.astype(BF)
        grad_pre = grad_pre + (
            jnp.dot(gate_bf, gates[half_no], preferred_element_type=jnp.float32)
            + jnp.dot(upward_bf, ups[half_no], preferred_element_type=jnp.float32)
        )
        downs_grad.append(outer_sum(inners[half_no], grad_ffn_bf).astype(BF))
        gates_grad.append(outer_sum(gate_bf, pre_bf).astype(BF))
        ups_grad.append(outer_sum(upward_bf, pre_bf).astype(BF))
    grads_b = [
        jnp.concatenate(
            [
                ups_grad[half_no].reshape(-1, rows_f, width),
                downs_grad[half_no].reshape(-1, rows_f, width),
            ],
            axis=1,
        )
        for half_no in range(2)
    ]
    grads_b = add_bf16(grads_b[0], swap_ctx(grads_b[1], 1)).astype(BF)
    grad_resid_a, grad_proj, grad_scale_attn, grad_scale_pre = mid_back((grad_mid, grad_pre))
    grad_proj_bf = grad_proj.astype(BF)
    grad_attn_bf = times_wt(grad_proj_bf, full_output).astype(BF)
    out_grad = reorder_back(order_q, outer_sum(attn_bf, grad_proj_bf))
    out_grad = out_grad.reshape(2, -1, rows_q, width)
    grads_a = [
        jnp.concatenate([gates_grad[half_no].reshape(-1, rows_f, width), out_grad[half_no]], axis=1)
        for half_no in range(2)
    ]
    grads_a = add_bf16(grads_a[0], swap_ctx(grads_a[1], 1)).astype(BF)
    grads_a, grads_b, grad_attn_bf, pre_bf = lax.optimization_barrier(
        (grads_a, grads_b, grad_attn_bf, pre_bf)
    )
    grads_a = halve(grads_a, swap_dp, 2)
    grads_b = halve_inner(grads_b, swap_dp, 1)

    grad_rows = jnp.swapaxes(grad_attn_bf.reshape(tokens, heads, head_width), 0, 1).reshape(
        heads * tokens, head_width
    )
    delta = jnp.sum(
        grad_rows.astype(jnp.float32) * mixed.astype(jnp.float32), axis=1, keepdims=True
    )
    grad_scores = (probs * (times_wt(grad_rows, value_bf) - delta)).astype(BF)
    grad_query = jnp.dot(grad_scores, key_bf, preferred_element_type=jnp.float32)
    grad_query = jnp.swapaxes(grad_query.reshape(heads, tokens, head_width), 0, 1)
    grad_key = outer_sum(grad_scores, query_bf)
    grad_value_bf = outer_sum(probs_bf, grad_rows).astype(BF)
    grad_qraw, grad_scale_query = query_back(grad_query)
    grad_kraw, grad_scale_key = key_back(grad_key)
    grad_qraw_bf = grad_qraw.reshape(tokens, heads * head_width).astype(BF)
    grad_kraw_bf = grad_kraw.astype(BF)

    grad_normed_q = jnp.dot(grad_qraw_bf, full_query, preferred_element_type=jnp.float32)
    grad_normed = jnp.dot(grad_kraw_bf, full_key, preferred_element_type=jnp.float32) + jnp.dot(
        grad_value_bf, full_value, preferred_element_type=jnp.float32
    )
    grad_scale_in = jnp.sum(grad_normed * unit_all, axis=0) + jnp.sum(
        grad_normed_q * unit_in, axis=0
    )
    far = grad_normed.astype(BF).reshape(2, chips, tokens, width)
    grad_w_query = reorder_back(order_q, outer_sum(grad_qraw_bf, normed))
    grad_w_key = reorder_back(order_k, outer_sum(grad_kraw_bf, normed_all))
    grad_w_value = reorder_back(order_k, outer_sum(grad_value_bf, normed_all))
    grad_scales = jnp.concatenate(
        [
            grad_scale_in,
            grad_scale_attn,
            grad_scale_pre,
            grad_scale_post,
            grad_scale_query,
            grad_scale_key,
        ]
    ).reshape(owners, scale_part)
    scales_back = reorder_back(order_s, grad_scales)
    packed = jnp.concatenate(
        [
            grad_w_query.reshape(owners, rows_q, width),
            grad_w_key.reshape(owners, rows_k, width),
            grad_w_value.reshape(owners, rows_k, width),
            jnp.zeros((owners, 8, width), BF).at[:, 0, :scale_part].set(scales_back),
        ],
        axis=1,
    ).reshape(2, -1, width)
    far_sum = add_bf16(far[0], swap_ctx(far[1], 1)).astype(BF)
    grads_a, grads_b, packed, far_sum = tie((grads_a, grads_b, packed, far_sum))
    grads_a = halve(grads_a, swap_dp, 1)
    grads_b = halve(grads_b, swap_dp, 2)
    own_normed = scatter_over(far_sum, swap_z, chips) + grad_normed_q
    packed = add_bf16(packed[0], swap_ctx(packed[1], 1)).astype(BF)
    grads_a, grads_b, packed, own_normed = tie((grads_a, grads_b, packed, own_normed))
    own_first = scatter_chip(packed)
    sum_a = scatter_over(grads_a, swap_z, chips)
    sum_b = scatter_over(grads_b, swap_z, chips)
    own_gate, own_output = sum_a[:rows_f], sum_a[rows_f:]
    own_up, own_down = sum_b[:rows_f], sum_b[rows_f:]
    own_query = own_first[:rows_q]
    own_key = own_first[rows_q : rows_q + rows_k]
    own_value = own_first[rows_q + rows_k : rows_q + 2 * rows_k]
    own_scales = own_first[rows_q + 2 * rows_k, :scale_part]
    grad_resid = grad_resid_a + rms_back(unit_in, inverse_in, own_normed * (1.0 + scale_in))
    return (
        block_out[None],
        grad_resid[None],
        own_query,
        own_key,
        own_value,
        own_output,
        own_gate,
        own_up,
        own_down,
        own_scales,
    )


def shards(*args):
    hidden_in, w_query, w_gate = args[0], args[2], args[6]
    fits = hidden_in.shape[1] * lax.axis_size("ctx") <= 2048 and lax.axis_size("ctx") == 8
    fits = fits and lax.axis_size("dp") == 4
    if fits and w_query.shape[0] % 16 == 0 and w_gate.shape[0] % 16 == 0 and args[3].shape[0] == 8:
        return shards_kernels(*args)
    return shards_plain(*args)


def swaps(block, swap):
    return [swap(block, bits) for bits in range(1, 4)]


def shards_kernels(
    hidden_in,
    positions,
    w_query,
    w_key,
    w_value,
    w_output,
    w_gate,
    w_up,
    w_down,
    norm_scales,
    grad_out,
):
    width = hidden_in.shape[2]
    groups = lax.axis_size("ctx")
    count_dp = lax.axis_size("dp")
    chips = groups // 2
    owners = count_dp * groups
    place = lax.axis_index("ctx")
    row = lax.axis_index("dp")
    resid = hidden_in[0]
    posit = positions[0]
    tokens = resid.shape[0]
    block = tokens // 2
    seq_len = groups * tokens
    head_width = w_key.shape[0] * owners
    heads = w_query.shape[0] * owners // head_width
    rows_q, rows_k, rows_f = w_query.shape[0], w_key.shape[0], w_gate.shape[0]
    last = rows_q + 2 * rows_k
    scale_part = norm_scales.shape[0]
    f32 = jnp.float32
    tie = lax.optimization_barrier

    far_core, far_dp, far_z = (
        jnp.arange(owners, dtype=jnp.int32) // (owners // 2),
        (jnp.arange(owners, dtype=jnp.int32) // chips) % count_dp,
        jnp.arange(owners, dtype=jnp.int32) % chips,
    )
    owner_of = (row ^ far_dp) * groups + (place ^ (2 * far_z + far_core))
    order_s = row_order(owner_of, 1)
    held_row = jnp.arange(2 * rows_k * owners, dtype=jnp.int32)
    held_at = (
        (held_row % (2 * rows_k)) // rows_k * head_width
        + jnp.repeat(owner_of, 2 * rows_k) * rows_k
        + held_row % rows_k
    )
    order_kv = (held_row[:, None] == held_at[None, :]).astype(BF)
    seq_core, seq_zed = (
        jnp.arange(groups, dtype=jnp.int32) // chips,
        jnp.arange(groups, dtype=jnp.int32) % chips,
    )
    key_index = natural_rows(place ^ (2 * seq_zed + seq_core), block, groups).reshape(1, seq_len)
    row_index = natural_rows(place[None], block, groups).reshape(tokens, 1)

    last_rows = jnp.concatenate(
        [
            jnp.pad(values[None], ((0, 0), (0, width - values.shape[0])))
            for values in (norm_scales, (posit // 64).astype(BF), (posit % 64).astype(BF))
        ]
        + [jnp.zeros((5, width), BF)],
        axis=0,
    )
    first = jnp.concatenate([w_query, w_key, w_value, last_rows], axis=0)
    feed = jnp.concatenate([w_gate, w_up, w_down], axis=0)
    inverse_in = lax.rsqrt(jnp.mean(resid * resid, axis=-1, keepdims=True) + EPS)
    unit_in = resid * inverse_in
    unit_bf = unit_in.astype(BF)
    first = gather_over(first[None], swap_z, chips)
    first, unit_bf, feed, w_output, order_kv = tie((first, unit_bf, feed, w_output, order_kv))
    last_far = swap_ctx(first[:, last:], 1)
    pos_all = jnp.stack([first[:, last:], last_far], axis=0)[:, :, :, :tokens].astype(f32)
    pos_all = (pos_all[:, :, 1] * 64.0 + pos_all[:, :, 2]).reshape(seq_len)
    half = head_width // 2
    freq_table = 1000000.0 ** (-jnp.arange(half, dtype=jnp.float32) / half)
    angle = pos_all[:, None] * freq_table[None, :]
    cos_all, sine_all = jnp.cos(angle), jnp.sin(angle)
    first = gather_over(first[None], swap_dp, count_dp).reshape((owners // 2,) + first.shape[1:])
    near = gather_over(unit_bf[None], swap_z, chips).reshape(chips * tokens, width)
    first, near, feed, w_output, cos_all, sine_all = tie(
        (first, near, feed, w_output, cos_all, sine_all)
    )
    other = swap_ctx(first, 1)
    far = swap_ctx(near, 1)
    out_own = gather_over(w_output[None], swap_z, chips)
    other, far, out_own, feed = tie((other, far, out_own, feed))
    scale_rows = jnp.concatenate([first[:, last, :scale_part], other[:, last, :scale_part]], axis=0)
    full_scales = reorder(order_s, scale_rows).reshape(-1)
    scale_in, scale_attn, scale_pre, scale_post, scale_query, scale_key = [
        scale[None] for scale in split_scales(full_scales, width, head_width)
    ]
    feed_z2 = swap_z(feed, 2)
    feed_z1 = swap_z(feed, 1)
    out_own = gather_over(out_own[None], swap_dp, count_dp).reshape((owners // 2, rows_q, width))
    (w_q, w_kv, normed, normed_all, query_raw, key_raw, query_bf, key_bf, value_bf, attn_bf, lse) = (
        call_kernel(
            attend_kernel,
            [
                ((heads * head_width, width), BF),
                ((2 * head_width, width), BF),
                ((tokens, width), BF),
                ((seq_len, width), BF),
                ((tokens, heads * head_width), f32),
                ((seq_len, head_width), f32),
                ((tokens, heads * head_width), BF),
                ((seq_len, head_width), BF),
                ((seq_len, head_width), BF),
                ((tokens, heads * head_width), BF),
                ((tokens, heads), f32),
            ],
            [((2 * head_width, width), BF)],
            12_000_000_000,
            (
                unit_in, near, far, first, other, owner_of, order_kv, scale_in, scale_query, scale_key,
                cos_all, sine_all, key_index, row_index,
            ),
            mebibytes=56,
        )
    )
    attn_bf, feed_z1, feed_z2, out_own, feed = tie((attn_bf, feed_z1, feed_z2, out_own, feed))
    out_other = swap_ctx(out_own, 1)
    feed_z3 = swap_z(feed, 3)
    feed_c0 = swap_ctx(feed, 1)
    feed_c1 = swap_ctx(feed_z1, 1)
    feed_c2 = swap_ctx(feed_z2, 1)
    full_output, projected, middle, pre = call_kernel(
        project_kernel,
        [
            ((owners * rows_q, width), BF),
            ((tokens, width), f32),
            ((tokens, width), f32),
            ((tokens, width), BF),
        ],
        [],
        2_000_000_000,
        (attn_bf, owner_of, out_own, out_other, resid, scale_attn, scale_pre),
    )
    pres = swaps(pre, swap_dp)
    pre, pres, feed_z3, feed_c0, feed_c1, feed_c2 = tie((pre, pres, feed_z3, feed_c0, feed_c1, feed_c2))
    feed_c3 = swap_ctx(feed_z3, 1)
    part_shapes = [((tokens, width), f32)] + [((tokens, width), BF)] * 3
    all_tokens = count_dp * tokens
    hidden = groups * rows_f
    outs = call_kernel(
        feed_kernel,
        part_shapes
        + [
            ((all_tokens, hidden), f32),
            ((all_tokens, hidden), f32),
            ((all_tokens, hidden), BF),
            ((all_tokens, width), BF),
        ]
        + [((hidden, width), BF)] * 3,
        [],
        3_000_000_000,
        [pre] + pres + [feed, feed_z1, feed_z2, feed_z3, feed_c0, feed_c1, feed_c2, feed_c3],
    )
    parts, kept = outs[:4], outs[4:]
    comes = [swap_dp(parts[bits], bits) for bits in range(1, 4)]
    block_out, grad_ffn, grad_s_post = call_kernel(
        turning_kernel,
        [((tokens, width), f32), ((tokens, width), BF), ((1, width), f32)],
        [],
        100_000_000,
        [parts[0]] + comes + [middle, grad_out[0], scale_post],
    )
    gate, up, inner, pre_all, w_g, w_u, w_d = kept
    outs = call_kernel(
        feed_back_kernel,
        part_shapes + [((all_tokens, width), BF), ((all_tokens, hidden), BF), ((all_tokens, hidden), BF)],
        [],
        3_000_000_000,
        [grad_ffn] + swaps(grad_ffn, swap_dp) + [gate, up, w_g, w_u, w_d],
    )
    parts, back = outs[:4], outs[4:]
    comes = [swap_dp(parts[bits], bits) for bits in range(1, 4)]
    g_feed, g_feed_far = call_kernel(
        feed_weights_kernel,
        [((chips, 3 * rows_f, width), BF)] * 2,
        [],
        3_000_000_000,
        [inner, pre_all] + list(back),
    )
    g_feed, g_feed_far, comes = tie((g_feed, g_feed_far, comes))
    g_feed = add_bf16(g_feed, swap_ctx(g_feed_far, 1)).astype(BF)
    grad_resid_a, grad_attn, g_out, g_out_far, grad_s_attn, grad_s_pre = call_kernel(
        project_back_kernel,
        [
            ((tokens, width), f32),
            ((tokens, heads * head_width), BF),
            (out_own.shape, BF),
            (out_own.shape, BF),
            ((1, width), f32),
            ((1, width), f32),
        ],
        [((owners * rows_q, width), BF)],
        3_000_000_000,
        [parts[0]]
        + comes
        + [grad_out[0], projected, middle, full_output, attn_bf, owner_of, scale_attn, scale_pre],
    )
    g_out = add_bf16(g_out, swap_ctx(g_out_far, 1)).astype(BF).reshape(count_dp, chips, rows_q, width)
    g_out, g_feed, grad_attn = tie((g_out, g_feed, grad_attn))
    feed_come1 = swap_z(g_feed[1], 1)
    feed_come2 = swap_z(g_feed[2], 2)
    out_comes = [swap_dp(g_out[bits], bits) for bits in range(1, 4)]
    (packed, packed_far, g_near, g_far, grad_normed_q, grad_s_in, grad_s_query, grad_s_key) = call_kernel(
        attend_back_kernel,
        [
            ((owners // 2, last, width), BF),
            ((owners // 2, last, width), BF),
            ((seq_len // 2, 2 * head_width), BF),
            ((seq_len // 2, 2 * head_width), BF),
            ((tokens, width), f32),
            ((1, width), f32),
            ((1, head_width), f32),
            ((1, head_width), f32),
        ],
        [
            ((heads * tokens, seq_len), BF),
            ((heads * tokens, seq_len), BF),
            ((heads * tokens, head_width), BF),
            ((heads * tokens, head_width), BF),
            ((tokens, heads * head_width), BF),
            ((2 * head_width, width), BF),
            ((heads * head_width, width), BF),
        ],
        12_000_000_000,
        (
            grad_attn, attn_bf, query_bf, key_bf, value_bf, lse, query_raw, key_raw, w_q, w_kv,
            scale_query, scale_key, cos_all, sine_all, key_index, row_index, normed, normed_all,
            unit_in, near, far, owner_of, order_kv,
        ),
        mebibytes=48,
    )
    back = (packed, packed_far, g_near, g_far, grad_normed_q, grad_s_in, grad_s_query, grad_s_key)
    back, feed_come1, feed_come2, out_comes, g_out, g_feed = tie(
        (back, feed_come1, feed_come2, out_comes, g_out, g_feed)
    )
    packed, packed_far, g_near, g_far, grad_normed_q, grad_s_in, grad_s_query, grad_s_key = back
    grad_scales = jnp.concatenate(
        [grad_s_in, grad_s_attn, grad_s_pre, grad_s_post, grad_s_query, grad_s_key], axis=1
    ).reshape(owners, scale_part)
    scales_back = reorder_back(order_s, grad_scales)
    scale_sum = add_bf16(scales_back[: owners // 2], swap_ctx(scales_back[owners // 2 :], 1))
    scale_sum = jnp.pad(scale_sum[:, None], ((0, 0), (last, 7), (0, width - scale_part)))
    packed = jnp.pad(add_bf16(packed, swap_ctx(packed_far, 1)), ((0, 0), (0, 8), (0, 0)))
    packed = (packed + scale_sum).astype(BF)
    feed_come3 = swap_z(g_feed[3, : 3 * rows_f // 2], 3)
    far_sum = add_bf16(g_near, swap_ctx(g_far, 1)).astype(BF).reshape(chips, tokens, 2 * head_width)
    out_sum = add_bf16(g_out[0], *out_comes).astype(BF)
    packed, far_sum, out_sum, g_feed, feed_come3 = tie((packed, far_sum, out_sum, g_feed, feed_come3))
    packed = scatter_over(packed.reshape((count_dp, chips) + packed.shape[1:]), swap_dp, count_dp)
    own_kv = scatter_over(far_sum, swap_z, chips).astype(BF)
    packed, own_kv, out_sum, g_feed = tie((packed.astype(BF), own_kv, out_sum, g_feed))
    own_normed = jnp.dot(own_kv, w_kv, preferred_element_type=jnp.float32) + grad_normed_q
    half_rows = 3 * rows_f // 2
    last_comes = []
    for bits in range(1, 4):
        blocks = [out_sum[bits], packed[bits]] + ([g_feed[3, half_rows:]] if bits == 3 else [])
        last_comes.append(swap_z(jnp.concatenate(blocks, axis=0), bits))
    own_query, own_key, own_value, own_last, own_output, own_gate, own_up, own_down = call_kernel(
        ending_kernel,
        [
            ((rows_q, width), f32),
            ((rows_k, width), f32),
            ((rows_k, width), f32),
            ((8, width), f32),
            ((rows_q, width), f32),
            ((rows_f, width), f32),
            ((rows_f, width), f32),
            ((rows_f, width), f32),
        ],
        [],
        10_000_000,
        [packed[0], out_sum[0]]
        + last_comes
        + [g_feed[0], feed_come1, feed_come2, feed_come3],
    )
    grad_resid = grad_resid_a + rms_back(unit_in, inverse_in, own_normed * (1.0 + scale_in))
    return (
        block_out[None],
        grad_resid[None],
        own_query,
        own_key,
        own_value,
        own_output,
        own_gate,
        own_up,
        own_down,
        own_last[0, :scale_part],
    )


def solution(mesh):
    in_specs = (
        P("dp", "ctx", None),
        P("dp", "ctx"),
        P(("dp", "ctx"), None),
        P(("dp", "ctx"), None),
        P(("dp", "ctx"), None),
        P(("dp", "ctx"), None),
        P(("dp", "ctx"), None),
        P(("dp", "ctx"), None),
        P(("dp", "ctx"), None),
        P(("dp", "ctx")),
        P("dp", "ctx", None),
    )
    out_specs = (
        P("dp", "ctx", None),
        P("dp", "ctx", None),
        P(("dp", "ctx"), None),
        P(("dp", "ctx"), None),
        P(("dp", "ctx"), None),
        P(("dp", "ctx"), None),
        P(("dp", "ctx"), None),
        P(("dp", "ctx"), None),
        P(("dp", "ctx"), None),
        P(("dp", "ctx")),
    )
    return jax.shard_map(shards, mesh=mesh, in_specs=in_specs, out_specs=out_specs, check_vma=False)
```
